32 devices in a mesh: group: 4 (over x, core), member: 8 (over z, y).
Axes of the slice: x: 2, y: 2, z: 4, core: 2. Of those that a mesh axis runs over, the one named last changes fastest.
Arguments:
- features: bfloat16 [16384, 512], P(('group', 'member')), may hold values from -6 to 6
- cotangent: bfloat16 [16384, 512], P(('group', 'member')), may hold values from -6 to 6
- w_self: bfloat16 [512, 512], replicated, may hold values from -0.25 to 0.25
- w_neigh: bfloat16 [512, 512], replicated, may hold values from -0.25 to 0.25
- bias: float32 [512], replicated, may hold values from -4 to 4
- neighbours: int32 [16384, 16], P(('group', 'member')), may hold values from 0 to 639
- neigh_count: int32 [16384], P(('group', 'member')), may hold values from 1 to 16
- serve_rows: int32 [32, 128], P(('group', 'member')), may hold values from 0 to 511
Outputs:
- grad_features: float32 [16384, 512], P(('group', 'member'))
- grad_self: float32 [512, 512], replicated
- grad_neigh: float32 [512, 512], replicated
- grad_bias: float32 [512], replicated
The draws below stay inside these ranges and needn't reach their ends.
All inputs are finite; a program needn't handle non-finite values.
Results may differ from the reference program's by a relative error of at most 0.0055.
Values may be sent and summed in bfloat16 or wider, within the bound.
No kernel may reach another device: no remote copies, remote signals or barrier semaphores. Data moves between devices by JAX's collectives and lax.ppermute only.
A program may use at most 64 MiB of HBM per device.

```python
import math
import jax
import jax.numpy as jnp
import numpy as np
from jax import lax

D = 512
FANOUT = 16
OWN_DEV = 512
CAP = 4
NODES = 16384
SLOTS = 128
N_GROUP = 4
N_MEMBER = 8


def set_ends(result, rng, least, top_value):
    index_at = [jax.random.randint(jax.random.fold_in(rng, axis), (), 0, length) for axis, length in enumerate(result.shape)]
    main_axis = result.shape.index(max(result.shape))
    next_to = index_at[:main_axis] + [(index_at[main_axis] + 1) % result.shape[main_axis]] + index_at[main_axis + 1:]
    return result.at[tuple(index_at)].set(least).at[tuple(next_to)].set(top_value)


def block_levels(key, dims, cuts, smallest, largest):
    gain, own = 1.0, jax.random.fold_in(key, 6)
    for position, shards_of in cuts:
        heights = jnp.exp(jax.random.uniform(jax.random.fold_in(own, position), (shards_of,), jnp.float32, smallest / len(cuts), largest / len(cuts)))
        gain = gain * jnp.repeat(heights, dims[position] // shards_of).reshape([-1 if axis == position else 1 for axis in range(len(dims))])
    return gain


def cumulative_ranks(number_of, skew):
    weights = [(1 << 20) // math.isqrt(grade ** skew) + 1 for grade in range(1, number_of + 1)]
    scale = 1 + sum(weights) // (1 << 30)
    return np.cumsum(np.array([max(1, weight // scale) for weight in weights]))


def skewed_ids(stream_key, extent, number_of, skew):
    table = cumulative_ranks(number_of, skew)
    pick = jax.random.randint(jax.random.fold_in(stream_key, 1), extent, 0, int(table[number_of - 1]))
    rank = jnp.searchsorted(jnp.asarray(table, jnp.int32), pick, side="right")
    return jax.random.permutation(jax.random.fold_in(stream_key, 2), number_of)[rank].astype(jnp.int32)


def centred(own_key, extent, scale, most, cuts=(), held_as=jnp.bfloat16):
    loudness = block_levels(own_key, extent, cuts, -0.22, 0.18) if cuts else 1.0
    result = jax.random.normal(own_key, extent, jnp.float32) * scale * loudness
    return jnp.minimum(jnp.maximum(result, -most), most).astype(held_as)


def setup_inputs(seed: int = 0) -> dict:
    seeds = jax.random.split(jax.random.key(seed), 9)
    return {
        "features": centred(seeds[0], (NODES, D), 1.0, 6.0, ((0, 32),)),
        "cotangent": centred(seeds[1], (NODES, D), 1.0, 6.0, ((0, 32),)),
        "w_self": centred(seeds[2], (D, D), D ** -0.5, 0.25),
        "w_neigh": centred(seeds[3], (D, D), D ** -0.5, 0.25),
        "bias": centred(seeds[4], (D,), 1.0, 4.0, (), jnp.float32),
        "neighbours": set_ends(jax.random.randint(seeds[5], (NODES, FANOUT), 0, OWN_DEV + SLOTS), jax.random.fold_in(seeds[5], 1), 0, (OWN_DEV + SLOTS) - 1).astype(jnp.int32),
        "neigh_count": set_ends(jax.random.randint(seeds[6], (NODES,), 1, FANOUT + 1), jax.random.fold_in(seeds[6], 1), 1, FANOUT).astype(jnp.int32),
        "serve_rows": set_ends(skewed_ids(seeds[7], (N_GROUP * N_MEMBER, SLOTS), OWN_DEV, 2), jax.random.fold_in(seeds[7], 3), 0, OWN_DEV - 1).astype(jnp.int32),
    }


def source_rows(device, refs, serve_rows):
    slot = jnp.clip(refs - OWN_DEV, 0, SLOTS - 1).astype(jnp.int32)
    owner = (slot // CAP).astype(jnp.int32)
    column = (device * CAP + slot % CAP).astype(jnp.int32)
    remote = serve_rows[owner, column] + owner * OWN_DEV
    return jnp.where(refs < OWN_DEV, refs + device * OWN_DEV, remote).astype(jnp.int32)

def reference(features, cotangent, w_self, w_neigh, bias, neighbours, neigh_count, serve_rows):
    devices = N_GROUP * N_MEMBER
    positions = jnp.arange(FANOUT, dtype=jnp.int32)

    def aggregate(device):
        refs = lax.dynamic_slice_in_dim(neighbours, device * OWN_DEV, OWN_DEV, 0)
        counts = lax.dynamic_slice_in_dim(neigh_count, device * OWN_DEV, OWN_DEV, 0)
        gathered = features[source_rows(device, refs, serve_rows)].astype(jnp.float32)
        in_use = (positions[None, :] < counts[:, None]).astype(jnp.float32)
        summed = jnp.einsum('nk,nkd->nd', in_use, gathered)
        return (summed / counts[:, None].astype(jnp.float32)).astype(jnp.bfloat16)
    aggregated = lax.map(aggregate, jnp.arange(devices, dtype=jnp.int32)).reshape(NODES, D)
    pre = jnp.dot(features, w_self, preferred_element_type=jnp.float32)
    pre = pre + jnp.dot(aggregated, w_neigh, preferred_element_type=jnp.float32) + bias
    sigmoid_pre = jax.nn.sigmoid(pre)
    pre_grad = (cotangent.astype(jnp.float32) * sigmoid_pre * (1.0 + pre * (1.0 - sigmoid_pre))).astype(jnp.bfloat16)
    factor = 1.0 / math.sqrt(NODES)
    grad_self = jnp.dot(features.T, pre_grad, preferred_element_type=jnp.float32) * factor
    grad_neigh = jnp.dot(aggregated.T, pre_grad, preferred_element_type=jnp.float32) * factor
    grad_bias = lax.optimization_barrier(jnp.sum(pre_grad.astype(jnp.float32), axis=0)) * factor
    agg_grad = jnp.dot(pre_grad, w_neigh.T, preferred_element_type=jnp.float32)
    message = (agg_grad / neigh_count[:, None].astype(jnp.float32)).astype(jnp.bfloat16)
    self_grad = jnp.dot(pre_grad, w_self.T, preferred_element_type=jnp.float32)
    sink = OWN_DEV + SLOTS
    owners = jnp.arange(devices, dtype=jnp.int32)[:, None]

    def spread(grad_all, device):
        refs = lax.dynamic_slice_in_dim(neighbours, device * OWN_DEV, OWN_DEV, 0)
        counts = lax.dynamic_slice_in_dim(neigh_count, device * OWN_DEV, OWN_DEV, 0)
        block_msg = lax.dynamic_slice_in_dim(message, device * OWN_DEV, OWN_DEV, 0)
        in_use = positions[None, :] < counts[:, None]
        target = jnp.where(in_use, refs, sink).reshape(-1).astype(jnp.int32)
        values = jnp.broadcast_to(block_msg.astype(jnp.float32)[:, None, :], (OWN_DEV, FANOUT, D)).reshape(-1, D)
        table = jnp.zeros((sink + 1, D), jnp.float32).at[target].add(values)
        own_part = table[:OWN_DEV]
        rounded = lax.optimization_barrier(table[OWN_DEV:sink].astype(jnp.bfloat16))
        remote = rounded.astype(jnp.float32)
        columns = lax.dynamic_slice_in_dim(serve_rows, device * CAP, CAP, 1)
        targets = (owners * OWN_DEV + columns).reshape(-1).astype(jnp.int32)
        current = lax.dynamic_slice_in_dim(grad_all, device * OWN_DEV, OWN_DEV, 0)
        grad_all = lax.dynamic_update_slice_in_dim(grad_all, current + own_part, device * OWN_DEV, 0)
        grad_all = grad_all.at[targets].add(remote)
        return (grad_all, None)
    grad_features, _ = lax.scan(spread, self_grad, jnp.arange(devices, dtype=jnp.int32))
    return (grad_features, grad_self, grad_neigh, grad_bias)
```

```python
import functools
import math

import jax
import jax.numpy as jnp
from jax import lax
from jax.experimental import pallas as pl
from jax.experimental.pallas import tpu as pltpu
from jax.sharding import Mesh
from jax.sharding import PartitionSpec as P

BF16 = jnp.bfloat16
F32 = jnp.float32


def product(left, right, left_dim, right_dim):
    return lax.dot_general(
        left, right, (((left_dim,), (right_dim,)), ((), ())), preferred_element_type=F32
    )


def call(body, outs, scratch=(), flops=0, moved=0, smem=0, name=None):
    def run(*operands):
        return pl.pallas_call(
            body,
            out_shape=outs,
            in_specs=[
                pl.BlockSpec(memory_space=pltpu.SMEM if at < smem else pltpu.VMEM)
                for at in range(len(operands))
            ],
            out_specs=jax.tree.map(lambda _: pl.BlockSpec(memory_space=pltpu.VMEM), outs),
            scratch_shapes=list(scratch),
            compiler_params=pltpu.CompilerParams(vmem_limit_bytes=40 * 1024 * 1024),
            cost_estimate=pl.CostEstimate(flops=flops, bytes_accessed=moved, transcendentals=0),
            name=name,
        )(*operands)

    return run


def serve_kernel(serve_ref, features_ref, out_ref):
    own_rows = features_ref.shape[0]
    slots = serve_ref.shape[1]
    row = lax.broadcasted_iota(jnp.int32, (own_rows, slots), 0)
    picks = (row == serve_ref[...]).astype(F32).astype(BF16)
    rows = product(picks, features_ref[...], 0, 0)
    out_ref[...] = rows.reshape(out_ref.shape).astype(BF16)


def own_kernel(
    neighbours_ref, count_ref, features_ref, w_self_ref, bias_ref,
    counts_ref, inverse_ref, own_sum_ref, pre_ref, live_ref,
):
    own_rows, fanout = neighbours_ref.shape
    table_rows = counts_ref.shape[0]
    count = count_ref[...]
    position = lax.broadcasted_iota(jnp.int32, (fanout, own_rows), 0)
    live_ref[...] = jnp.where(position < count, neighbours_ref[...].T, -1)
    inverse_ref[...] = jnp.broadcast_to(1.0 / count.astype(F32), (128, own_rows)).T
    step = 32

    def fill(at, carry):
        start = pl.multiple_of(at * step, step)
        row = lax.broadcasted_iota(jnp.int32, (step, own_rows), 0) + start
        total = jnp.zeros((step, own_rows), F32)
        for k in range(fanout):
            total = total + jnp.where(row == live_ref[k : k + 1, :], 1.0, 0.0)
        counts_ref[pl.ds(start, step), :] = total.astype(BF16)
        return carry

    lax.fori_loop(0, table_rows // step, fill, 0)
    features = features_ref[...]
    own_sum_ref[...] = product(counts_ref[:own_rows, :], features, 0, 0)
    pre_ref[...] = product(features, w_self_ref[...], 1, 0) + bias_ref[...]


def spread_wide(inverse, width):
    return jnp.concatenate([inverse] * (width // 128), axis=1)


def main_kernel(
    core_ref, incoming_ref, counts_ref, inverse_ref, own_sum_ref, pre_ref, features_ref, cotangent_ref, w_neigh_ref,
    send_ref, keep_ref, keep_rows_ref, bias_ref, pre_grad_ref, message_ref, rows_ref,
):
    own_rows, width = features_ref.shape
    slots = rows_ref.shape[0]
    first = core_ref[0] == 0
    inverse = spread_wide(inverse_ref[...], width)
    slot_counts = counts_ref[own_rows:, :]
    incoming = incoming_ref[...].astype(F32).reshape(slots, width).astype(BF16)
    summed = own_sum_ref[...] + product(slot_counts, incoming, 0, 0)
    aggregated = (summed * inverse).astype(BF16)
    pre = pre_ref[...] + product(aggregated, w_neigh_ref[...], 1, 0)
    sigmoid_pre = jax.nn.sigmoid(pre)
    pre_grad = (
        cotangent_ref[...].astype(F32) * sigmoid_pre * (1.0 + pre * (1.0 - sigmoid_pre))
    ).astype(BF16)
    pre_grad_ref[...] = pre_grad
    features = features_ref[...]
    keep_ref[...] = product(jnp.where(first, features, aggregated), pre_grad, 0, 0)
    send_ref[:own_rows, :] = product(
        jnp.where(first, aggregated, features), pre_grad, 0, 0
    ).astype(BF16)
    message = (product(pre_grad, w_neigh_ref[...], 1, 1) * inverse).astype(BF16)
    message_ref[...] = message
    rows_ref[...] = product(slot_counts, message, 1, 0)
    half = slots // 2
    blocks, length = keep_rows_ref.shape[0], keep_rows_ref.shape[1]
    for at in range(blocks):
        mine = pl.multiple_of((at * 2 + core_ref[0]) * length, length)
        other = pl.multiple_of((at * 2 + 1 - core_ref[0]) * length, length)
        keep_rows_ref[at] = rows_ref[pl.ds(mine, length), :].astype(BF16)
        send_ref[own_rows + at * length : own_rows + (at + 1) * length, :] = rows_ref[
            pl.ds(other, length), :
        ].astype(BF16)
    bias = jnp.sum(pre_grad.astype(F32), axis=0, keepdims=True).astype(BF16)
    bias_ref[...] = jnp.broadcast_to(bias, bias_ref.shape)
    send_ref[own_rows + half :, :] = jnp.broadcast_to(bias, bias_ref.shape)


def pack_kernel(order, received_ref, keep_ref, keep_rows_ref, bias_ref, out_ref):
    width = keep_ref.shape[1]
    peers, length = out_ref.shape[0], out_ref.shape[1]
    blocks, block_rows = keep_rows_ref.shape[0], keep_rows_ref.shape[1]
    half = blocks * block_rows
    own_rows = keep_ref.shape[0]
    share = own_rows // peers
    cap = half // peers
    keep_rows = keep_rows_ref[...].astype(F32).reshape(half, width)
    other_rows = received_ref[own_rows : own_rows + half, :].astype(F32)
    bias = (
        bias_ref[...].astype(F32) + received_ref[own_rows + half :, :].astype(F32)
    )
    summed = keep_ref[...] + received_ref[:own_rows, :].astype(F32)
    for peer in range(peers):
        at = order[peer] * share
        parts = [
            summed[at : at + share],
            keep_rows[peer * cap : (peer + 1) * cap],
            other_rows[peer * cap : (peer + 1) * cap],
            bias[: length - share - 2 * cap],
        ]
        out_ref[peer] = jnp.concatenate(parts, axis=0).astype(BF16)


def own_grad_kernel(pre_grad_ref, w_self_ref, counts_ref, message_ref, out_ref):
    own_rows = pre_grad_ref.shape[0]
    out_ref[...] = product(pre_grad_ref[...], w_self_ref[...], 1, 1) + product(
        counts_ref[:own_rows, :], message_ref[...], 1, 0
    )


def sum_kernel(factor, share, cap, payload_ref, out_ref, bias_ref):
    out = jnp.sum(payload_ref[:, :share, :].astype(F32), axis=0).astype(BF16)
    for copy in range(out_ref.shape[0]):
        out_ref[copy] = out
    at = share + 2 * cap
    tail = payload_ref[:, share:, :].astype(F32)
    bias_ref[...] = jnp.sum(tail[:, at - share, :], axis=0, keepdims=True) * factor


def owner_kernel(share, cap, core_ref, serve_ref, payload_ref, base_ref, out_ref):
    own_rows, width = base_ref.shape
    slots = serve_ref.shape[1]
    peers = payload_ref.shape[0]
    blocks = serve_ref.shape[0]
    tail = payload_ref[:, share:, :].astype(F32)
    half = peers * cap
    mine = tail[:, :cap, :].reshape(half, width)
    other = tail[:, cap : 2 * cap, :].reshape(half, width)
    first = core_ref[0] == 0
    rows = jnp.concatenate(
        [jnp.where(first, mine, other), jnp.where(first, other, mine)], axis=0
    ).astype(BF16)
    row = lax.broadcasted_iota(jnp.int32, (own_rows, slots), 0)
    picks = (row == serve_ref[...]).astype(F32).astype(BF16)
    out_ref[...] = base_ref[...] + product(picks, rows, 1, 0)


def finish_kernel(factor, core_ref, mine_ref, other_ref, self_ref, neigh_ref):
    first = core_ref[0] == 0
    mine, other = mine_ref[...], other_ref[...]
    self_ref[...] = jnp.where(first, mine, other).astype(F32) * factor
    neigh_ref[...] = jnp.where(first, other, mine).astype(F32) * factor


def local(features, cotangent, w_self, w_neigh, bias, neighbours, neigh_count, serve_rows):
    own_rows, width = features.shape
    fanout = neighbours.shape[1]
    across = lax.axis_size("across")
    outer, inner = lax.axis_size("outer"), lax.axis_size("inner")
    members = outer * inner
    peers = across * members
    devices = 2 * peers
    slots = serve_rows.shape[1]
    cap = slots // devices
    half = slots // 2
    table_rows = own_rows + slots
    share = own_rows // peers
    length = -(-(share + 2 * cap + 1) // 16) * 16
    everyone = ("across", "core", "outer", "inner")
    plane = ("across", "outer", "inner")
    core = lax.axis_index("core").astype(jnp.int32).reshape(1)
    swap = [(0, 1), (1, 0)]
    factor = 1.0 / math.sqrt(own_rows * devices)
    shape = jax.ShapeDtypeStruct
    cube = 2 * own_rows * own_rows * width

    outgoing = call(
        serve_kernel, shape((devices, cap, width), BF16), flops=cube // 4, moved=1 << 20, name="serve"
    )(serve_rows, features)
    incoming = lax.all_to_all(outgoing, everyone, 0, 0, tiled=True)
    counts, inverse, own_sum, pre = call(
        own_kernel,
        (
            shape((table_rows, own_rows), BF16),
            shape((own_rows, 128), F32),
            shape((own_rows, width), F32),
            shape((own_rows, width), F32),
        ),
        scratch=[pltpu.VMEM((fanout, own_rows), jnp.int32)],
        flops=20 * cube,
        moved=4 << 20,
        name="own_aggregate",
    )(neighbours, neigh_count.reshape(1, own_rows), features, w_self, bias.reshape(1, width))
    send, keep, keep_rows, own_bias, pre_grad, message = call(
        main_kernel,
        (
            shape((own_rows + half + 16, width), BF16),
            shape((own_rows, width), F32),
            shape((across, members * cap, width), BF16),
            shape((16, width), BF16),
            shape((own_rows, width), BF16),
            shape((own_rows, width), BF16),
        ),
        scratch=[pltpu.VMEM((slots, width), F32)],
        flops=5 * cube,
        moved=8 << 20,
        smem=1,
        name="layer_grad",
    )(core, incoming, counts, inverse, own_sum, pre, features, cotangent, w_neigh)
    received = lax.ppermute(send, "core", swap)
    order = [
        (a * inner + i) * outer + o
        for a in range(across) for o in range(outer) for i in range(inner)
    ]
    payload = call(
        functools.partial(pack_kernel, order),
        shape((peers, length, width), BF16),
        flops=cube // 4,
        moved=4 << 20,
        name="pack",
    )(received, keep, keep_rows, own_bias)
    arrived = lax.all_to_all(payload, plane, 0, 0, tiled=True)
    base = call(
        own_grad_kernel, shape((own_rows, width), F32), flops=2 * cube, moved=4 << 20, name="own_grad"
    )(pre_grad, w_self, counts, message)
    summed, bias_sum = call(
        functools.partial(sum_kernel, factor, share, cap),
        (shape((outer, share, width), BF16), shape((1, width), F32)),
        flops=cube // 8,
        moved=1 << 20,
        name="sum_shares",
    )(arrived)
    column = lax.all_to_all(summed, "outer", 0, 0, tiled=True).reshape(outer * share, width)
    mine = lax.all_gather(column, ("across", "inner"), axis=0, tiled=True)
    serve_order = serve_rows.reshape(across, 2, members * cap).transpose(1, 0, 2).reshape(1, slots)
    grad_features = call(
        functools.partial(owner_kernel, share, cap),
        shape((own_rows, width), F32),
        flops=cube // 4,
        moved=3 << 20,
        smem=1,
        name="owner_sum",
    )(core, serve_order, arrived, base)
    other = lax.ppermute(mine, "core", swap)
    grad_self, grad_neigh = call(
        functools.partial(finish_kernel, factor),
        (shape((own_rows, width), F32), shape((own_rows, width), F32)),
        flops=cube // 8,
        moved=3 << 20,
        smem=1,
        name="finish",
    )(core, mine, other)
    return grad_features, grad_self, grad_neigh, bias_sum.reshape(width)


def solution(mesh):
    groups, members = mesh.shape["group"], mesh.shape["member"]
    outer = 2
    while outer * outer < members:
        outer *= 2
    fine = Mesh(
        mesh.devices.reshape(groups // 2, 2, outer, members // outer),
        ("across", "core", "outer", "inner"),
    )
    nodes = ("across", "core", "outer", "inner")
    rows = P(nodes, None)
    return jax.shard_map(
        local,
        mesh=fine,
        in_specs=(rows, rows, P(), P(), P(), rows, P(nodes), rows),
        out_specs=(rows, P(), P(), P()),
        check_vma=False,
    )
```

```python
import functools
import math

import jax
import jax.numpy as jnp
from jax import lax
from jax.experimental import pallas as pl
from jax.experimental.pallas import tpu as pltpu
from jax.sharding import Mesh
from jax.sharding import PartitionSpec as P

BF16 = jnp.bfloat16
F32 = jnp.float32
SMEM, VMEM, HBM = pltpu.SMEM, pltpu.VMEM, pltpu.HBM
shape = jax.ShapeDtypeStruct


def product(left, right, left_dim, right_dim):
    return lax.dot_general(
        left, right, (((left_dim,), (right_dim,)), ((), ())), preferred_element_type=F32
    )


def call(name, body, ins, outs, scratch=(), copies=0, flops=0, moved=0, aliases=None):
    scratch = list(scratch)
    if copies:
        scratch.append(pltpu.SemaphoreType.DMA((copies,)))
    return pl.pallas_call(
        body,
        out_shape=tuple(out for out, _ in outs),
        in_specs=[pl.BlockSpec(memory_space=memory) for memory in ins],
        out_specs=tuple(pl.BlockSpec(memory_space=memory) for _, memory in outs),
        scratch_shapes=scratch,
        input_output_aliases=aliases or {},
        compiler_params=pltpu.CompilerParams(vmem_limit_bytes=48 * 1024 * 1024),
        cost_estimate=pl.CostEstimate(flops=flops, bytes_accessed=moved, transcendentals=0),
        name=name,
    )


def start_all(sems, *pairs):
    copies = [pltpu.make_async_copy(a, b, sems.at[at]) for at, (a, b) in enumerate(pairs)]
    for copy in copies:
        copy.start()
    return copies


def serve_kernel(serve_hbm, features_hbm, out_ref, serve_ref, features_ref, sems):
    copies = start_all(sems, (serve_hbm, serve_ref), (features_hbm, features_ref))
    own_rows = features_ref.shape[0]
    slots = serve_ref.shape[1]
    copies[0].wait()
    row = lax.broadcasted_iota(jnp.int32, (own_rows, slots), 0)
    picks = (row == serve_ref[...]).astype(F32).astype(BF16)
    copies[1].wait()
    rows = product(picks, features_ref[...], 0, 0)
    out_ref[...] = rows.reshape(out_ref.shape).astype(BF16)


def own_kernel(
    dims, place_ref, neighbours_hbm, count_hbm, serve_hbm, features_hbm, w_self_hbm, bias_hbm,
    counts_hbm, inverse_hbm, own_sum_hbm, pre_hbm, order_hbm,
    neighbours_ref, count_ref, serve_ref, features_ref, w_self_ref, bias_ref,
    counts_ref, inverse_ref, own_sum_ref, pre_ref, order_ref, live_ref, sems,
):
    ins = start_all(
        sems,
        (neighbours_hbm, neighbours_ref),
        (count_hbm, count_ref),
        (features_hbm, features_ref),
        (w_self_hbm, w_self_ref),
        (bias_hbm, bias_ref),
        (serve_hbm, serve_ref),
    )

    def send(at, source, target):
        copy = pltpu.make_async_copy(source, target, sems.at[len(ins) + at])
        copy.start()
        return copy

    fanout, own_rows = neighbours_ref.shape
    table_rows = counts_ref.shape[0]
    for copy in ins[:2]:
        copy.wait()
    count = count_ref[...]
    position = lax.broadcasted_iota(jnp.int32, (fanout, own_rows), 0)
    live_ref[...] = jnp.where(position < count, neighbours_ref[...], -1)
    inverse_ref[...] = jnp.broadcast_to(1.0 / count.astype(F32), (128, own_rows)).T
    outs = [send(0, inverse_ref, inverse_hbm)]
    step = 32

    def fill(at, carry):
        start = pl.multiple_of(at * step, step)
        row = lax.broadcasted_iota(jnp.int32, (step, own_rows), 0) + start
        total = jnp.zeros((step, own_rows), F32)
        for k in range(fanout):
            total = total + jnp.where(row == live_ref[k : k + 1, :], 1.0, 0.0)
        counts_ref[pl.ds(start, step), :] = total.astype(BF16)
        return carry

    lax.fori_loop(0, table_rows // step, fill, 0)
    outs.append(send(1, counts_ref, counts_hbm))
    ins[2].wait()
    features = features_ref[...]
    own_sum_ref[...] = product(counts_ref[:own_rows, :], features, 0, 0)
    outs.append(send(2, own_sum_ref, own_sum_hbm))
    ins[3].wait()
    ins[4].wait()
    pre_ref[...] = product(features, w_self_ref[...], 1, 0) + bias_ref[...]
    outs.append(send(3, pre_ref, pre_hbm))
    ins[5].wait()
    across, near, cap = dims
    slots = serve_ref.shape[1]
    to = lax.broadcasted_iota(jnp.int32, (slots, slots), 1)
    slot = to % cap
    core = (to // cap % 2 + place_ref[0]) % 2
    n = to // (2 * cap) % near
    a = to // (2 * cap * near) % across
    wide = (to // (2 * cap * near * across) + place_ref[1]) % 2
    source = (((a * 2 + core) * 2 + wide) * near + n) * cap + slot
    at = lax.broadcasted_iota(jnp.int32, (slots, slots), 0)
    moves = (at == source).astype(F32).astype(BF16)
    serve = serve_ref[...]
    high = (serve // 32).astype(F32).astype(BF16)
    low = (serve % 32).astype(F32).astype(BF16)
    order_ref[...] = (
        product(high, moves, 1, 0) * 32.0 + product(low, moves, 1, 0)
    ).astype(jnp.int32)
    outs.append(send(4, order_ref, order_hbm))
    for copy in outs:
        copy.wait()


def spread_wide(inverse, width):
    return jnp.concatenate([inverse] * (width // 128), axis=1)


def main_kernel(
    place_ref, incoming_ref, counts_hbm, inverse_hbm, own_sum_hbm, pre_hbm, features_hbm, cotangent_hbm, w_neigh_hbm,
    send_ref, keep_ref, keep_rows_ref, bias_ref, pre_grad_ref, message_ref,
    counts_ref, inverse_ref, own_sum_ref, pre_ref, features_ref, cotangent_ref, w_neigh_ref, rows_ref, sems,
):
    own_rows, width = features_ref.shape
    slots = rows_ref.shape[0]
    copies = start_all(
        sems,
        (counts_hbm.at[pl.ds(own_rows, slots), :], counts_ref),
        (own_sum_hbm, own_sum_ref),
        (inverse_hbm, inverse_ref),
        (w_neigh_hbm, w_neigh_ref),
        (pre_hbm, pre_ref),
        (cotangent_hbm, cotangent_ref),
        (features_hbm, features_ref),
    )
    first = place_ref[0] == 0
    incoming = incoming_ref[...].astype(F32).reshape(slots, width).astype(BF16)
    copies[0].wait()
    slot_counts = counts_ref[...]
    fetched = product(slot_counts, incoming, 0, 0)
    copies[1].wait()
    copies[2].wait()
    inverse = spread_wide(inverse_ref[...], width)
    aggregated = ((own_sum_ref[...] + fetched) * inverse).astype(BF16)
    copies[3].wait()
    mixed = product(aggregated, w_neigh_ref[...], 1, 0)
    copies[4].wait()
    pre = pre_ref[...] + mixed
    sigmoid_pre = jax.nn.sigmoid(pre)
    copies[5].wait()
    pre_grad = (
        cotangent_ref[...].astype(F32) * sigmoid_pre * (1.0 + pre * (1.0 - sigmoid_pre))
    ).astype(BF16)
    pre_grad_ref[...] = pre_grad
    copies[6].wait()
    features = features_ref[...]
    keep_ref[...] = product(jnp.where(first, features, aggregated), pre_grad, 0, 0)
    send_ref[:own_rows, :] = product(
        jnp.where(first, aggregated, features), pre_grad, 0, 0
    ).astype(BF16)
    message = (product(pre_grad, w_neigh_ref[...], 1, 1) * inverse).astype(BF16)
    message_ref[...] = message
    rows_ref[...] = product(slot_counts, message, 1, 0)
    half = slots // 2
    blocks, length = keep_rows_ref.shape[0], keep_rows_ref.shape[1]
    for at in range(blocks):
        mine = pl.multiple_of((at * 2 + place_ref[0]) * length, length)
        other = pl.multiple_of((at * 2 + 1 - place_ref[0]) * length, length)
        keep_rows_ref[at] = rows_ref[pl.ds(mine, length), :].astype(BF16)
        send_ref[own_rows + at * length : own_rows + (at + 1) * length, :] = rows_ref[
            pl.ds(other, length), :
        ].astype(BF16)
    bias = jnp.sum(pre_grad.astype(F32), axis=0, keepdims=True).astype(BF16)
    bias_ref[...] = jnp.broadcast_to(bias, bias_ref.shape)
    send_ref[own_rows + half :, :] = jnp.broadcast_to(bias, bias_ref.shape)


def own_grad_kernel(
    pre_grad_ref, message_ref, w_self_hbm, counts_hbm, out_hbm, w_self_ref, counts_ref, out_ref, sems
):
    own_rows = pre_grad_ref.shape[0]
    copies = start_all(
        sems, (w_self_hbm, w_self_ref), (counts_hbm.at[pl.ds(0, own_rows), :], counts_ref)
    )
    copies[0].wait()
    out_ref[...] = product(pre_grad_ref[...], w_self_ref[...], 1, 1)
    copies[1].wait()
    out_ref[...] += product(counts_ref[...], message_ref[...], 1, 0)
    copy = pltpu.make_async_copy(out_ref, out_hbm, sems.at[2])
    copy.start()
    copy.wait()


def pack_kernel(dims, received_ref, keep_ref, keep_rows_ref, bias_ref, after_hbm, out_ref):
    across, near, cap = dims
    own_rows, width = keep_ref.shape
    peers, length = out_ref.shape[0], out_ref.shape[1]
    half = 2 * peers * cap
    share = own_rows // peers
    keep_rows = keep_rows_ref[...].astype(F32).reshape(half, width)
    other_rows = received_ref[own_rows : own_rows + half, :].astype(F32)
    bias = bias_ref[...].astype(F32) + received_ref[own_rows + half :, :].astype(F32)
    summed = keep_ref[...] + received_ref[:own_rows, :].astype(F32)
    for peer in range(peers):
        parts = [summed[peer * share : (peer + 1) * share]]
        for wide in range(2):
            at = ((peer // near * 2 + wide) * near + peer % near) * cap
            parts += [keep_rows[at : at + cap], other_rows[at : at + cap]]
        parts.append(bias[: length - share - 4 * cap])
        out_ref[peer] = jnp.concatenate(parts, axis=0).astype(BF16)


def sum_kernel(cap, share, place_ref, payload_ref, keep_ref, send_ref):
    peers, length, width = payload_ref.shape
    pair = 2 * cap
    count = peers * pair
    payload = payload_ref[...].astype(F32)
    grads = jnp.sum(payload[:, :share, :], axis=0).astype(BF16)
    tail = payload[:, share + 2 * pair :, :]
    bias = jnp.broadcast_to(
        jnp.sum(tail[:, 0:1, :], axis=0), (keep_ref.shape[0] - share - count, width)
    ).astype(BF16)
    first = place_ref[1] == 0
    lower = payload[:, share : share + pair, :].reshape(count, width)
    upper = payload[:, share + pair : share + 2 * pair, :].reshape(count, width)
    for ref, rows in (
        (keep_ref, jnp.where(first, lower, upper)),
        (send_ref, jnp.where(first, upper, lower)),
    ):
        ref[:share, :] = grads
        ref[share : share + count, :] = rows.astype(BF16)
        ref[share + count :, :] = bias


def total_kernel(factor, keep_ref, received_ref, out_ref, bias_ref):
    peers, share, width = out_ref.shape
    total = (keep_ref[:share, :].astype(F32) + received_ref[:share, :].astype(F32)).astype(BF16)
    for peer in range(peers):
        out_ref[peer] = total
    last = keep_ref.shape[0] - 16
    bias = keep_ref[last:, :].astype(F32) + received_ref[last:, :].astype(F32)
    bias_ref[...] = bias[:1] * factor


def owner_kernel(share, order_hbm, keep_ref, received_ref, base_hbm, out_hbm, order_ref, base_ref, sems):
    copies = start_all(sems, (order_hbm, order_ref), (base_hbm, base_ref))
    own_rows = base_ref.shape[0]
    slots = order_ref.shape[1]
    half = slots // 2
    rows = jnp.concatenate(
        [keep_ref[share : share + half, :], received_ref[share : share + half, :]], axis=0
    )
    copies[0].wait()
    row = lax.broadcasted_iota(jnp.int32, (own_rows, slots), 0)
    picks = (row == order_ref[...]).astype(F32).astype(BF16)
    added = product(picks, rows, 1, 0)
    copies[1].wait()
    base_ref[...] += added
    copy = pltpu.make_async_copy(base_ref, out_hbm, sems.at[2])
    copy.start()
    copy.wait()


def finish_kernel(factor, which, place_ref, half_ref, *refs):
    self_hbm, neigh_hbm, wide_ref, sems = refs[-4:]
    wide_ref[...] = half_ref[...].astype(F32) * factor
    matrix = (place_ref[0] + which) % 2

    @pl.when(matrix == 0)
    def _():
        pltpu.sync_copy(wide_ref, self_hbm)

    @pl.when(matrix == 1)
    def _():
        pltpu.sync_copy(wide_ref, neigh_hbm)


def local(features, cotangent, w_self, w_neigh, bias, neighbours, neigh_count, serve_rows):
    own_rows, width = features.shape
    fanout = neighbours.shape[1]
    across, near = lax.axis_size("across"), lax.axis_size("near")
    peers = across * near
    devices = 4 * peers
    slots = serve_rows.shape[1]
    cap = slots // devices
    half = slots // 2
    table_rows = own_rows + slots
    share = own_rows // peers
    length = -(-(share + 4 * cap + 1) // 8) * 8
    everyone = ("across", "core", "wide", "near")
    cube = ("across", "near")
    dims = (across, near, cap)
    place = jnp.stack([lax.axis_index("core"), lax.axis_index("wide")]).astype(jnp.int32)
    swap = [(0, 1), (1, 0)]
    factor = 1.0 / math.sqrt(own_rows * devices)
    work = 2 * own_rows * own_rows * width
    square16 = shape((own_rows, width), BF16)
    square32 = shape((own_rows, width), F32)

    (outgoing,) = call(
        "serve", serve_kernel, (HBM, HBM), ((shape((devices, cap, width), BF16), VMEM),),
        scratch=[VMEM((1, slots), jnp.int32), VMEM((own_rows, width), BF16)],
        copies=2, flops=work // 4, moved=1 << 20,
    )(serve_rows, features)
    incoming = lax.all_to_all(outgoing, everyone, 0, 0, tiled=True)
    results = (
        shape((table_rows, own_rows), BF16),
        shape((own_rows, 128), F32),
        square32,
        square32,
        shape((1, slots), jnp.int32),
    )
    counts, inverse, own_sum, pre, order = call(
        "own_aggregate", functools.partial(own_kernel, dims),
        (SMEM,) + (HBM,) * 6, tuple((result, HBM) for result in results),
        scratch=[
            VMEM((fanout, own_rows), jnp.int32),
            VMEM((1, own_rows), jnp.int32),
            VMEM((1, slots), jnp.int32),
            VMEM((own_rows, width), BF16),
            VMEM((width, width), BF16),
            VMEM((1, width), F32),
            *(VMEM(result.shape, result.dtype) for result in results),
            VMEM((fanout, own_rows), jnp.int32),
        ],
        copies=11, flops=20 * work, moved=4 << 20,
    )(
        place, neighbours.T, neigh_count.reshape(1, own_rows), serve_rows, features, w_self,
        bias.reshape(1, width),
    )
    send, keep, keep_rows, own_bias, pre_grad, message = call(
        "layer_grad", main_kernel, (SMEM, VMEM) + (HBM,) * 7,
        (
            (shape((own_rows + half + 16, width), BF16), VMEM),
            (square32, VMEM),
            (shape((across, 2 * near * cap, width), BF16), VMEM),
            (shape((16, width), BF16), VMEM),
            (square16, VMEM),
            (square16, VMEM),
        ),
        scratch=[
            VMEM((slots, own_rows), BF16),
            VMEM((own_rows, 128), F32),
            VMEM((own_rows, width), F32),
            VMEM((own_rows, width), F32),
            VMEM((own_rows, width), BF16),
            VMEM((own_rows, width), BF16),
            VMEM((width, width), BF16),
            VMEM((slots, width), F32),
        ],
        copies=7, flops=5 * work, moved=8 << 20,
    )(place, incoming, counts, inverse, own_sum, pre, features, cotangent, w_neigh)
    received = lax.ppermute(send, "core", swap)
    (base,) = call(
        "own_grad", own_grad_kernel, (VMEM, VMEM, HBM, HBM), ((square32, HBM),),
        scratch=[
            VMEM((width, width), BF16), VMEM((own_rows, own_rows), BF16), VMEM((own_rows, width), F32)
        ],
        copies=3, flops=2 * work, moved=4 << 20,
    )(pre_grad, message, w_self, counts)
    (payload,) = call(
        "pack", functools.partial(pack_kernel, dims), (VMEM,) * 4 + (HBM,),
        ((shape((peers, length, width), BF16), VMEM),), flops=work // 4, moved=4 << 20,
    )(received, keep, keep_rows, own_bias, base)
    arrived = lax.all_to_all(payload, cube, 0, 0, tiled=True)
    pairs = shape((share + half + 16, width), BF16)
    keep_sum, send_sum = call(
        "sum_shares", functools.partial(sum_kernel, cap, share), (SMEM, VMEM), ((pairs, VMEM), (pairs, VMEM)),
        flops=work // 8, moved=1 << 20,
    )(place, arrived)
    received_sum = lax.ppermute(send_sum, "wide", swap)
    copies_out, bias_sum = call(
        "total", functools.partial(total_kernel, factor), (VMEM, VMEM),
        ((shape((peers, share, width), BF16), VMEM), (shape((1, width), F32), VMEM)),
        flops=work // 8, moved=1 << 20,
    )(keep_sum, received_sum)
    mine = lax.all_to_all(copies_out, cube, 0, 0, tiled=True).reshape(own_rows, width)
    (grad_features,) = call(
        "owner_sum", functools.partial(owner_kernel, share), (HBM, VMEM, VMEM, HBM), ((square32, HBM),),
        scratch=[VMEM((1, slots), jnp.int32), VMEM((own_rows, width), F32)],
        copies=3, flops=work, moved=3 << 20,
    )(order, keep_sum, received_sum, base)
    other = lax.ppermute(mine, "core", swap)
    halves = ((square32, HBM), (square32, HBM))
    scratch = [VMEM((own_rows, width), F32)]
    parts = call(
        "finish_mine", functools.partial(finish_kernel, factor, 0), (SMEM, VMEM, HBM), halves,
        scratch=scratch, copies=1, flops=work // 2, moved=3 << 20,
    )(place, mine, grad_features)
    grad_self, grad_neigh = call(
        "finish_other", functools.partial(finish_kernel, factor, 1), (SMEM, VMEM, HBM, HBM), halves,
        scratch=scratch, copies=1, flops=work // 2, moved=3 << 20, aliases={2: 0, 3: 1},
    )(place, other, *parts)
    return grad_features, grad_self, grad_neigh, bias_sum.reshape(width)


def solution(mesh):
    groups, members = mesh.shape["group"], mesh.shape["member"]
    nodes = ("across", "core", "wide", "near")
    fine = Mesh(mesh.devices.reshape(groups // 2, 2, 2, members // 2), nodes)
    rows = P(nodes, None)
    return jax.shard_map(
        local,
        mesh=fine,
        in_specs=(rows, rows, P(), P(), P(), rows, P(nodes), rows),
        out_specs=(rows, P(), P(), P()),
        check_vma=False,
    )
```

```python
import functools
import math

import jax
import jax.numpy as jnp
from jax import lax
from jax.experimental import pallas as pl
from jax.experimental.pallas import tpu as pltpu
from jax.sharding import Mesh
from jax.sharding import PartitionSpec as P

BF16 = jnp.bfloat16
F32 = jnp.float32
VMEM, HBM = pltpu.VMEM, pltpu.HBM
shape = jax.ShapeDtypeStruct


def product(left, right, left_dim, right_dim):
    return lax.dot_general(
        left, right, (((left_dim,), (right_dim,)), ((), ())), preferred_element_type=F32
    )


def call(name, body, ins, outs, scratch=(), copies=0, flops=0, moved=0, aliases=None):
    scratch = list(scratch)
    if copies:
        scratch.append(pltpu.SemaphoreType.DMA((copies,)))
    run = pl.pallas_call(
        body,
        out_shape=tuple(
            HBM(out.shape, out.dtype) if memory is HBM else out for out, memory in outs
        ),
        in_specs=[pl.BlockSpec(memory_space=memory) for memory in ins],
        out_specs=tuple(pl.BlockSpec(memory_space=memory) for _, memory in outs),
        scratch_shapes=scratch,
        input_output_aliases=aliases or {},
        compiler_params=pltpu.CompilerParams(vmem_limit_bytes=48 * 1024 * 1024),
        cost_estimate=pl.CostEstimate(flops=flops, bytes_accessed=moved, transcendentals=0),
        name=name,
    )

    def held(*operands):
        return run(*(
            pltpu.with_memory_space_constraint(operand, HBM) if memory is HBM else operand
            for operand, memory in zip(operands, ins, strict=True)
        ))

    return held


def start_all(sems, *pairs):
    copies = [pltpu.make_async_copy(a, b, sems.at[at]) for at, (a, b) in enumerate(pairs)]
    for copy in copies:
        copy.start()
    return copies


def serve_kernel(serve_hbm, features_hbm, out_ref, serve_ref, features_ref, sems):
    copies = start_all(sems, (serve_hbm, serve_ref), (features_hbm, features_ref))
    own_rows = features_ref.shape[0]
    slots = serve_ref.shape[1]
    copies[0].wait()
    row = lax.broadcasted_iota(jnp.int32, (own_rows, slots), 0)
    picks = (row == serve_ref[...]).astype(F32).astype(BF16)
    copies[1].wait()
    rows = product(picks, features_ref[...], 0, 0)
    out_ref[...] = rows.reshape(out_ref.shape).astype(BF16)


def own_kernel(
    dims, neighbours_ref, count_ref, serve_ref, features_ref, w_self_ref, bias_ref,
    counts_ref, slot_counts_ref, inverse_ref, order_ref, flipped_hbm, pre_hbm,
    flipped_ref, pre_ref, live_ref, table_ref, sems,
):
    fanout, own_rows = neighbours_ref.shape
    table_rows = table_ref.shape[0]
    features = features_ref[...]
    flipped_ref[...] = features.T
    pre_ref[...] = product(features, w_self_ref[...], 1, 0) + bias_ref[...]
    copies = start_all(sems, (flipped_ref, flipped_hbm), (pre_ref, pre_hbm))
    count = count_ref[...]
    position = lax.broadcasted_iota(jnp.int32, (fanout, own_rows), 0)
    live_ref[...] = jnp.where(position < count, neighbours_ref[...], -1)
    inverse_ref[...] = jnp.broadcast_to(1.0 / count.astype(F32), (128, own_rows)).T
    step = 32

    def fill(at, carry):
        start = pl.multiple_of(at * step, step)
        row = lax.broadcasted_iota(jnp.int32, (step, own_rows), 0) + start
        total = jnp.zeros((step, own_rows), F32)
        for k in range(fanout):
            total = total + jnp.where(row == live_ref[k : k + 1, :], 1.0, 0.0)
        table_ref[pl.ds(start, step), :] = total.astype(BF16)
        return carry

    lax.fori_loop(0, table_rows // step, fill, 0)
    counts_ref[...] = table_ref[...].T
    slot_counts_ref[...] = table_ref[own_rows:, :]
    across, near, cap = dims
    slots = serve_ref.shape[1]
    to = lax.broadcasted_iota(jnp.int32, (slots, slots), 1)
    slot = to % cap
    core = (to // cap % 2 + lax.axis_index("core")) % 2
    n = to // (2 * cap) % near
    a = to // (2 * cap * near) % across
    wide = (to // (2 * cap * near * across) + lax.axis_index("wide")) % 2
    source = (((a * 2 + core) * 2 + wide) * near + n) * cap + slot
    at = lax.broadcasted_iota(jnp.int32, (slots, slots), 0)
    moves = (at == source).astype(F32).astype(BF16)
    serve = serve_ref[...]
    high = (serve // 32).astype(F32).astype(BF16)
    low = (serve % 32).astype(F32).astype(BF16)
    order_ref[...] = (
        product(high, moves, 1, 0) * 32.0 + product(low, moves, 1, 0)
    ).astype(jnp.int32)
    for copy in copies:
        copy.wait()


def spread_wide(inverse, width):
    return jnp.concatenate([inverse] * (width // 128), axis=1)


def main_kernel(
    incoming_ref, counts_ref, slot_counts_ref, inverse_ref, features_ref, w_neigh_ref,
    pre_hbm, cotangent_hbm, flipped_hbm,
    send_ref, keep_ref, keep_rows_ref, bias_ref, pre_grad_ref, message_ref,
    pre_ref, cotangent_ref, flipped_ref, rows_ref, sems,
):
    own_rows, width = features_ref.shape
    slots = rows_ref.shape[0]
    copies = start_all(
        sems, (pre_hbm, pre_ref), (cotangent_hbm, cotangent_ref), (flipped_hbm, flipped_ref)
    )
    core = lax.axis_index("core")
    first = core == 0
    incoming = incoming_ref[...].astype(F32).reshape(slots, width).astype(BF16)
    summed = product(counts_ref[:, :own_rows], features_ref[...], 1, 0) + product(
        counts_ref[:, own_rows:], incoming, 1, 0
    )
    inverse = spread_wide(inverse_ref[...], width)
    aggregated = (summed * inverse).astype(BF16)
    mixed = product(aggregated, w_neigh_ref[...], 1, 0)
    copies[0].wait()
    pre = pre_ref[...] + mixed
    sigmoid_pre = jax.nn.sigmoid(pre)
    copies[1].wait()
    pre_grad = (
        cotangent_ref[...].astype(F32) * sigmoid_pre * (1.0 + pre * (1.0 - sigmoid_pre))
    ).astype(BF16)
    pre_grad_ref[...] = pre_grad
    copies[2].wait()
    grad_self = product(flipped_ref[...], pre_grad, 1, 0)
    grad_neigh = product(aggregated, pre_grad, 0, 0)
    keep_ref[...] = jnp.where(first, grad_self, grad_neigh)
    send_ref[:own_rows, :] = jnp.where(first, grad_neigh, grad_self).astype(BF16)
    message = (product(pre_grad, w_neigh_ref[...], 1, 1) * inverse).astype(BF16)
    message_ref[...] = message
    rows_ref[...] = product(slot_counts_ref[...], message, 1, 0)
    half = slots // 2
    blocks, length = keep_rows_ref.shape[0], keep_rows_ref.shape[1]
    for at in range(blocks):
        mine = pl.multiple_of((at * 2 + core) * length, length)
        other = pl.multiple_of((at * 2 + 1 - core) * length, length)
        keep_rows_ref[at] = rows_ref[pl.ds(mine, length), :].astype(BF16)
        send_ref[own_rows + at * length : own_rows + (at + 1) * length, :] = rows_ref[
            pl.ds(other, length), :
        ].astype(BF16)
    bias = jnp.sum(pre_grad.astype(F32), axis=0, keepdims=True).astype(BF16)
    bias_ref[...] = jnp.broadcast_to(bias, bias_ref.shape)
    send_ref[own_rows + half :, :] = jnp.broadcast_to(bias, bias_ref.shape)


def own_grad_kernel(pre_grad_ref, message_ref, w_self_ref, counts_ref, out_ref):
    own_rows = pre_grad_ref.shape[0]
    out_ref[...] = product(pre_grad_ref[...], w_self_ref[...], 1, 1) + product(
        counts_ref[:, :own_rows], message_ref[...], 0, 0
    )


def pack_kernel(dims, received_ref, keep_ref, keep_rows_ref, bias_ref, after_ref, out_ref):
    across, near, cap = dims
    own_rows, width = keep_ref.shape
    peers, length = out_ref.shape[0], out_ref.shape[1]
    half = 2 * peers * cap
    share = own_rows // peers
    keep_rows = keep_rows_ref[...].astype(F32).reshape(half, width)
    other_rows = received_ref[own_rows : own_rows + half, :].astype(F32)
    bias = bias_ref[...].astype(F32) + received_ref[own_rows + half :, :].astype(F32)
    summed = keep_ref[...] + received_ref[:own_rows, :].astype(F32)
    for peer in range(peers):
        parts = [summed[peer * share : (peer + 1) * share]]
        for wide in range(2):
            at = ((peer // near * 2 + wide) * near + peer % near) * cap
            parts += [keep_rows[at : at + cap], other_rows[at : at + cap]]
        parts.append(bias[: length - share - 4 * cap])
        out_ref[peer] = jnp.concatenate(parts, axis=0).astype(BF16)


def sum_kernel(cap, share, payload_ref, keep_ref, send_ref):
    peers, length, width = payload_ref.shape
    pair = 2 * cap
    count = peers * pair
    grads = jnp.zeros((share, width), F32)
    bias = jnp.zeros((8, width), F32)
    lower, upper = [], []
    for peer in range(peers):
        grads = grads + payload_ref[peer, :share, :].astype(F32)
        rest = payload_ref[peer, share:, :].astype(F32)
        lower.append(rest[:pair])
        upper.append(rest[pair : 2 * pair])
        bias = bias + jnp.broadcast_to(rest[2 * pair : 2 * pair + 1], bias.shape)
    grads = grads.astype(BF16)
    bias = jnp.concatenate([bias, bias], axis=0).astype(BF16)
    first = lax.axis_index("wide") == 0
    lower, upper = jnp.concatenate(lower, axis=0), jnp.concatenate(upper, axis=0)
    for ref, rows in (
        (keep_ref, jnp.where(first, lower, upper)),
        (send_ref, jnp.where(first, upper, lower)),
    ):
        ref[:share, :] = grads
        ref[share : share + count, :] = rows.astype(BF16)
        ref[share + count :, :] = bias


def total_kernel(keep_ref, received_ref, out_ref):
    peers, share, width = out_ref.shape
    total = (keep_ref[:share, :].astype(F32) + received_ref[:share, :].astype(F32)).astype(BF16)
    for peer in range(peers):
        out_ref[peer] = total


def send_half(matrix, source_ref, self_hbm, neigh_hbm, sem, rows, wait):
    source = source_ref.at[rows, :]
    for index, target in enumerate((self_hbm, neigh_hbm)):

        @pl.when(matrix == index)
        def _(target=target):
            copy = pltpu.make_async_copy(source, target.at[rows, :], sem)
            if wait:
                copy.wait()
            else:
                copy.start()


def tail_kernel(
    factor, share, order_ref, keep_ref, received_ref, base_ref, mine_ref,
    out_hbm, self_hbm, neigh_hbm, bias_hbm, wide_ref, out_ref, bias_ref, sems,
):
    own_rows, slots = base_ref.shape[0], order_ref.shape[1]
    half = slots // 2
    matrix = lax.axis_index("core")
    everything = pl.ds(0, own_rows)
    wide_ref[...] = mine_ref[...].astype(F32) * factor
    send_half(matrix, wide_ref, self_hbm, neigh_hbm, sems.at[0], everything, False)
    last = keep_ref.shape[0] - 16
    bias = keep_ref[last:, :].astype(F32) + received_ref[last:, :].astype(F32)
    bias_ref[...] = bias[:1] * factor
    copies = [pltpu.make_async_copy(bias_ref, bias_hbm, sems.at[1])]
    copies[0].start()
    rows = jnp.concatenate(
        [keep_ref[share : share + half, :], received_ref[share : share + half, :]], axis=0
    )
    row = lax.broadcasted_iota(jnp.int32, (own_rows, slots), 0)
    picks = (row == order_ref[...]).astype(F32).astype(BF16)
    out_ref[...] = base_ref[...] + product(picks, rows, 1, 0)
    copies.append(pltpu.make_async_copy(out_ref, out_hbm, sems.at[2]))
    copies[1].start()
    send_half(matrix, wide_ref, self_hbm, neigh_hbm, sems.at[0], everything, True)
    for copy in copies:
        copy.wait()


def other_kernel(factor, half_ref, self_in, neigh_in, self_hbm, neigh_hbm, wide_ref, sems):
    own_rows = half_ref.shape[0]
    pieces = 4
    length = own_rows // pieces
    matrix = 1 - lax.axis_index("core")
    spans = [pl.ds(at * length, length) for at in range(pieces)]
    for at, span in enumerate(spans):
        wide_ref[span, :] = half_ref[span, :].astype(F32) * factor
        send_half(matrix, wide_ref, self_hbm, neigh_hbm, sems.at[at], span, False)
    for at, span in enumerate(spans):
        send_half(matrix, wide_ref, self_hbm, neigh_hbm, sems.at[at], span, True)


def local(features, cotangent, w_self, w_neigh, bias, neighbours, neigh_count, serve_rows):
    own_rows, width = features.shape
    fanout = neighbours.shape[1]
    across, near = lax.axis_size("across"), lax.axis_size("near")
    peers = across * near
    devices = 4 * peers
    slots = serve_rows.shape[1]
    cap = slots // devices
    half = slots // 2
    table_rows = own_rows + slots
    share = own_rows // peers
    length = -(-(share + 4 * cap + 1) // 8) * 8
    everyone = ("across", "core", "wide", "near")
    cube = ("across", "near")
    dims = (across, near, cap)
    swap = [(0, 1), (1, 0)]
    factor = 1.0 / math.sqrt(own_rows * devices)
    work = 2 * own_rows * own_rows * width
    square16 = shape((own_rows, width), BF16)
    square32 = shape((own_rows, width), F32)

    (outgoing,) = call(
        "serve", serve_kernel, (HBM, HBM), ((shape((devices, cap, width), BF16), VMEM),),
        scratch=[VMEM((1, slots), jnp.int32), VMEM((own_rows, width), BF16)],
        copies=2, flops=work // 4, moved=1 << 20,
    )(serve_rows, features)
    incoming = lax.all_to_all(outgoing, everyone, 0, 0, tiled=True)
    counts, slot_counts, inverse, order, flipped, pre = call(
        "own_aggregate", functools.partial(own_kernel, dims), (VMEM,) * 6,
        (
            (shape((own_rows, table_rows), BF16), VMEM),
            (shape((slots, own_rows), BF16), VMEM),
            (shape((own_rows, 128), F32), VMEM),
            (shape((1, slots), jnp.int32), VMEM),
            (shape((width, own_rows), BF16), HBM),
            (square32, HBM),
        ),
        scratch=[
            VMEM((width, own_rows), BF16),
            VMEM((own_rows, width), F32),
            VMEM((fanout, own_rows), jnp.int32),
            VMEM((table_rows, own_rows), BF16),
        ],
        copies=2, flops=20 * work, moved=4 << 20,
    )(
        neighbours.T, neigh_count.reshape(1, own_rows), serve_rows, features, w_self,
        bias.reshape(1, width),
    )
    send, keep, keep_rows, own_bias, pre_grad, message = call(
        "layer_grad", main_kernel, (VMEM,) * 6 + (HBM,) * 3,
        (
            (shape((own_rows + half + 16, width), BF16), VMEM),
            (square32, VMEM),
            (shape((across, 2 * near * cap, width), BF16), VMEM),
            (shape((16, width), BF16), VMEM),
            (square16, VMEM),
            (square16, VMEM),
        ),
        scratch=[
            VMEM((own_rows, width), F32),
            VMEM((own_rows, width), BF16),
            VMEM((width, own_rows), BF16),
            VMEM((slots, width), F32),
        ],
        copies=3, flops=5 * work, moved=8 << 20,
    )(incoming, counts, slot_counts, inverse, features, w_neigh, pre, cotangent, flipped)
    received = lax.ppermute(send, "core", swap)
    (base,) = call(
        "own_grad", own_grad_kernel, (VMEM,) * 4, ((square32, VMEM),), flops=2 * work, moved=4 << 20,
    )(pre_grad, message, w_self, counts)
    (payload,) = call(
        "pack", functools.partial(pack_kernel, dims), (VMEM,) * 5,
        ((shape((peers, length, width), BF16), VMEM),), flops=work // 4, moved=4 << 20,
    )(received, keep, keep_rows, own_bias, base)
    arrived = lax.all_to_all(payload, cube, 0, 0, tiled=True)
    pairs = shape((share + half + 16, width), BF16)
    keep_sum, send_sum = call(
        "sum_shares", functools.partial(sum_kernel, cap, share), (VMEM,),
        ((pairs, VMEM), (pairs, VMEM)), flops=work // 8, moved=1 << 20,
    )(arrived)
    received_sum = lax.ppermute(send_sum, "wide", swap)
    (total,) = call(
        "total", total_kernel, (VMEM, VMEM), ((shape((peers, share, width), BF16), VMEM),),
        flops=work // 8, moved=1 << 20,
    )(keep_sum, received_sum)
    mine = lax.all_to_all(total, cube, 0, 0, tiled=True).reshape(own_rows, width)
    other = lax.ppermute(mine, "core", swap)
    wide = VMEM((own_rows, width), F32)
    grad_features, self_part, neigh_part, bias_sum = call(
        "tail", functools.partial(tail_kernel, factor, share), (VMEM,) * 5,
        ((square32, HBM), (square32, HBM), (square32, HBM), (shape((1, width), F32), HBM)),
        scratch=[wide, wide, VMEM((1, width), F32)], copies=3, flops=work, moved=4 << 20,
    )(order, keep_sum, received_sum, base, mine)
    grad_self, grad_neigh = call(
        "other_half", functools.partial(other_kernel, factor), (VMEM, HBM, HBM),
        ((square32, HBM), (square32, HBM)),
        scratch=[wide], copies=4, flops=work // 2, moved=3 << 20, aliases={1: 0, 2: 1},
    )(other, self_part, neigh_part)
    return grad_features, grad_self, grad_neigh, bias_sum.reshape(width)


def solution(mesh):
    groups, members = mesh.shape["group"], mesh.shape["member"]
    nodes = ("across", "core", "wide", "near")
    fine = Mesh(mesh.devices.reshape(groups // 2, 2, 2, members // 2), nodes)
    rows = P(nodes, None)
    return jax.shard_map(
        local,
        mesh=fine,
        in_specs=(rows, rows, P(), P(), P(), rows, P(nodes), rows),
        out_specs=(rows, P(), P(), P()),
        check_vma=False,
    )
```

```python
import functools
import math

import jax
import jax.numpy as jnp
from jax import lax
from jax.experimental import pallas as pl
from jax.experimental.pallas import tpu as pltpu
from jax.sharding import Mesh
from jax.sharding import PartitionSpec as P

BF16 = jnp.bfloat16
F32 = jnp.float32
VMEM, HBM = pltpu.VMEM, pltpu.HBM
shape = jax.ShapeDtypeStruct


def product(left, right, left_dim, right_dim):
    return lax.dot_general(
        left, right, (((left_dim,), (right_dim,)), ((), ())), preferred_element_type=F32
    )


def call(name, body, ins, outs, scratch=(), copies=0, flops=0, moved=0, aliases=None):
    scratch = list(scratch)
    if copies:
        scratch.append(pltpu.SemaphoreType.DMA((copies,)))
    run = pl.pallas_call(
        body,
        out_shape=tuple(
            HBM(out.shape, out.dtype) if memory is HBM else out for out, memory in outs
        ),
        in_specs=[pl.BlockSpec(memory_space=memory) for memory in ins],
        out_specs=tuple(pl.BlockSpec(memory_space=memory) for _, memory in outs),
        scratch_shapes=scratch,
        input_output_aliases=aliases or {},
        compiler_params=pltpu.CompilerParams(vmem_limit_bytes=48 * 1024 * 1024),
        cost_estimate=pl.CostEstimate(flops=flops, bytes_accessed=moved, transcendentals=0),
        name=name,
    )

    def held(*operands):
        return run(*(
            pltpu.with_memory_space_constraint(operand, HBM) if memory is HBM else operand
            for operand, memory in zip(operands, ins, strict=True)
        ))

    return held


def start_all(sems, *pairs):
    copies = [pltpu.make_async_copy(a, b, sems.at[at]) for at, (a, b) in enumerate(pairs)]
    for copy in copies:
        copy.start()
    return copies


def serve_kernel(serve_hbm, features_hbm, out_ref, serve_ref, features_ref, sems):
    copies = start_all(sems, (serve_hbm, serve_ref), (features_hbm, features_ref))
    own_rows = features_ref.shape[0]
    slots = serve_ref.shape[1]
    copies[0].wait()
    wanted = jnp.broadcast_to(serve_ref[...], (128, slots)).astype(F32).T
    row = lax.broadcasted_iota(jnp.int32, (slots, 128), 1).astype(F32)
    picks = jnp.concatenate(
        [
            jnp.where(row + float(at) == wanted, 1.0, 0.0).astype(BF16)
            for at in range(0, own_rows, 128)
        ],
        axis=1,
    )
    copies[1].wait()
    rows = product(picks, features_ref[...], 1, 0)
    out_ref[...] = rows.reshape(out_ref.shape).astype(BF16)


def own_kernel(
    dims, neighbours_hbm, count_hbm, serve_hbm, features_hbm, w_self_hbm, bias_hbm,
    own_sum_ref, fetch_counts_ref, slot_counts_ref, inverse_ref, order_ref, top_ref, low_hbm, own_counts_hbm,
    neighbours_ref, count_ref, serve_ref, features_ref, w_self_ref, bias_ref, low_ref, live_ref, table_ref, sems,
):
    ins = start_all(
        sems,
        (neighbours_hbm, neighbours_ref),
        (count_hbm, count_ref),
        (serve_hbm, serve_ref),
        (features_hbm, features_ref),
        (w_self_hbm, w_self_ref),
        (bias_hbm, bias_ref),
    )
    fanout, own_rows = neighbours_ref.shape
    table_rows = table_ref.shape[0]
    for copy in ins:
        copy.wait()
    features = features_ref[...]
    upper = own_rows // 2
    low_ref[...] = product(features[upper:], w_self_ref[...], 1, 0) + bias_ref[...]
    copies = [pltpu.make_async_copy(low_ref, low_hbm, sems.at[len(ins)])]
    copies[0].start()
    top_ref[...] = product(features[:upper], w_self_ref[...], 1, 0) + bias_ref[...]
    count = count_ref[...]
    position = lax.broadcasted_iota(jnp.int32, (fanout, own_rows), 0)
    live_ref[...] = jnp.where(position < count, neighbours_ref[...], -1)
    inverse_ref[...] = jnp.broadcast_to(1.0 / count.astype(F32), (128, own_rows)).T
    step = 32

    def fill(at, carry):
        start = pl.multiple_of(at * step, step)
        row = lax.broadcasted_iota(jnp.int32, (step, own_rows), 0) + start
        total = jnp.zeros((step, own_rows), F32)
        for k in range(fanout):
            total = total + jnp.where(row == live_ref[k : k + 1, :], 1.0, 0.0)
        table_ref[pl.ds(start, step), :] = total.astype(BF16)
        return carry

    lax.fori_loop(0, table_rows // step, fill, 0)
    own_counts = table_ref.at[pl.ds(0, own_rows), :]
    copies.append(pltpu.make_async_copy(own_counts, own_counts_hbm, sems.at[len(ins) + 1]))
    copies[-1].start()
    own_sum_ref[...] = product(table_ref[:own_rows, :], features, 0, 0)
    fetch_counts_ref[...] = table_ref[own_rows:, :].T
    slot_counts_ref[...] = table_ref[own_rows:, :]
    across, near, cap = dims
    slots = serve_ref.shape[1]
    to = lax.broadcasted_iota(jnp.int32, (slots, slots), 1)
    slot = to % cap
    core = (to // cap % 2 + lax.axis_index("core")) % 2
    n = to // (2 * cap) % near
    a = to // (2 * cap * near) % across
    wide = (to // (2 * cap * near * across) + lax.axis_index("wide")) % 2
    source = (((a * 2 + core) * 2 + wide) * near + n) * cap + slot
    at = lax.broadcasted_iota(jnp.int32, (slots, slots), 0)
    moves = (at == source).astype(F32).astype(BF16)
    serve = serve_ref[...]
    high = (serve // 32).astype(F32).astype(BF16)
    low = (serve % 32).astype(F32).astype(BF16)
    order_ref[...] = (
        product(high, moves, 1, 0) * 32.0 + product(low, moves, 1, 0)
    ).astype(jnp.int32)
    for copy in copies:
        copy.wait()


def spread_wide(inverse, width):
    return jnp.concatenate([inverse] * (width // 128), axis=1)


def main_kernel(
    incoming_ref, own_sum_ref, fetch_counts_ref, slot_counts_ref, inverse_ref, w_neigh_ref, cotangent_ref, top_ref,
    low_hbm, features_hbm,
    send_ref, keep_ref, keep_rows_ref, bias_ref, pre_grad_ref, message_ref,
    low_ref, left_ref, rows_ref, sems,
):
    own_rows, width = own_sum_ref.shape
    slots = rows_ref.shape[0]
    core = lax.axis_index("core")
    copies = start_all(sems, (low_hbm, low_ref), (features_hbm, left_ref.at[0]))
    incoming = incoming_ref[...].astype(F32).reshape(slots, width).astype(BF16)
    inverse = spread_wide(inverse_ref[...], width)
    summed = own_sum_ref[...] + product(fetch_counts_ref[...], incoming, 1, 0)
    aggregated = (summed * inverse).astype(BF16)
    left_ref[1] = aggregated
    upper = own_rows // 2
    for at, part_ref in enumerate((top_ref, low_ref)):
        rows = slice(at * upper, (at + 1) * upper)
        mixed = product(aggregated[rows], w_neigh_ref[...], 1, 0)
        if at:
            copies[0].wait()
        pre = part_ref[...] + mixed
        sigmoid_pre = jax.nn.sigmoid(pre)
        pre_grad_ref[rows] = (
            cotangent_ref[rows].astype(F32) * sigmoid_pre * (1.0 + pre * (1.0 - sigmoid_pre))
        ).astype(BF16)
    pre_grad = pre_grad_ref[...]
    message = (product(pre_grad, w_neigh_ref[...], 1, 1) * inverse).astype(BF16)
    message_ref[...] = message
    rows_ref[...] = product(slot_counts_ref[...], message, 1, 0)
    copies[1].wait()
    keep_ref[...] = product(left_ref[core], pre_grad, 0, 0)
    send_ref[:own_rows, :] = product(left_ref[1 - core], pre_grad, 0, 0).astype(BF16)
    half = slots // 2
    blocks, length = keep_rows_ref.shape[0], keep_rows_ref.shape[1]
    for at in range(blocks):
        mine = pl.multiple_of((at * 2 + core) * length, length)
        other = pl.multiple_of((at * 2 + 1 - core) * length, length)
        keep_rows_ref[at] = rows_ref[pl.ds(mine, length), :].astype(BF16)
        send_ref[own_rows + at * length : own_rows + (at + 1) * length, :] = rows_ref[
            pl.ds(other, length), :
        ].astype(BF16)
    bias = jnp.sum(pre_grad.astype(F32), axis=0, keepdims=True).astype(BF16)
    bias_ref[...] = jnp.broadcast_to(bias, bias_ref.shape)
    send_ref[own_rows + half :, :] = jnp.broadcast_to(bias, bias_ref.shape)


def own_grad_kernel(
    pre_grad_ref, message_ref, w_self_hbm, counts_hbm, out_ref, w_self_ref, counts_ref, sems
):
    copies = start_all(sems, (counts_hbm, counts_ref), (w_self_hbm, w_self_ref))
    copies[0].wait()
    spread = product(counts_ref[...], message_ref[...], 1, 0)
    copies[1].wait()
    out_ref[...] = spread + product(pre_grad_ref[...], w_self_ref[...], 1, 1)


def pack_kernel(dims, received_ref, keep_ref, keep_rows_ref, bias_ref, out_ref):
    across, near, cap = dims
    own_rows, width = keep_ref.shape
    peers, length = out_ref.shape[0], out_ref.shape[1]
    half = 2 * peers * cap
    share = own_rows // peers
    keep_rows = keep_rows_ref[...].astype(F32).reshape(half, width)
    other_rows = received_ref[own_rows : own_rows + half, :].astype(F32)
    bias = bias_ref[...].astype(F32) + received_ref[own_rows + half :, :].astype(F32)
    summed = keep_ref[...] + received_ref[:own_rows, :].astype(F32)
    for peer in range(peers):
        parts = [summed[peer * share : (peer + 1) * share]]
        for wide in range(2):
            at = ((peer // near * 2 + wide) * near + peer % near) * cap
            parts += [keep_rows[at : at + cap], other_rows[at : at + cap]]
        parts.append(bias[: length - share - 4 * cap])
        out_ref[peer] = jnp.concatenate(parts, axis=0).astype(BF16)


def sum_kernel(cap, share, payload_ref, keep_ref, send_ref):
    peers, length, width = payload_ref.shape
    pair = 2 * cap
    count = peers * pair
    grads = jnp.zeros((share, width), F32)
    bias = jnp.zeros((8, width), F32)
    lower, upper = [], []
    for peer in range(peers):
        grads = grads + payload_ref[peer, :share, :].astype(F32)
        rest = payload_ref[peer, share:, :].astype(F32)
        lower.append(rest[:pair])
        upper.append(rest[pair : 2 * pair])
        bias = bias + jnp.broadcast_to(rest[2 * pair : 2 * pair + 1], bias.shape)
    grads = grads.astype(BF16)
    bias = bias.astype(BF16)
    first = lax.axis_index("wide") == 0
    lower, upper = jnp.concatenate(lower, axis=0), jnp.concatenate(upper, axis=0)
    for ref, rows in (
        (keep_ref, jnp.where(first, lower, upper)),
        (send_ref, jnp.where(first, upper, lower)),
    ):
        ref[:share, :] = grads
        ref[share : share + count, :] = rows.astype(BF16)
        ref[share + count :, :] = bias


def total_kernel(keep_ref, received_ref, after_ref, out_ref):
    peers, share, width = out_ref.shape
    total = (keep_ref[:share, :].astype(F32) + received_ref[:share, :].astype(F32)).astype(BF16)
    for peer in range(peers):
        out_ref[peer] = total


def send_half(matrix, source_ref, self_hbm, neigh_hbm, sem, rows, wait):
    source = source_ref.at[rows, :]
    for index, target in enumerate((self_hbm, neigh_hbm)):

        @pl.when(matrix == index)
        def _(target=target):
            copy = pltpu.make_async_copy(source, target.at[rows, :], sem)
            if wait:
                copy.wait()
            else:
                copy.start()


def tail_kernel(
    factor, share, order_ref, keep_ref, received_ref, base_ref, mine_ref,
    out_hbm, self_hbm, neigh_hbm, bias_hbm, wide_ref, out_ref, bias_ref, sems,
):
    own_rows, slots = base_ref.shape[0], order_ref.shape[1]
    half = slots // 2
    matrix = lax.axis_index("core")
    everything = pl.ds(0, own_rows)
    wide_ref[...] = mine_ref[...].astype(F32) * factor
    send_half(matrix, wide_ref, self_hbm, neigh_hbm, sems.at[0], everything, False)
    last = keep_ref.shape[0] - 8
    bias = keep_ref[last:, :].astype(F32) + received_ref[last:, :].astype(F32)
    bias_ref[...] = bias[:1] * factor
    copies = [pltpu.make_async_copy(bias_ref, bias_hbm, sems.at[1])]
    copies[0].start()
    rows = jnp.concatenate(
        [keep_ref[share : share + half, :], received_ref[share : share + half, :]], axis=0
    )
    row = lax.broadcasted_iota(jnp.int32, (own_rows, slots), 0)
    picks = (row == order_ref[...]).astype(F32).astype(BF16)
    out_ref[...] = base_ref[...] + product(picks, rows, 1, 0)
    copies.append(pltpu.make_async_copy(out_ref, out_hbm, sems.at[2]))
    copies[1].start()
    send_half(matrix, wide_ref, self_hbm, neigh_hbm, sems.at[0], everything, True)
    for copy in copies:
        copy.wait()


def other_kernel(factor, half_ref, self_in, neigh_in, self_hbm, neigh_hbm, wide_ref, sems):
    own_rows = half_ref.shape[0]
    pieces = 4
    length = own_rows // pieces
    matrix = 1 - lax.axis_index("core")
    spans = [pl.ds(at * length, length) for at in range(pieces)]
    for at, span in enumerate(spans):
        wide_ref[span, :] = half_ref[span, :].astype(F32) * factor
        send_half(matrix, wide_ref, self_hbm, neigh_hbm, sems.at[at], span, False)
    for at, span in enumerate(spans):
        send_half(matrix, wide_ref, self_hbm, neigh_hbm, sems.at[at], span, True)


def local(features, cotangent, w_self, w_neigh, bias, neighbours, neigh_count, serve_rows):
    own_rows, width = features.shape
    fanout = neighbours.shape[1]
    across, near = lax.axis_size("across"), lax.axis_size("near")
    peers = across * near
    devices = 4 * peers
    slots = serve_rows.shape[1]
    cap = slots // devices
    half = slots // 2
    table_rows = own_rows + slots
    share = own_rows // peers
    length = -(-(share + 4 * cap + 1) // 8) * 8
    everyone = ("across", "core", "wide", "near")
    cube = ("across", "near")
    dims = (across, near, cap)
    swap = [(0, 1), (1, 0)]
    factor = 1.0 / math.sqrt(own_rows * devices)
    work = 2 * own_rows * own_rows * width
    square16 = shape((own_rows, width), BF16)
    square32 = shape((own_rows, width), F32)

    (outgoing,) = call(
        "serve", serve_kernel, (HBM, HBM), ((shape((devices, cap, width), BF16), VMEM),),
        scratch=[VMEM((1, slots), jnp.int32), VMEM((own_rows, width), BF16)],
        copies=2, flops=work // 4, moved=1 << 20,
    )(serve_rows, features)
    incoming = lax.all_to_all(outgoing, everyone, 0, 0, tiled=True)
    upper = shape((own_rows // 2, width), F32)
    own_sum, fetch_counts, slot_counts, inverse, order, top, low, own_counts = call(
        "own_aggregate", functools.partial(own_kernel, dims), (HBM,) * 6,
        (
            (square32, VMEM),
            (shape((own_rows, slots), BF16), VMEM),
            (shape((slots, own_rows), BF16), VMEM),
            (shape((own_rows, 128), F32), VMEM),
            (shape((1, slots), jnp.int32), VMEM),
            (upper, VMEM),
            (upper, HBM),
            (shape((own_rows, own_rows), BF16), HBM),
        ),
        scratch=[
            VMEM((fanout, own_rows), jnp.int32),
            VMEM((1, own_rows), jnp.int32),
            VMEM((1, slots), jnp.int32),
            VMEM((own_rows, width), BF16),
            VMEM((width, width), BF16),
            VMEM((1, width), F32),
            VMEM(upper.shape, F32),
            VMEM((fanout, own_rows), jnp.int32),
            VMEM((table_rows, own_rows), BF16),
        ],
        copies=8, flops=20 * work, moved=4 << 20,
    )(
        neighbours.T, neigh_count.reshape(1, own_rows), serve_rows, features, w_self,
        bias.reshape(1, width),
    )
    send, keep, keep_rows, own_bias, pre_grad, message = call(
        "layer_grad", main_kernel, (VMEM,) * 8 + (HBM,) * 2,
        (
            (shape((own_rows + half + 8, width), BF16), VMEM),
            (square32, VMEM),
            (shape((across, 2 * near * cap, width), BF16), VMEM),
            (shape((8, width), BF16), VMEM),
            (square16, VMEM),
            (square16, VMEM),
        ),
        scratch=[
            VMEM(upper.shape, F32),
            VMEM((2, own_rows, width), BF16),
            VMEM((slots, width), F32),
        ],
        copies=2, flops=5 * work, moved=8 << 20,
    )(incoming, own_sum, fetch_counts, slot_counts, inverse, w_neigh, cotangent, top, low, features)
    received = lax.ppermute(send, "core", swap)
    (base,) = call(
        "own_grad", own_grad_kernel, (VMEM, VMEM, HBM, HBM), ((square32, VMEM),),
        scratch=[VMEM((width, width), BF16), VMEM((own_rows, own_rows), BF16)],
        copies=2, flops=2 * work, moved=4 << 20,
    )(pre_grad, message, w_self, own_counts)
    (payload,) = call(
        "pack", functools.partial(pack_kernel, dims), (VMEM,) * 4,
        ((shape((peers, length, width), BF16), VMEM),), flops=work // 4, moved=4 << 20,
    )(received, keep, keep_rows, own_bias)
    arrived = lax.all_to_all(payload, cube, 0, 0, tiled=True)
    pairs = shape((share + half + 8, width), BF16)
    keep_sum, send_sum = call(
        "sum_shares", functools.partial(sum_kernel, cap, share), (VMEM,),
        ((pairs, VMEM), (pairs, VMEM)), flops=work // 8, moved=1 << 20,
    )(arrived)
    received_sum = lax.ppermute(send_sum, "wide", swap)
    (total,) = call(
        "total", total_kernel, (VMEM, VMEM, VMEM), ((shape((peers, share, width), BF16), VMEM),),
        flops=work // 8, moved=1 << 20,
    )(keep_sum, received_sum, base)
    mine = lax.all_to_all(total, cube, 0, 0, tiled=True).reshape(own_rows, width)
    other = lax.ppermute(mine, "core", swap)
    wide = VMEM((own_rows, width), F32)
    grad_features, self_part, neigh_part, bias_sum = call(
        "tail", functools.partial(tail_kernel, factor, share), (VMEM,) * 5,
        ((square32, HBM), (square32, HBM), (square32, HBM), (shape((1, width), F32), HBM)),
        scratch=[wide, wide, VMEM((1, width), F32)], copies=3, flops=work, moved=4 << 20,
    )(order, keep_sum, received_sum, base, mine)
    grad_self, grad_neigh = call(
        "other_half", functools.partial(other_kernel, factor), (VMEM, HBM, HBM),
        ((square32, HBM), (square32, HBM)),
        scratch=[wide], copies=4, flops=work // 2, moved=3 << 20, aliases={1: 0, 2: 1},
    )(other, self_part, neigh_part)
    return grad_features, grad_self, grad_neigh, bias_sum.reshape(width)


def solution(mesh):
    groups, members = mesh.shape["group"], mesh.shape["member"]
    nodes = ("across", "core", "wide", "near")
    fine = Mesh(mesh.devices.reshape(groups // 2, 2, 2, members // 2), nodes)
    rows = P(nodes, None)
    return jax.shard_map(
        local,
        mesh=fine,
        in_specs=(rows, rows, P(), P(), P(), rows, P(nodes), rows),
        out_specs=(rows, P(), P(), P()),
        check_vma=False,
    )
```

```python
import functools
import math

import jax
import jax.numpy as jnp
from jax import lax
from jax.experimental import pallas as pl
from jax.experimental.pallas import tpu as pltpu
from jax.sharding import Mesh
from jax.sharding import PartitionSpec as P

BF16 = jnp.bfloat16
F32 = jnp.float32
VMEM, HBM = pltpu.VMEM, pltpu.HBM
shape = jax.ShapeDtypeStruct


def product(left, right, left_dim, right_dim):
    return lax.dot_general(
        left, right, (((left_dim,), (right_dim,)), ((), ())), preferred_element_type=F32
    )


def call(name, body, ins, outs, scratch=(), copies=0, flops=0, moved=0, aliases=None):
    scratch = list(scratch)
    if copies:
        scratch.append(pltpu.SemaphoreType.DMA((copies,)))
    run = pl.pallas_call(
        body,
        out_shape=tuple(
            HBM(out.shape, out.dtype) if memory is HBM else out for out, memory in outs
        ),
        in_specs=[pl.BlockSpec(memory_space=memory) for memory in ins],
        out_specs=tuple(pl.BlockSpec(memory_space=memory) for _, memory in outs),
        scratch_shapes=scratch,
        input_output_aliases=aliases or {},
        compiler_params=pltpu.CompilerParams(vmem_limit_bytes=48 * 1024 * 1024),
        cost_estimate=pl.CostEstimate(flops=flops, bytes_accessed=moved, transcendentals=0),
        name=name,
    )

    def held(*operands):
        return run(*(
            pltpu.with_memory_space_constraint(operand, HBM) if memory is HBM else operand
            for operand, memory in zip(operands, ins, strict=True)
        ))

    return held


def core_of(near):
    return lax.axis_index("node") // (2 * near) % 2


def wide_of(near):
    return lax.axis_index("node") // near % 2


def start_all(sems, *pairs):
    copies = [pltpu.make_async_copy(a, b, sems.at[at]) for at, (a, b) in enumerate(pairs)]
    for copy in copies:
        copy.start()
    return copies


def serve_kernel(serve_hbm, features_hbm, out_ref, serve_ref, features_ref, sems):
    copies = start_all(sems, (serve_hbm, serve_ref), (features_hbm, features_ref))
    own_rows = features_ref.shape[0]
    slots = serve_ref.shape[1]
    copies[0].wait()
    wanted = jnp.broadcast_to(serve_ref[...], (128, slots)).astype(F32).T
    row = lax.broadcasted_iota(jnp.int32, (slots, 128), 1).astype(F32)
    picks = jnp.concatenate(
        [
            jnp.where(row + float(at) == wanted, 1.0, 0.0).astype(BF16)
            for at in range(0, own_rows, 128)
        ],
        axis=1,
    )
    copies[1].wait()
    rows = product(picks, features_ref[...], 1, 0)
    out_ref[...] = rows.reshape(out_ref.shape).astype(BF16)


def find_live(neighbours_ref, count_ref):
    fanout, own_rows = neighbours_ref.shape
    position = lax.broadcasted_iota(jnp.int32, (fanout, own_rows), 0)
    return jnp.where(position < count_ref[...], neighbours_ref[...], -1)


def fill_counts(live, live_ref, table_ref, base):
    fanout, own_rows = live.shape
    for block in range(0, table_ref.shape[0], 256):
        table_rows = min(256, table_ref.shape[0] - block)
        step = min(64, table_rows)
        live_ref[...] = (live - (base + block)).astype(F32).astype(BF16)

        def fill(at, carry):
            start = pl.multiple_of(at * step, step)
            row = (lax.broadcasted_iota(jnp.int32, (step, own_rows), 0) + start).astype(F32).astype(BF16)
            total = jnp.zeros((step, own_rows), BF16)
            for k in range(fanout):
                named = jnp.broadcast_to(live_ref[k : k + 1, :], (step, own_rows))
                total = total + jnp.where(row == named, jnp.bfloat16(1), jnp.bfloat16(0))
            table_ref[pl.ds(pl.multiple_of(block + start, step), step), :] = total
            return carry

        lax.fori_loop(0, table_rows // step, fill, 0)


def own_kernel(
    neighbours_hbm, count_hbm, features_hbm, w_self_hbm, bias_hbm,
    own_sum_ref, fetch_counts_ref, slot_counts_ref, inverse_ref, pre_ref,
    neighbours_ref, count_ref, features_ref, w_self_ref, bias_ref, live_ref, table_ref, sems,
):
    copies = start_all(
        sems,
        (neighbours_hbm, neighbours_ref),
        (count_hbm, count_ref),
        (features_hbm, features_ref),
        (w_self_hbm, w_self_ref),
        (bias_hbm, bias_ref),
    )
    own_rows = features_ref.shape[0]
    for copy in copies[:2]:
        copy.wait()
    inverse_ref[...] = jnp.broadcast_to(1.0 / count_ref[...].astype(F32), (128, own_rows)).T
    live = find_live(neighbours_ref, count_ref)
    fill_counts(live, live_ref, slot_counts_ref, own_rows)
    fetch_counts_ref[...] = slot_counts_ref[...].T
    fill_counts(live, live_ref, table_ref, 0)
    for copy in copies[2:]:
        copy.wait()
    features = features_ref[...]
    own_sum_ref[...] = product(table_ref[...], features, 0, 0)
    pre_ref[...] = product(features, w_self_ref[...], 1, 0) + bias_ref[...]


def spread_wide(inverse, width):
    return jnp.concatenate([inverse] * (width // 128), axis=1)


def main_kernel(
    near, incoming_ref, own_sum_ref, fetch_counts_ref, slot_counts_ref, inverse_ref, pre_ref, w_neigh_ref,
    cotangent_hbm, features_hbm,
    send_ref, keep_ref, keep_rows_ref, bias_ref, pre_grad_ref, message_ref,
    cotangent_ref, left_ref, rows_ref, sems,
):
    own_rows, width = own_sum_ref.shape
    slots = rows_ref.shape[0]
    core = core_of(near)
    copies = start_all(sems, (cotangent_hbm, cotangent_ref), (features_hbm, left_ref.at[0]))
    incoming = incoming_ref[...].astype(F32).reshape(slots, width).astype(BF16)
    inverse = spread_wide(inverse_ref[...], width)
    summed = own_sum_ref[...] + product(fetch_counts_ref[...], incoming, 1, 0)
    aggregated = (summed * inverse).astype(BF16)
    left_ref[1] = aggregated
    pre = pre_ref[...] + product(aggregated, w_neigh_ref[...], 1, 0)
    sigmoid_pre = jax.nn.sigmoid(pre)
    slope = sigmoid_pre * (1.0 + pre * (1.0 - sigmoid_pre))
    slope_ref = keep_ref
    slope_ref[...] = slope
    copies[0].wait()
    pre_grad_ref[...] = (cotangent_ref[...].astype(F32) * slope_ref[...]).astype(BF16)
    pre_grad = pre_grad_ref[...]
    message = (product(pre_grad, w_neigh_ref[...], 1, 1) * inverse).astype(BF16)
    message_ref[...] = message
    rows_ref[...] = product(slot_counts_ref[...], message, 1, 0)
    copies[1].wait()
    keep_ref[...] = product(left_ref[core], pre_grad, 0, 0)
    send_ref[:own_rows, :] = product(left_ref[1 - core], pre_grad, 0, 0).astype(BF16)
    half = slots // 2
    blocks, length = keep_rows_ref.shape[0], keep_rows_ref.shape[1]
    for at in range(blocks):
        mine = pl.multiple_of((at * 2 + core) * length, length)
        other = pl.multiple_of((at * 2 + 1 - core) * length, length)
        keep_rows_ref[at] = rows_ref[pl.ds(mine, length), :].astype(BF16)
        send_ref[own_rows + at * length : own_rows + (at + 1) * length, :] = rows_ref[
            pl.ds(other, length), :
        ].astype(BF16)
    bias = jnp.sum(pre_grad.astype(F32), axis=0, keepdims=True).astype(BF16)
    bias_ref[...] = jnp.broadcast_to(bias, bias_ref.shape)
    send_ref[own_rows + half :, :] = jnp.broadcast_to(bias, bias_ref.shape)


def own_grad_kernel(
    dims, pre_grad_ref, message_ref, neighbours_hbm, count_hbm, serve_hbm, w_self_hbm, out_ref, order_ref,
    neighbours_ref, count_ref, serve_ref, w_self_ref, live_ref, table_ref, sems,
):
    copies = start_all(
        sems,
        (neighbours_hbm, neighbours_ref),
        (count_hbm, count_ref),
        (serve_hbm, serve_ref),
        (w_self_hbm, w_self_ref),
    )
    for copy in copies:
        copy.wait()
    fill_counts(find_live(neighbours_ref, count_ref), live_ref, table_ref, 0)
    out_ref[...] = product(pre_grad_ref[...], w_self_ref[...], 1, 1) + product(
        table_ref[...], message_ref[...], 1, 0
    )
    across, near, cap = dims
    slots = serve_ref.shape[1]
    to = lax.broadcasted_iota(jnp.int32, (slots, slots), 1)
    slot = to % cap
    core = (to // cap % 2 + core_of(near)) % 2
    n = to // (2 * cap) % near
    a = to // (2 * cap * near) % across
    wide = (to // (2 * cap * near * across) + wide_of(near)) % 2
    source = (((a * 2 + core) * 2 + wide) * near + n) * cap + slot
    at = lax.broadcasted_iota(jnp.int32, (slots, slots), 0)
    moves = (at == source).astype(F32).astype(BF16)
    serve = serve_ref[...]
    high = (serve // 32).astype(F32).astype(BF16)
    low = (serve % 32).astype(F32).astype(BF16)
    order_ref[...] = (
        product(high, moves, 1, 0) * 32.0 + product(low, moves, 1, 0)
    ).astype(jnp.int32)


def pack_kernel(dims, order, received_ref, keep_ref, keep_rows_ref, bias_ref, out_ref):
    across, near, cap = dims
    own_rows, width = keep_ref.shape
    peers, length = out_ref.shape[0], out_ref.shape[1]
    half = 2 * peers * cap
    share = own_rows // peers
    keep_rows = keep_rows_ref[...].astype(F32).reshape(half, width)
    other_rows = received_ref[own_rows : own_rows + half, :].astype(F32)
    bias = bias_ref[...].astype(F32) + received_ref[own_rows + half :, :].astype(F32)
    summed = keep_ref[...] + received_ref[:own_rows, :].astype(F32)
    for peer in range(peers):
        parts = [summed[peer * share : (peer + 1) * share]]
        for wide in range(2):
            place = order[peer]
            at = ((place // near * 2 + wide) * near + place % near) * cap
            parts += [keep_rows[at : at + cap], other_rows[at : at + cap]]
        parts.append(bias[: length - share - 4 * cap])
        out_ref[peer] = jnp.concatenate(parts, axis=0).astype(BF16)


def sum_kernel(dims, order, payload_ref, keep_ref, send_ref):
    cap = dims[2]
    peers, length, width = payload_ref.shape
    pair = 2 * cap
    count = peers * pair
    share = keep_ref.shape[0] - count - 8
    grads = jnp.zeros((share, width), F32)
    bias = jnp.zeros((8, width), F32)
    lower, upper = [None] * peers, [None] * peers
    for peer in range(peers):
        grads = grads + payload_ref[peer, :share, :].astype(F32)
        rest = payload_ref[peer, share:, :].astype(F32)
        lower[order[peer]] = rest[:pair]
        upper[order[peer]] = rest[pair : 2 * pair]
        bias = bias + jnp.broadcast_to(rest[2 * pair : 2 * pair + 1], bias.shape)
    grads = grads.astype(BF16)
    bias = bias.astype(BF16)
    first = wide_of(dims[1]) == 0
    lower, upper = jnp.concatenate(lower, axis=0), jnp.concatenate(upper, axis=0)
    for ref, rows in (
        (keep_ref, jnp.where(first, lower, upper)),
        (send_ref, jnp.where(first, upper, lower)),
    ):
        ref[:share, :] = grads
        ref[share : share + count, :] = rows.astype(BF16)
        ref[share + count :, :] = bias


def total_kernel(keep_ref, received_ref, after_ref, out_ref):
    peers, share, width = out_ref.shape
    total = (keep_ref[:share, :].astype(F32) + received_ref[:share, :].astype(F32)).astype(BF16)
    for peer in range(peers):
        out_ref[peer] = total


def send_half(matrix, source_ref, self_hbm, neigh_hbm, sem, rows, wait):
    source = source_ref.at[rows, :]
    for index, target in enumerate((self_hbm, neigh_hbm)):

        @pl.when(matrix == index)
        def _(target=target):
            copy = pltpu.make_async_copy(source, target.at[rows, :], sem)
            if wait:
                copy.wait()
            else:
                copy.start()


def tail_kernel(
    factor, share, near, order_ref, keep_ref, received_ref, base_ref, mine_ref,
    out_hbm, self_hbm, neigh_hbm, bias_hbm, wide_ref, out_ref, bias_ref, sems,
):
    own_rows, slots = base_ref.shape[0], order_ref.shape[1]
    half = slots // 2
    matrix = core_of(near)
    everything = pl.ds(0, own_rows)
    wide_ref[...] = mine_ref[...].astype(F32) * factor
    send_half(matrix, wide_ref, self_hbm, neigh_hbm, sems.at[0], everything, False)
    last = keep_ref.shape[0] - 8
    bias = keep_ref[last:, :].astype(F32) + received_ref[last:, :].astype(F32)
    bias_ref[...] = bias[:1] * factor
    copies = [pltpu.make_async_copy(bias_ref, bias_hbm, sems.at[1])]
    copies[0].start()
    rows = jnp.concatenate(
        [keep_ref[share : share + half, :], received_ref[share : share + half, :]], axis=0
    )
    row = lax.broadcasted_iota(jnp.int32, (own_rows, slots), 0)
    picks = (row == order_ref[...]).astype(F32).astype(BF16)
    out_ref[...] = base_ref[...] + product(picks, rows, 1, 0)
    copies.append(pltpu.make_async_copy(out_ref, out_hbm, sems.at[2]))
    copies[1].start()
    send_half(matrix, wide_ref, self_hbm, neigh_hbm, sems.at[0], everything, True)
    for copy in copies:
        copy.wait()


def other_kernel(factor, near, half_ref, self_in, neigh_in, self_hbm, neigh_hbm, wide_ref, sems):
    own_rows = half_ref.shape[0]
    pieces = 4
    length = own_rows // pieces
    matrix = 1 - core_of(near)
    spans = [pl.ds(at * length, length) for at in range(pieces)]
    for at, span in enumerate(spans):
        wide_ref[span, :] = half_ref[span, :].astype(F32) * factor
        send_half(matrix, wide_ref, self_hbm, neigh_hbm, sems.at[at], span, False)
    for at, span in enumerate(spans):
        send_half(matrix, wide_ref, self_hbm, neigh_hbm, sems.at[at], span, True)


def local(across, near, features, cotangent, w_self, w_neigh, bias, neighbours, neigh_count, serve_rows):
    own_rows, width = features.shape
    fanout = neighbours.shape[1]
    peers = across * near
    devices = 4 * peers
    slots = serve_rows.shape[1]
    cap = slots // devices
    half = slots // 2
    share = own_rows // peers
    length = -(-(share + 4 * cap + 1) // 8) * 8
    dims = (across, near, cap)
    chips = [place ^ (place >> 1) for place in reversed(range(peers))]
    cubes = [
        [(place // near * 4 + plane) * near + place % near for place in chips]
        for plane in range(4)
    ]
    swap_core = [(at, at ^ (2 * near)) for at in range(devices)]
    swap_wide = [(at, at ^ near) for at in range(devices)]
    factor = 1.0 / math.sqrt(own_rows * devices)
    work = 2 * own_rows * own_rows * width
    square16 = shape((own_rows, width), BF16)
    square32 = shape((own_rows, width), F32)

    (outgoing,) = call(
        "serve", serve_kernel, (HBM, HBM), ((shape((devices, cap, width), BF16), VMEM),),
        scratch=[VMEM((1, slots), jnp.int32), VMEM((own_rows, width), BF16)],
        copies=2, flops=work // 4, moved=1 << 20,
    )(serve_rows, features)
    incoming = lax.all_to_all(outgoing, "node", 0, 0, tiled=True)
    neighbours = neighbours.T
    neigh_count = neigh_count.reshape(1, own_rows)
    held = [VMEM((fanout, own_rows), jnp.int32), VMEM((1, own_rows), jnp.int32)]
    counted = [VMEM((fanout, own_rows), BF16), VMEM((own_rows, own_rows), BF16)]
    own_sum, fetch_counts, slot_counts, inverse, pre = call(
        "own_aggregate", own_kernel, (HBM,) * 5,
        (
            (square32, VMEM),
            (shape((own_rows, slots), BF16), VMEM),
            (shape((slots, own_rows), BF16), VMEM),
            (shape((own_rows, 128), F32), VMEM),
            (square32, VMEM),
        ),
        scratch=[
            *held,
            VMEM((own_rows, width), BF16),
            VMEM((width, width), BF16),
            VMEM((1, width), F32),
            *counted,
        ],
        copies=5, flops=20 * work, moved=4 << 20,
    )(neighbours, neigh_count, features, w_self, bias.reshape(1, width))
    send, keep, keep_rows, own_bias, pre_grad, message = call(
        "layer_grad", functools.partial(main_kernel, near), (VMEM,) * 7 + (HBM,) * 2,
        (
            (shape((own_rows + half + 8, width), BF16), VMEM),
            (square32, VMEM),
            (shape((across, 2 * near * cap, width), BF16), VMEM),
            (shape((8, width), BF16), VMEM),
            (square16, VMEM),
            (square16, VMEM),
        ),
        scratch=[
            VMEM((own_rows, width), BF16),
            VMEM((2, own_rows, width), BF16),
            VMEM((slots, width), F32),
        ],
        copies=2, flops=5 * work, moved=8 << 20,
    )(incoming, own_sum, fetch_counts, slot_counts, inverse, pre, w_neigh, cotangent, features)
    received = lax.ppermute(send, "node", swap_core)
    base, order = call(
        "own_grad", functools.partial(own_grad_kernel, dims), (VMEM,) * 2 + (HBM,) * 4,
        ((square32, VMEM), (shape((1, slots), jnp.int32), VMEM)),
        scratch=[*held, VMEM((1, slots), jnp.int32), VMEM((width, width), BF16), *counted],
        copies=4, flops=2 * work, moved=4 << 20,
    )(pre_grad, message, neighbours, neigh_count, serve_rows, w_self)
    (payload,) = call(
        "pack", functools.partial(pack_kernel, dims, chips), (VMEM,) * 4,
        ((shape((peers, length, width), BF16), VMEM),), flops=work // 4, moved=4 << 20,
    )(received, keep, keep_rows, own_bias)
    arrived = lax.all_to_all(payload, "node", 0, 0, axis_index_groups=cubes, tiled=True)
    pairs = shape((share + half + 8, width), BF16)
    keep_sum, send_sum = call(
        "sum_shares", functools.partial(sum_kernel, dims, chips), (VMEM,),
        ((pairs, VMEM), (pairs, VMEM)), flops=work // 8, moved=1 << 20,
    )(arrived)
    received_sum = lax.ppermute(send_sum, "node", swap_wide)
    (total,) = call(
        "total", total_kernel, (VMEM, VMEM, VMEM), ((shape((peers, share, width), BF16), VMEM),),
        flops=work // 8, moved=1 << 20,
    )(keep_sum, received_sum, base)
    mine = lax.all_to_all(total, "node", 0, 0, axis_index_groups=cubes, tiled=True).reshape(own_rows, width)
    other = lax.ppermute(mine, "node", swap_core)
    wide = VMEM((own_rows, width), F32)
    grad_features, self_part, neigh_part, bias_sum = call(
        "tail", functools.partial(tail_kernel, factor, share, near), (VMEM,) * 5,
        ((square32, HBM), (square32, HBM), (square32, HBM), (shape((1, width), F32), HBM)),
        scratch=[wide, wide, VMEM((1, width), F32)], copies=3, flops=work, moved=4 << 20,
    )(order, keep_sum, received_sum, base, mine)
    grad_self, grad_neigh = call(
        "other_half", functools.partial(other_kernel, factor, near), (VMEM, HBM, HBM),
        ((square32, HBM), (square32, HBM)),
        scratch=[wide], copies=4, flops=work // 2, moved=3 << 20, aliases={1: 0, 2: 1},
    )(other, self_part, neigh_part)
    return grad_features, grad_self, grad_neigh, bias_sum.reshape(width)


def solution(mesh):
    across, near = mesh.shape["group"] // 2, mesh.shape["member"] // 2
    line = Mesh(mesh.devices.reshape(-1), ("node",))
    rows = P("node", None)
    return jax.shard_map(
        functools.partial(local, across, near),
        mesh=line,
        in_specs=(rows, rows, P(), P(), P(), rows, P("node"), rows),
        out_specs=(rows, P(), P(), P()),
        check_vma=False,
    )
```

```python
import functools
import math

import jax
import jax.numpy as jnp
from jax import lax
from jax.experimental import pallas as pl
from jax.experimental.pallas import tpu as pltpu
from jax.sharding import Mesh
from jax.sharding import PartitionSpec as P

BF16 = jnp.bfloat16
F32 = jnp.float32
VMEM, HBM = pltpu.VMEM, pltpu.HBM
shape = jax.ShapeDtypeStruct


def product(left, right, left_dim, right_dim):
    return lax.dot_general(
        left, right, (((left_dim,), (right_dim,)), ((), ())), preferred_element_type=F32
    )


def call(name, body, ins, outs, scratch=(), copies=0, flops=0, moved=0, aliases=None):
    scratch = list(scratch)
    if copies:
        scratch.append(pltpu.SemaphoreType.DMA((copies,)))
    run = pl.pallas_call(
        body,
        out_shape=tuple(
            HBM(out.shape, out.dtype) if memory is HBM else out for out, memory in outs
        ),
        in_specs=[pl.BlockSpec(memory_space=memory) for memory in ins],
        out_specs=tuple(pl.BlockSpec(memory_space=memory) for _, memory in outs),
        scratch_shapes=scratch,
        input_output_aliases=aliases or {},
        compiler_params=pltpu.CompilerParams(vmem_limit_bytes=48 * 1024 * 1024),
        cost_estimate=pl.CostEstimate(flops=flops, bytes_accessed=moved, transcendentals=0),
        name=name,
    )

    def held(*operands):
        return run(*(
            pltpu.with_memory_space_constraint(operand, HBM) if memory is HBM else operand
            for operand, memory in zip(operands, ins, strict=True)
        ))

    return held


def core_of(near):
    return lax.axis_index("node") // (2 * near) % 2


def wide_of(near):
    return lax.axis_index("node") // near % 2


def start_all(sems, *pairs):
    copies = [pltpu.make_async_copy(a, b, sems.at[at]) for at, (a, b) in enumerate(pairs)]
    for copy in copies:
        copy.start()
    return copies


def serve_kernel(serve_hbm, features_hbm, out_ref, serve_ref, features_ref, sems):
    copies = start_all(sems, (serve_hbm, serve_ref), (features_hbm, features_ref))
    own_rows = features_ref.shape[0]
    slots = serve_ref.shape[1]
    copies[0].wait()
    wanted = jnp.broadcast_to(serve_ref[...], (128, slots)).astype(F32).T
    row = lax.broadcasted_iota(jnp.int32, (slots, 128), 1).astype(F32)
    picks = jnp.concatenate(
        [
            jnp.where(row + float(at) == wanted, 1.0, 0.0).astype(BF16)
            for at in range(0, own_rows, 128)
        ],
        axis=1,
    )
    copies[1].wait()
    rows = product(picks, features_ref[...], 1, 0)
    out_ref[...] = rows.reshape(out_ref.shape).astype(BF16)


def find_live(neighbours_ref, count_ref):
    fanout, own_rows = neighbours_ref.shape
    position = lax.broadcasted_iota(jnp.int32, (fanout, own_rows), 0)
    return jnp.where(position < count_ref[...], neighbours_ref[...], -1)


def fill_counts(live, live_ref, table_ref, base):
    fanout, own_rows = live.shape
    for block in range(0, table_ref.shape[0], 256):
        table_rows = min(256, table_ref.shape[0] - block)
        step = min(64, table_rows)
        live_ref[...] = (live - (base + block)).astype(F32).astype(BF16)

        def fill(at, carry):
            start = pl.multiple_of(at * step, step)
            row = (lax.broadcasted_iota(jnp.int32, (step, own_rows), 0) + start).astype(F32).astype(BF16)
            total = jnp.zeros((step, own_rows), BF16)
            for k in range(fanout):
                named = jnp.broadcast_to(live_ref[k : k + 1, :], (step, own_rows))
                total = total + jnp.where(row == named, jnp.bfloat16(1), jnp.bfloat16(0))
            table_ref[pl.ds(pl.multiple_of(block + start, step), step), :] = total
            return carry

        lax.fori_loop(0, table_rows // step, fill, 0)


def own_kernel(
    neighbours_hbm, count_hbm, features_hbm, w_self_hbm, bias_hbm,
    own_sum_ref, fetch_counts_ref, slot_counts_ref, inverse_ref, pre_ref,
    neighbours_ref, count_ref, features_ref, w_self_ref, bias_ref, live_ref, table_ref, sems,
):
    copies = start_all(
        sems,
        (neighbours_hbm, neighbours_ref),
        (count_hbm, count_ref),
        (features_hbm, features_ref),
        (w_self_hbm, w_self_ref),
        (bias_hbm, bias_ref),
    )
    own_rows = features_ref.shape[0]
    for copy in copies[:2]:
        copy.wait()
    inverse_ref[...] = jnp.broadcast_to(1.0 / count_ref[...].astype(F32), (128, own_rows)).T
    live = find_live(neighbours_ref, count_ref)
    fill_counts(live, live_ref, slot_counts_ref, own_rows)
    fetch_counts_ref[...] = slot_counts_ref[...].T
    fill_counts(live, live_ref, table_ref, 0)
    for copy in copies[2:]:
        copy.wait()
    features = features_ref[...]
    own_sum_ref[...] = product(table_ref[...], features, 0, 0)
    pre_ref[...] = product(features, w_self_ref[...], 1, 0) + bias_ref[...]


def spread_wide(inverse, width):
    return jnp.concatenate([inverse] * (width // 128), axis=1)


def main_kernel(
    near, incoming_ref, own_sum_ref, fetch_counts_ref, inverse_ref, pre_ref, w_neigh_ref,
    cotangent_hbm, features_hbm,
    send_ref, left_ref, pre_grad_ref,
    cotangent_ref, slope_ref, sems,
):
    own_rows, width = own_sum_ref.shape
    slots = fetch_counts_ref.shape[1]
    core = core_of(near)
    copies = start_all(sems, (cotangent_hbm, cotangent_ref), (features_hbm, left_ref.at[0]))
    incoming = incoming_ref[...].astype(F32).reshape(slots, width).astype(BF16)
    inverse = spread_wide(inverse_ref[...], width)
    summed = own_sum_ref[...] + product(fetch_counts_ref[...], incoming, 1, 0)
    aggregated = (summed * inverse).astype(BF16)
    left_ref[1] = aggregated
    pre = pre_ref[...] + product(aggregated, w_neigh_ref[...], 1, 0)
    sigmoid_pre = jax.nn.sigmoid(pre)
    slope = sigmoid_pre * (1.0 + pre * (1.0 - sigmoid_pre))
    slope_ref[...] = slope
    copies[0].wait()
    pre_grad_ref[...] = (cotangent_ref[...].astype(F32) * slope_ref[...]).astype(BF16)
    pre_grad = pre_grad_ref[...]
    copies[1].wait()
    send_ref[...] = product(left_ref[1 - core], pre_grad, 0, 0).astype(BF16)


def keep_kernel(near, left_ref, pre_grad_ref, keep_ref):
    keep_ref[...] = product(left_ref[core_of(near)], pre_grad_ref[...], 0, 0)


def message_kernel(
    dims, pre_grad_ref, w_neigh_ref, inverse_ref, slot_counts_ref, message_ref, send_ref, keep_ref, rows_ref
):
    own_rows, width = pre_grad_ref.shape
    slots = rows_ref.shape[0]
    _, near, cap = dims
    core = core_of(near)
    pre_grad = pre_grad_ref[...]
    inverse = spread_wide(inverse_ref[...], width)
    message = (product(pre_grad, w_neigh_ref[...], 1, 1) * inverse).astype(BF16)
    message_ref[...] = message
    rows_ref[...] = product(slot_counts_ref[...], message, 1, 0)
    half = slots // 2
    length = 2 * near * cap
    bias = jnp.sum(pre_grad.astype(F32), axis=0, keepdims=True).astype(BF16)
    for index, ref in ((core, keep_ref), (1 - core, send_ref)):
        for at in range(half // length):
            start = pl.multiple_of((at * 2 + index) * length, length)
            ref[at * length : (at + 1) * length, :] = rows_ref[pl.ds(start, length), :].astype(BF16)
        ref[half:, :] = jnp.broadcast_to(bias, (8, width))


def own_grad_kernel(
    dims, pre_grad_ref, message_ref, neighbours_hbm, count_hbm, serve_hbm, w_self_hbm, out_ref, order_ref,
    neighbours_ref, count_ref, serve_ref, w_self_ref, live_ref, table_ref, sems,
):
    copies = start_all(
        sems,
        (neighbours_hbm, neighbours_ref),
        (count_hbm, count_ref),
        (serve_hbm, serve_ref),
        (w_self_hbm, w_self_ref),
    )
    for copy in copies:
        copy.wait()
    fill_counts(find_live(neighbours_ref, count_ref), live_ref, table_ref, 0)
    out_ref[...] = product(pre_grad_ref[...], w_self_ref[...], 1, 1) + product(
        table_ref[...], message_ref[...], 1, 0
    )
    across, near, cap = dims
    slots = serve_ref.shape[1]
    to = lax.broadcasted_iota(jnp.int32, (slots, slots), 1)
    slot = to % cap
    core = (to // cap % 2 + core_of(near)) % 2
    n = to // (2 * cap) % near
    a = to // (2 * cap * near) % across
    wide = (to // (2 * cap * near * across) + wide_of(near)) % 2
    source = (((a * 2 + core) * 2 + wide) * near + n) * cap + slot
    at = lax.broadcasted_iota(jnp.int32, (slots, slots), 0)
    moves = (at == source).astype(F32).astype(BF16)
    serve = serve_ref[...]
    high = (serve // 32).astype(F32).astype(BF16)
    low = (serve % 32).astype(F32).astype(BF16)
    order_ref[...] = (
        product(high, moves, 1, 0) * 32.0 + product(low, moves, 1, 0)
    ).astype(jnp.int32)


def pack_kernel(dims, order, received_ref, keep_ref, received_rows_ref, keep_rows_ref, out_ref):
    across, near, cap = dims
    own_rows, width = keep_ref.shape
    peers, length = out_ref.shape[0], out_ref.shape[1]
    half = 2 * peers * cap
    share = own_rows // peers
    keep_rows = keep_rows_ref[...].astype(F32)
    other_rows = received_rows_ref[...].astype(F32)
    bias = keep_rows[half:] + other_rows[half:]
    summed = keep_ref[...] + received_ref[...].astype(F32)
    for peer in range(peers):
        parts = [summed[peer * share : (peer + 1) * share]]
        for wide in range(2):
            place = order[peer]
            at = ((place // near * 2 + wide) * near + place % near) * cap
            parts += [keep_rows[at : at + cap], other_rows[at : at + cap]]
        parts.append(bias[: length - share - 4 * cap])
        out_ref[peer] = jnp.concatenate(parts, axis=0).astype(BF16)


def sum_kernel(dims, order, payload_ref, keep_ref, send_ref):
    cap = dims[2]
    peers, length, width = payload_ref.shape
    pair = 2 * cap
    count = peers * pair
    share = keep_ref.shape[0] - count - 8
    grads = jnp.zeros((share, width), F32)
    bias = jnp.zeros((8, width), F32)
    lower, upper = [None] * peers, [None] * peers
    for peer in range(peers):
        grads = grads + payload_ref[peer, :share, :].astype(F32)
        rest = payload_ref[peer, share:, :].astype(F32)
        lower[order[peer]] = rest[:pair]
        upper[order[peer]] = rest[pair : 2 * pair]
        bias = bias + jnp.broadcast_to(rest[2 * pair : 2 * pair + 1], bias.shape)
    grads = grads.astype(BF16)
    bias = bias.astype(BF16)
    first = wide_of(dims[1]) == 0
    lower, upper = jnp.concatenate(lower, axis=0), jnp.concatenate(upper, axis=0)
    for ref, rows in (
        (keep_ref, jnp.where(first, lower, upper)),
        (send_ref, jnp.where(first, upper, lower)),
    ):
        ref[:share, :] = grads
        ref[share : share + count, :] = rows.astype(BF16)
        ref[share + count :, :] = bias


def total_kernel(keep_ref, received_ref, after_ref, out_ref):
    peers, share, width = out_ref.shape
    total = (keep_ref[:share, :].astype(F32) + received_ref[:share, :].astype(F32)).astype(BF16)
    for peer in range(peers):
        out_ref[peer] = total


def send_half(matrix, source_ref, self_hbm, neigh_hbm, sem, rows, wait):
    source = source_ref.at[rows, :]
    for index, target in enumerate((self_hbm, neigh_hbm)):

        @pl.when(matrix == index)
        def _(target=target):
            copy = pltpu.make_async_copy(source, target.at[rows, :], sem)
            if wait:
                copy.wait()
            else:
                copy.start()


def tail_kernel(
    factor, share, near, order_ref, keep_ref, received_ref, base_ref, mine_ref,
    out_hbm, self_hbm, neigh_hbm, bias_hbm, wide_ref, out_ref, bias_ref, sems,
):
    own_rows, slots = base_ref.shape[0], order_ref.shape[1]
    half = slots // 2
    matrix = core_of(near)
    everything = pl.ds(0, own_rows)
    wide_ref[...] = mine_ref[...].astype(F32) * factor
    send_half(matrix, wide_ref, self_hbm, neigh_hbm, sems.at[0], everything, False)
    last = keep_ref.shape[0] - 8
    bias = keep_ref[last:, :].astype(F32) + received_ref[last:, :].astype(F32)
    bias_ref[...] = bias[:1] * factor
    copies = [pltpu.make_async_copy(bias_ref, bias_hbm, sems.at[1])]
    copies[0].start()
    rows = jnp.concatenate(
        [keep_ref[share : share + half, :], received_ref[share : share + half, :]], axis=0
    )
    row = lax.broadcasted_iota(jnp.int32, (own_rows, slots), 0)
    picks = (row == order_ref[...]).astype(F32).astype(BF16)
    out_ref[...] = base_ref[...] + product(picks, rows, 1, 0)
    copies.append(pltpu.make_async_copy(out_ref, out_hbm, sems.at[2]))
    copies[1].start()
    send_half(matrix, wide_ref, self_hbm, neigh_hbm, sems.at[0], everything, True)
    for copy in copies:
        copy.wait()


def other_kernel(factor, near, half_ref, self_in, neigh_in, self_hbm, neigh_hbm, wide_ref, sems):
    own_rows = half_ref.shape[0]
    pieces = 4
    length = own_rows // pieces
    matrix = 1 - core_of(near)
    spans = [pl.ds(at * length, length) for at in range(pieces)]
    for at, span in enumerate(spans):
        wide_ref[span, :] = half_ref[span, :].astype(F32) * factor
        send_half(matrix, wide_ref, self_hbm, neigh_hbm, sems.at[at], span, False)
    for at, span in enumerate(spans):
        send_half(matrix, wide_ref, self_hbm, neigh_hbm, sems.at[at], span, True)


def local(across, near, features, cotangent, w_self, w_neigh, bias, neighbours, neigh_count, serve_rows):
    own_rows, width = features.shape
    fanout = neighbours.shape[1]
    peers = across * near
    devices = 4 * peers
    slots = serve_rows.shape[1]
    cap = slots // devices
    half = slots // 2
    share = own_rows // peers
    length = -(-(share + 4 * cap + 1) // 8) * 8
    dims = (across, near, cap)
    chips = list(reversed(range(peers)))
    cubes = [
        [(place // near * 4 + plane) * near + place % near for place in chips]
        for plane in range(4)
    ]
    swap_core = [(at, at ^ (2 * near)) for at in range(devices)]
    swap_wide = [(at, at ^ near) for at in range(devices)]
    factor = 1.0 / math.sqrt(own_rows * devices)
    work = 2 * own_rows * own_rows * width
    square16 = shape((own_rows, width), BF16)
    square32 = shape((own_rows, width), F32)

    (outgoing,) = call(
        "serve", serve_kernel, (HBM, HBM), ((shape((devices, cap, width), BF16), VMEM),),
        scratch=[VMEM((1, slots), jnp.int32), VMEM((own_rows, width), BF16)],
        copies=2, flops=work // 4, moved=1 << 20,
    )(serve_rows, features)
    incoming = lax.all_to_all(outgoing, "node", 0, 0, tiled=True)
    neighbours = neighbours.T
    neigh_count = neigh_count.reshape(1, own_rows)
    held = [VMEM((fanout, own_rows), jnp.int32), VMEM((1, own_rows), jnp.int32)]
    counted = [VMEM((fanout, own_rows), BF16), VMEM((own_rows, own_rows), BF16)]
    own_sum, fetch_counts, slot_counts, inverse, pre = call(
        "own_aggregate", own_kernel, (HBM,) * 5,
        (
            (square32, VMEM),
            (shape((own_rows, slots), BF16), VMEM),
            (shape((slots, own_rows), BF16), VMEM),
            (shape((own_rows, 128), F32), VMEM),
            (square32, VMEM),
        ),
        scratch=[
            *held,
            VMEM((own_rows, width), BF16),
            VMEM((width, width), BF16),
            VMEM((1, width), F32),
            *counted,
        ],
        copies=5, flops=20 * work, moved=4 << 20,
    )(neighbours, neigh_count, features, w_self, bias.reshape(1, width))
    send, left, pre_grad = call(
        "layer_grad", functools.partial(main_kernel, near), (VMEM,) * 6 + (HBM,) * 2,
        ((square16, VMEM), (shape((2, own_rows, width), BF16), VMEM), (square16, VMEM)),
        scratch=[VMEM((own_rows, width), BF16), VMEM((own_rows, width), F32)],
        copies=2, flops=5 * work, moved=8 << 20,
    )(incoming, own_sum, fetch_counts, inverse, pre, w_neigh, cotangent, features)
    received = lax.ppermute(send, "node", swap_core)
    returns = shape((half + 8, width), BF16)
    message, send_rows, keep_rows = call(
        "messages", functools.partial(message_kernel, dims), (VMEM,) * 4,
        ((square16, VMEM), (returns, VMEM), (returns, VMEM)),
        scratch=[VMEM((slots, width), F32)], flops=2 * work, moved=4 << 20,
    )(pre_grad, w_neigh, inverse, slot_counts)
    received_rows = lax.ppermute(send_rows, "node", swap_core)
    (keep,) = call(
        "keep_grad", functools.partial(keep_kernel, near), (VMEM, VMEM), ((square32, VMEM),),
        flops=work, moved=2 << 20,
    )(left, pre_grad)
    base, order = call(
        "own_grad", functools.partial(own_grad_kernel, dims), (VMEM,) * 2 + (HBM,) * 4,
        ((square32, VMEM), (shape((1, slots), jnp.int32), VMEM)),
        scratch=[*held, VMEM((1, slots), jnp.int32), VMEM((width, width), BF16), *counted],
        copies=4, flops=2 * work, moved=4 << 20,
    )(pre_grad, message, neighbours, neigh_count, serve_rows, w_self)
    (payload,) = call(
        "pack", functools.partial(pack_kernel, dims, chips), (VMEM,) * 4,
        ((shape((peers, length, width), BF16), VMEM),), flops=work // 4, moved=4 << 20,
    )(received, keep, received_rows, keep_rows)
    arrived = lax.all_to_all(payload, "node", 0, 0, axis_index_groups=cubes, tiled=True)
    pairs = shape((share + half + 8, width), BF16)
    keep_sum, send_sum = call(
        "sum_shares", functools.partial(sum_kernel, dims, chips), (VMEM,),
        ((pairs, VMEM), (pairs, VMEM)), flops=work // 8, moved=1 << 20,
    )(arrived)
    received_sum = lax.ppermute(send_sum, "node", swap_wide)
    (total,) = call(
        "total", total_kernel, (VMEM, VMEM, VMEM), ((shape((peers, share, width), BF16), VMEM),),
        flops=work // 8, moved=1 << 20,
    )(keep_sum, received_sum, base)
    mine = lax.all_to_all(total, "node", 0, 0, axis_index_groups=cubes, tiled=True).reshape(own_rows, width)
    other = lax.ppermute(mine, "node", swap_core)
    wide = VMEM((own_rows, width), F32)
    grad_features, self_part, neigh_part, bias_sum = call(
        "tail", functools.partial(tail_kernel, factor, share, near), (VMEM,) * 5,
        ((square32, HBM), (square32, HBM), (square32, HBM), (shape((1, width), F32), HBM)),
        scratch=[wide, wide, VMEM((1, width), F32)], copies=3, flops=work, moved=4 << 20,
    )(order, keep_sum, received_sum, base, mine)
    grad_self, grad_neigh = call(
        "other_half", functools.partial(other_kernel, factor, near), (VMEM, HBM, HBM),
        ((square32, HBM), (square32, HBM)),
        scratch=[wide], copies=4, flops=work // 2, moved=3 << 20, aliases={1: 0, 2: 1},
    )(other, self_part, neigh_part)
    return grad_features, grad_self, grad_neigh, bias_sum.reshape(width)


def solution(mesh):
    across, near = mesh.shape["group"] // 2, mesh.shape["member"] // 2
    line = Mesh(mesh.devices.reshape(-1), ("node",))
    rows = P("node", None)
    return jax.shard_map(
        functools.partial(local, across, near),
        mesh=line,
        in_specs=(rows, rows, P(), P(), P(), rows, P("node"), rows),
        out_specs=(rows, P(), P(), P()),
        check_vma=False,
    )
```

```python
import functools
import math

import jax
import jax.numpy as jnp
from jax import lax
from jax.experimental import pallas as pl
from jax.experimental.pallas import tpu as pltpu
from jax.sharding import Mesh
from jax.sharding import PartitionSpec as P

BF16 = jnp.bfloat16
F32 = jnp.float32
VMEM, HBM = pltpu.VMEM, pltpu.HBM
shape = jax.ShapeDtypeStruct


def product(left, right, left_dim, right_dim):
    return lax.dot_general(
        left, right, (((left_dim,), (right_dim,)), ((), ())), preferred_element_type=F32
    )


def call(name, body, ins, outs, scratch=(), copies=0, flops=0, moved=0, aliases=None):
    scratch = list(scratch)
    if copies:
        scratch.append(pltpu.SemaphoreType.DMA((copies,)))
    run = pl.pallas_call(
        body,
        out_shape=tuple(
            HBM(out.shape, out.dtype) if memory is HBM else out for out, memory in outs
        ),
        in_specs=[pl.BlockSpec(memory_space=memory) for memory in ins],
        out_specs=tuple(pl.BlockSpec(memory_space=memory) for _, memory in outs),
        scratch_shapes=scratch,
        input_output_aliases=aliases or {},
        compiler_params=pltpu.CompilerParams(vmem_limit_bytes=48 * 1024 * 1024),
        cost_estimate=pl.CostEstimate(flops=flops, bytes_accessed=moved, transcendentals=0),
        name=name,
    )

    def held(*operands):
        return run(*(
            pltpu.with_memory_space_constraint(operand, HBM) if memory is HBM else operand
            for operand, memory in zip(operands, ins, strict=True)
        ))

    return held


def core_of(near):
    return lax.axis_index("node") // (2 * near) % 2


def wide_of(near):
    return lax.axis_index("node") // near % 2


def start_all(sems, *pairs):
    copies = [pltpu.make_async_copy(a, b, sems.at[at]) for at, (a, b) in enumerate(pairs)]
    for copy in copies:
        copy.start()
    return copies


def serve_kernel(serve_hbm, features_hbm, out_ref, serve_ref, features_ref, sems):
    copies = start_all(sems, (serve_hbm, serve_ref), (features_hbm, features_ref))
    own_rows = features_ref.shape[0]
    slots = serve_ref.shape[1]
    copies[0].wait()
    wanted = jnp.broadcast_to(serve_ref[...], (128, slots)).astype(F32).T
    row = lax.broadcasted_iota(jnp.int32, (slots, 128), 1).astype(F32)
    picks = jnp.concatenate(
        [
            jnp.where(row + float(at) == wanted, 1.0, 0.0).astype(BF16)
            for at in range(0, own_rows, 128)
        ],
        axis=1,
    )
    copies[1].wait()
    rows = product(picks, features_ref[...], 1, 0)
    out_ref[...] = rows.reshape(out_ref.shape).astype(BF16)


def find_live(neighbours_ref, count_ref):
    fanout, own_rows = neighbours_ref.shape
    position = lax.broadcasted_iota(jnp.int32, (fanout, own_rows), 0)
    return jnp.where(position < count_ref[...], neighbours_ref[...], -1)


def fill_counts(live, live_ref, table_ref, base):
    fanout, own_rows = live.shape
    for block in range(0, table_ref.shape[0], 256):
        table_rows = min(256, table_ref.shape[0] - block)
        step = min(64, table_rows)
        live_ref[...] = (live - (base + block)).astype(F32).astype(BF16)

        def fill(at, carry):
            start = pl.multiple_of(at * step, step)
            row = (lax.broadcasted_iota(jnp.int32, (step, own_rows), 0) + start).astype(F32).astype(BF16)
            total = jnp.zeros((step, own_rows), BF16)
            for k in range(fanout):
                named = jnp.broadcast_to(live_ref[k : k + 1, :], (step, own_rows))
                total = total + jnp.where(row == named, jnp.bfloat16(1), jnp.bfloat16(0))
            table_ref[pl.ds(pl.multiple_of(block + start, step), step), :] = total
            return carry

        lax.fori_loop(0, table_rows // step, fill, 0)


def own_kernel(
    neighbours_hbm, count_hbm, features_hbm, w_self_hbm, bias_hbm,
    own_sum_ref, fetch_counts_ref, slot_counts_ref, inverse_ref, pre_ref,
    neighbours_ref, count_ref, features_ref, w_self_ref, bias_ref, live_ref, table_ref, sems,
):
    copies = start_all(
        sems,
        (neighbours_hbm, neighbours_ref),
        (count_hbm, count_ref),
        (features_hbm, features_ref),
        (w_self_hbm, w_self_ref),
        (bias_hbm, bias_ref),
    )
    own_rows = features_ref.shape[0]
    for copy in copies[:2]:
        copy.wait()
    inverse_ref[...] = jnp.broadcast_to(1.0 / count_ref[...].astype(F32), (128, own_rows)).T
    live = find_live(neighbours_ref, count_ref)
    fill_counts(live, live_ref, slot_counts_ref, own_rows)
    fetch_counts_ref[...] = slot_counts_ref[...].T
    fill_counts(live, live_ref, table_ref, 0)
    for copy in copies[2:]:
        copy.wait()
    features = features_ref[...]
    own_sum_ref[...] = product(table_ref[...], features, 0, 0)
    pre_ref[...] = product(features, w_self_ref[...], 1, 0) + bias_ref[...]


def split_in_two(bias):
    high = bias.astype(BF16).astype(F32)
    row = lax.broadcasted_iota(jnp.int32, (8, bias.shape[1]), 0)
    return jnp.where(row == 0, high, jnp.where(row == 1, bias - high, 0.0)).astype(BF16)


def join_two(rows):
    rows = rows.astype(F32)
    return rows[0:1] + rows[1:2]


def spread_wide(inverse, width):
    return jnp.concatenate([inverse] * (width // 128), axis=1)


def main_kernel(
    near, incoming_ref, own_sum_ref, fetch_counts_ref, inverse_ref, pre_ref, w_neigh_ref,
    cotangent_hbm, features_hbm,
    send_ref, left_ref, pre_grad_ref,
    cotangent_ref, slope_ref, sems,
):
    own_rows, width = own_sum_ref.shape
    slots = fetch_counts_ref.shape[1]
    core = core_of(near)
    parts = 2
    spans = [pl.ds(at * own_rows // parts, own_rows // parts) for at in range(parts)]
    copies = start_all(
        sems,
        *((cotangent_hbm.at[span, :], cotangent_ref.at[span, :]) for span in spans),
        (features_hbm, left_ref.at[0]),
    )
    incoming = incoming_ref[...].astype(F32).reshape(slots, width).astype(BF16)
    inverse = spread_wide(inverse_ref[...], width)
    summed = own_sum_ref[...] + product(fetch_counts_ref[...], incoming, 1, 0)
    aggregated = (summed * inverse).astype(BF16)
    left_ref[1] = aggregated
    pre = pre_ref[...] + product(aggregated, w_neigh_ref[...], 1, 0)
    sigmoid_pre = jax.nn.sigmoid(pre)
    slope = sigmoid_pre * (1.0 + pre * (1.0 - sigmoid_pre))
    slope_ref[...] = slope
    for span, copy in zip(spans, copies[:parts], strict=True):
        copy.wait()
        pre_grad_ref[span, :] = (
            cotangent_ref[span, :].astype(F32) * slope_ref[span, :]
        ).astype(BF16)
    pre_grad = pre_grad_ref[...]
    copies[parts].wait()
    send_ref[...] = product(left_ref[1 - core], pre_grad, 0, 0).astype(BF16)


def keep_kernel(near, left_ref, pre_grad_ref, keep_ref):
    keep_ref[...] = product(left_ref[core_of(near)], pre_grad_ref[...], 0, 0)


def message_kernel(
    dims, pre_grad_ref, w_neigh_ref, inverse_ref, slot_counts_ref, message_ref, send_ref, keep_ref, rows_ref
):
    own_rows, width = pre_grad_ref.shape
    slots = rows_ref.shape[0]
    _, near, cap = dims
    core = core_of(near)
    pre_grad = pre_grad_ref[...]
    inverse = spread_wide(inverse_ref[...], width)
    message = (product(pre_grad, w_neigh_ref[...], 1, 1) * inverse).astype(BF16)
    message_ref[...] = message
    rows_ref[...] = product(slot_counts_ref[...], message, 1, 0)
    half = slots // 2
    length = 2 * near * cap
    bias = split_in_two(jnp.sum(pre_grad.astype(F32), axis=0, keepdims=True))
    for index, ref in ((core, keep_ref), (1 - core, send_ref)):
        for at in range(half // length):
            start = pl.multiple_of((at * 2 + index) * length, length)
            ref[at * length : (at + 1) * length, :] = rows_ref[pl.ds(start, length), :].astype(BF16)
        ref[half:, :] = bias


def own_grad_kernel(
    dims, pre_grad_ref, message_ref, neighbours_hbm, count_hbm, serve_hbm, w_self_hbm, out_ref, order_ref,
    neighbours_ref, count_ref, serve_ref, w_self_ref, live_ref, table_ref, sems,
):
    copies = start_all(
        sems,
        (neighbours_hbm, neighbours_ref),
        (count_hbm, count_ref),
        (serve_hbm, serve_ref),
        (w_self_hbm, w_self_ref),
    )
    for copy in copies:
        copy.wait()
    fill_counts(find_live(neighbours_ref, count_ref), live_ref, table_ref, 0)
    out_ref[...] = product(pre_grad_ref[...], w_self_ref[...], 1, 1) + product(
        table_ref[...], message_ref[...], 1, 0
    )
    across, near, cap = dims
    slots = serve_ref.shape[1]
    to = lax.broadcasted_iota(jnp.int32, (slots, slots), 1)
    slot = to % cap
    core = (to // cap % 2 + core_of(near)) % 2
    n = to // (2 * cap) % near
    a = to // (2 * cap * near) % across
    wide = (to // (2 * cap * near * across) + wide_of(near)) % 2
    source = (((a * 2 + core) * 2 + wide) * near + n) * cap + slot
    at = lax.broadcasted_iota(jnp.int32, (slots, slots), 0)
    moves = (at == source).astype(F32).astype(BF16)
    serve = serve_ref[...]
    high = (serve // 32).astype(F32).astype(BF16)
    low = (serve % 32).astype(F32).astype(BF16)
    order_ref[...] = (
        product(high, moves, 1, 0) * 32.0 + product(low, moves, 1, 0)
    ).astype(jnp.int32)


def pack_kernel(dims, order, gather_order, received_ref, keep_ref, received_rows_ref, keep_rows_ref, out_ref):
    across, near, cap = dims
    own_rows, width = keep_ref.shape
    peers, length = out_ref.shape[0], out_ref.shape[1]
    half = 2 * peers * cap
    share = own_rows // peers
    keep_rows = keep_rows_ref[...].astype(F32)
    other_rows = received_rows_ref[...].astype(F32)
    bias = split_in_two(join_two(keep_rows[half:]) + join_two(other_rows[half:])).astype(F32)
    summed = keep_ref[...] + received_ref[...].astype(F32)
    for peer in range(peers):
        start = gather_order.index(order[peer]) * share
        parts = [summed[start : start + share]]
        for wide in range(2):
            place = order[peer]
            at = ((place // near * 2 + wide) * near + place % near) * cap
            parts += [keep_rows[at : at + cap], other_rows[at : at + cap]]
        parts.append(bias[: length - share - 4 * cap])
        out_ref[peer] = jnp.concatenate(parts, axis=0).astype(BF16)


def sum_kernel(dims, order, payload_ref, keep_ref, send_ref):
    cap = dims[2]
    peers, length, width = payload_ref.shape
    pair = 2 * cap
    count = peers * pair
    share = keep_ref.shape[0] - count - 8
    grads = jnp.zeros((share, width), F32)
    bias = jnp.zeros((1, width), F32)
    lower, upper = [None] * peers, [None] * peers
    for peer in range(peers):
        grads = grads + payload_ref[peer, :share, :].astype(F32)
        rest = payload_ref[peer, share:, :].astype(F32)
        lower[order[peer]] = rest[:pair]
        upper[order[peer]] = rest[pair : 2 * pair]
        bias = bias + join_two(rest[2 * pair :])
    grads = grads.astype(BF16)
    bias = split_in_two(bias)
    first = wide_of(dims[1]) == 0
    lower, upper = jnp.concatenate(lower, axis=0), jnp.concatenate(upper, axis=0)
    for ref, rows in (
        (keep_ref, jnp.where(first, lower, upper)),
        (send_ref, jnp.where(first, upper, lower)),
    ):
        ref[:share, :] = grads
        ref[share : share + count, :] = rows.astype(BF16)
        ref[share + count :, :] = bias


def total_kernel(keep_ref, received_ref, after_ref, out_ref):
    peers, share, width = out_ref.shape
    total = (keep_ref[:share, :].astype(F32) + received_ref[:share, :].astype(F32)).astype(BF16)
    for peer in range(peers):
        out_ref[peer] = total


def send_half(matrix, source_ref, self_hbm, neigh_hbm, sem, rows, wait):
    source = source_ref.at[rows, :]
    for index, target in enumerate((self_hbm, neigh_hbm)):

        @pl.when(matrix == index)
        def _(target=target):
            copy = pltpu.make_async_copy(source, target.at[rows, :], sem)
            if wait:
                copy.wait()
            else:
                copy.start()


def tail_kernel(
    factor, share, near, order_ref, keep_ref, received_ref, base_ref, mine_ref,
    out_hbm, self_hbm, neigh_hbm, bias_hbm, wide_ref, out_ref, bias_ref, sems,
):
    own_rows, slots = base_ref.shape[0], order_ref.shape[1]
    half = slots // 2
    matrix = core_of(near)
    everything = pl.ds(0, own_rows)
    wide_ref[...] = mine_ref[...].astype(F32) * factor
    send_half(matrix, wide_ref, self_hbm, neigh_hbm, sems.at[0], everything, False)
    last = keep_ref.shape[0] - 8
    bias_ref[...] = (join_two(keep_ref[last:, :]) + join_two(received_ref[last:, :])) * factor
    copies = [pltpu.make_async_copy(bias_ref, bias_hbm, sems.at[1])]
    copies[0].start()
    rows = jnp.concatenate(
        [keep_ref[share : share + half, :], received_ref[share : share + half, :]], axis=0
    )
    row = lax.broadcasted_iota(jnp.int32, (own_rows, slots), 0)
    picks = (row == order_ref[...]).astype(F32).astype(BF16)
    out_ref[...] = base_ref[...] + product(picks, rows, 1, 0)
    copies.append(pltpu.make_async_copy(out_ref, out_hbm, sems.at[2]))
    copies[1].start()
    send_half(matrix, wide_ref, self_hbm, neigh_hbm, sems.at[0], everything, True)
    for copy in copies:
        copy.wait()


def other_kernel(factor, near, half_ref, self_in, neigh_in, self_hbm, neigh_hbm, wide_ref, sems):
    own_rows = half_ref.shape[0]
    pieces = 4
    length = own_rows // pieces
    matrix = 1 - core_of(near)
    spans = [pl.ds(at * length, length) for at in range(pieces)]
    for at, span in enumerate(spans):
        wide_ref[span, :] = half_ref[span, :].astype(F32) * factor
        send_half(matrix, wide_ref, self_hbm, neigh_hbm, sems.at[at], span, False)
    for at, span in enumerate(spans):
        send_half(matrix, wide_ref, self_hbm, neigh_hbm, sems.at[at], span, True)


def local(across, near, features, cotangent, w_self, w_neigh, bias, neighbours, neigh_count, serve_rows):
    own_rows, width = features.shape
    fanout = neighbours.shape[1]
    peers = across * near
    devices = 4 * peers
    slots = serve_rows.shape[1]
    cap = slots // devices
    half = slots // 2
    share = own_rows // peers
    length = -(-(share + 4 * cap + 1) // 8) * 8
    dims = (across, near, cap)
    chips = [place ^ (place >> 1) for place in reversed(range(peers))]
    gather_chips = list(reversed(range(peers)))
    cubes, gather_cubes = (
        [[(place // near * 4 + plane) * near + place % near for place in listed] for plane in range(4)]
        for listed in (chips, gather_chips)
    )
    swap_core = [(at, at ^ (2 * near)) for at in range(devices)]
    swap_wide = [(at, at ^ near) for at in range(devices)]
    factor = 1.0 / math.sqrt(own_rows * devices)
    work = 2 * own_rows * own_rows * width
    square16 = shape((own_rows, width), BF16)
    square32 = shape((own_rows, width), F32)

    (outgoing,) = call(
        "serve", serve_kernel, (HBM, HBM), ((shape((devices, cap, width), BF16), VMEM),),
        scratch=[VMEM((1, slots), jnp.int32), VMEM((own_rows, width), BF16)],
        copies=2, flops=work // 4, moved=1 << 20,
    )(serve_rows, features)
    incoming = lax.all_to_all(outgoing, "node", 0, 0, tiled=True)
    neighbours = neighbours.T
    neigh_count = neigh_count.reshape(1, own_rows)
    held = [VMEM((fanout, own_rows), jnp.int32), VMEM((1, own_rows), jnp.int32)]
    counted = [VMEM((fanout, own_rows), BF16), VMEM((own_rows, own_rows), BF16)]
    own_sum, fetch_counts, slot_counts, inverse, pre = call(
        "own_aggregate", own_kernel, (HBM,) * 5,
        (
            (square32, VMEM),
            (shape((own_rows, slots), BF16), VMEM),
            (shape((slots, own_rows), BF16), VMEM),
            (shape((own_rows, 128), F32), VMEM),
            (square32, VMEM),
        ),
        scratch=[
            *held,
            VMEM((own_rows, width), BF16),
            VMEM((width, width), BF16),
            VMEM((1, width), F32),
            *counted,
        ],
        copies=5, flops=20 * work, moved=4 << 20,
    )(neighbours, neigh_count, features, w_self, bias.reshape(1, width))
    send, left, pre_grad = call(
        "layer_grad", functools.partial(main_kernel, near), (VMEM,) * 6 + (HBM,) * 2,
        ((square16, VMEM), (shape((2, own_rows, width), BF16), VMEM), (square16, VMEM)),
        scratch=[VMEM((own_rows, width), BF16), VMEM((own_rows, width), F32)],
        copies=3, flops=5 * work, moved=8 << 20,
    )(incoming, own_sum, fetch_counts, inverse, pre, w_neigh, cotangent, features)
    received = lax.ppermute(send, "node", swap_core)
    returns = shape((half + 8, width), BF16)
    message, send_rows, keep_rows = call(
        "messages", functools.partial(message_kernel, dims), (VMEM,) * 4,
        ((square16, VMEM), (returns, VMEM), (returns, VMEM)),
        scratch=[VMEM((slots, width), F32)], flops=2 * work, moved=4 << 20,
    )(pre_grad, w_neigh, inverse, slot_counts)
    received_rows = lax.ppermute(send_rows, "node", swap_core)
    (keep,) = call(
        "keep_grad", functools.partial(keep_kernel, near), (VMEM, VMEM), ((square32, VMEM),),
        flops=work, moved=2 << 20,
    )(left, pre_grad)
    base, order = call(
        "own_grad", functools.partial(own_grad_kernel, dims), (VMEM,) * 2 + (HBM,) * 4,
        ((square32, VMEM), (shape((1, slots), jnp.int32), VMEM)),
        scratch=[*held, VMEM((1, slots), jnp.int32), VMEM((width, width), BF16), *counted],
        copies=4, flops=2 * work, moved=4 << 20,
    )(pre_grad, message, neighbours, neigh_count, serve_rows, w_self)
    (payload,) = call(
        "pack", functools.partial(pack_kernel, dims, chips, gather_chips), (VMEM,) * 4,
        ((shape((peers, length, width), BF16), VMEM),), flops=work // 4, moved=4 << 20,
    )(received, keep, received_rows, keep_rows)
    arrived = lax.all_to_all(payload, "node", 0, 0, axis_index_groups=cubes, tiled=True)
    pairs = shape((share + half + 8, width), BF16)
    keep_sum, send_sum = call(
        "sum_shares", functools.partial(sum_kernel, dims, chips), (VMEM,),
        ((pairs, VMEM), (pairs, VMEM)), flops=work // 8, moved=1 << 20,
    )(arrived)
    received_sum = lax.ppermute(send_sum, "node", swap_wide)
    (total,) = call(
        "total", total_kernel, (VMEM, VMEM, VMEM), ((shape((peers, share, width), BF16), VMEM),),
        flops=work // 8, moved=1 << 20,
    )(keep_sum, received_sum, base)
    mine = lax.all_to_all(total, "node", 0, 0, axis_index_groups=gather_cubes, tiled=True).reshape(own_rows, width)
    other = lax.ppermute(mine, "node", swap_core)
    wide = VMEM((own_rows, width), F32)
    grad_features, self_part, neigh_part, bias_sum = call(
        "tail", functools.partial(tail_kernel, factor, share, near), (VMEM,) * 5,
        ((square32, HBM), (square32, HBM), (square32, HBM), (shape((1, width), F32), HBM)),
        scratch=[wide, wide, VMEM((1, width), F32)], copies=3, flops=work, moved=4 << 20,
    )(order, keep_sum, received_sum, base, mine)
    grad_self, grad_neigh = call(
        "other_half", functools.partial(other_kernel, factor, near), (VMEM, HBM, HBM),
        ((square32, HBM), (square32, HBM)),
        scratch=[wide], copies=4, flops=work // 2, moved=3 << 20, aliases={1: 0, 2: 1},
    )(other, self_part, neigh_part)
    return grad_features, grad_self, grad_neigh, bias_sum.reshape(width)


def solution(mesh):
    across, near = mesh.shape["group"] // 2, mesh.shape["member"] // 2
    line = Mesh(mesh.devices.reshape(-1), ("node",))
    rows = P("node", None)
    return jax.shard_map(
        functools.partial(local, across, near),
        mesh=line,
        in_specs=(rows, rows, P(), P(), P(), rows, P("node"), rows),
        out_specs=(rows, P(), P(), P()),
        check_vma=False,
    )
```

```python
import functools
import math

import jax
import jax.numpy as jnp
from jax import lax
from jax.experimental import pallas as pl
from jax.experimental.pallas import tpu as pltpu
from jax.sharding import Mesh
from jax.sharding import PartitionSpec as P

BF16 = jnp.bfloat16
F32 = jnp.float32
VMEM, HBM = pltpu.VMEM, pltpu.HBM
shape = jax.ShapeDtypeStruct


def product(left, right, left_dim, right_dim):
    return lax.dot_general(
        left, right, (((left_dim,), (right_dim,)), ((), ())), preferred_element_type=F32
    )


def call(name, body, ins, outs, scratch=(), copies=0, flops=0, moved=0, aliases=None):
    scratch = list(scratch)
    if copies:
        scratch.append(pltpu.SemaphoreType.DMA((copies,)))
    run = pl.pallas_call(
        body,
        out_shape=tuple(
            HBM(out.shape, out.dtype) if memory is HBM else out for out, memory in outs
        ),
        in_specs=[pl.BlockSpec(memory_space=memory) for memory in ins],
        out_specs=tuple(pl.BlockSpec(memory_space=memory) for _, memory in outs),
        scratch_shapes=scratch,
        input_output_aliases=aliases or {},
        compiler_params=pltpu.CompilerParams(vmem_limit_bytes=48 * 1024 * 1024),
        cost_estimate=pl.CostEstimate(flops=flops, bytes_accessed=moved, transcendentals=0),
        name=name,
    )

    def held(*operands):
        return run(*(
            pltpu.with_memory_space_constraint(operand, HBM) if memory is HBM else operand
            for operand, memory in zip(operands, ins, strict=True)
        ))

    return held


def core_of(near):
    return lax.axis_index("node") // (2 * near) % 2


def wide_of(near):
    return lax.axis_index("node") // near % 2


def start_all(sems, *pairs):
    copies = [pltpu.make_async_copy(a, b, sems.at[at]) for at, (a, b) in enumerate(pairs)]
    for copy in copies:
        copy.start()
    return copies


def serve_kernel(serve_hbm, features_hbm, out_ref, serve_ref, features_ref, sems):
    copies = start_all(sems, (serve_hbm, serve_ref), (features_hbm, features_ref))
    own_rows = features_ref.shape[0]
    slots = serve_ref.shape[1]
    copies[0].wait()
    wanted = jnp.broadcast_to(serve_ref[...], (128, slots)).astype(F32).T
    row = lax.broadcasted_iota(jnp.int32, (slots, 128), 1).astype(F32)
    picks = jnp.concatenate(
        [
            jnp.where(row + float(at) == wanted, 1.0, 0.0).astype(BF16)
            for at in range(0, own_rows, 128)
        ],
        axis=1,
    )
    copies[1].wait()
    rows = product(picks, features_ref[...], 1, 0)
    out_ref[...] = rows.reshape(out_ref.shape).astype(BF16)


def find_live(neighbours_ref, count_ref):
    fanout, own_rows = neighbours_ref.shape
    position = lax.broadcasted_iota(jnp.int32, (fanout, own_rows), 0)
    return jnp.where(position < count_ref[...], neighbours_ref[...], -1)


def fill_counts(live, live_ref, table_ref, base):
    fanout, own_rows = live.shape
    for block in range(0, table_ref.shape[0], 256):
        table_rows = min(256, table_ref.shape[0] - block)
        step = min(64, table_rows)
        live_ref[...] = (live - (base + block)).astype(F32).astype(BF16)

        def fill(at, carry):
            start = pl.multiple_of(at * step, step)
            row = (lax.broadcasted_iota(jnp.int32, (step, own_rows), 0) + start).astype(F32).astype(BF16)
            total = jnp.zeros((step, own_rows), BF16)
            for k in range(fanout):
                named = jnp.broadcast_to(live_ref[k : k + 1, :], (step, own_rows))
                total = total + jnp.where(row == named, jnp.bfloat16(1), jnp.bfloat16(0))
            table_ref[pl.ds(pl.multiple_of(block + start, step), step), :] = total
            return carry

        lax.fori_loop(0, table_rows // step, fill, 0)


def own_kernel(
    neighbours_hbm, count_hbm, features_hbm, w_self_hbm, bias_hbm,
    own_sum_ref, fetch_counts_ref, slot_counts_ref, inverse_ref, pre_ref,
    neighbours_ref, count_ref, features_ref, w_self_ref, bias_ref, live_ref, table_ref, sems,
):
    copies = start_all(
        sems,
        (neighbours_hbm, neighbours_ref),
        (count_hbm, count_ref),
        (features_hbm, features_ref),
        (w_self_hbm, w_self_ref),
        (bias_hbm, bias_ref),
    )
    own_rows = features_ref.shape[0]
    for copy in copies[:2]:
        copy.wait()
    inverse_ref[...] = jnp.broadcast_to(1.0 / count_ref[...].astype(F32), (128, own_rows)).T
    live = find_live(neighbours_ref, count_ref)
    fill_counts(live, live_ref, slot_counts_ref, own_rows)
    fetch_counts_ref[...] = slot_counts_ref[...].T
    fill_counts(live, live_ref, table_ref, 0)
    for copy in copies[2:]:
        copy.wait()
    features = features_ref[...]
    own_sum_ref[...] = product(table_ref[...], features, 0, 0)
    pre_ref[...] = product(features, w_self_ref[...], 1, 0) + bias_ref[...]


def split_in_two(bias):
    high = bias.astype(BF16).astype(F32)
    row = lax.broadcasted_iota(jnp.int32, (8, bias.shape[1]), 0)
    return jnp.where(row == 0, high, jnp.where(row == 1, bias - high, 0.0)).astype(BF16)


def join_two(rows):
    rows = rows.astype(F32)
    return rows[0:1] + rows[1:2]


def spread_wide(inverse, width):
    return jnp.concatenate([inverse] * (width // 128), axis=1)


def main_kernel(
    near, incoming_ref, own_sum_ref, fetch_counts_ref, inverse_ref, pre_ref, w_neigh_ref,
    cotangent_hbm, features_hbm,
    send_ref, left_ref, pre_grad_ref,
    cotangent_ref, slope_ref, sems,
):
    own_rows, width = own_sum_ref.shape
    slots = fetch_counts_ref.shape[1]
    core = core_of(near)
    parts = 2
    spans = [pl.ds(at * own_rows // parts, own_rows // parts) for at in range(parts)]
    copies = start_all(
        sems,
        *((cotangent_hbm.at[span, :], cotangent_ref.at[span, :]) for span in spans),
        (features_hbm, left_ref.at[0]),
    )
    incoming = incoming_ref[...].astype(F32).reshape(slots, width).astype(BF16)
    inverse = spread_wide(inverse_ref[...], width)
    summed = own_sum_ref[...] + product(fetch_counts_ref[...], incoming, 1, 0)
    aggregated = (summed * inverse).astype(BF16)
    left_ref[1] = aggregated
    pre = pre_ref[...] + product(aggregated, w_neigh_ref[...], 1, 0)
    sigmoid_pre = jax.nn.sigmoid(pre)
    slope = sigmoid_pre * (1.0 + pre * (1.0 - sigmoid_pre))
    slope_ref[...] = slope
    for span, copy in zip(spans, copies[:parts], strict=True):
        copy.wait()
        pre_grad_ref[span, :] = (
            cotangent_ref[span, :].astype(F32) * slope_ref[span, :]
        ).astype(BF16)
    pre_grad = pre_grad_ref[...]
    copies[parts].wait()
    send_ref[...] = product(left_ref[1 - core], pre_grad, 0, 0).astype(BF16)


def keep_kernel(near, left_ref, pre_grad_ref, keep_ref):
    keep_ref[...] = product(left_ref[core_of(near)], pre_grad_ref[...], 0, 0)


def message_kernel(
    dims, pre_grad_ref, w_neigh_ref, inverse_ref, slot_counts_ref, message_ref, send_ref, keep_ref, rows_ref
):
    own_rows, width = pre_grad_ref.shape
    slots = rows_ref.shape[0]
    _, near, cap = dims
    core = core_of(near)
    pre_grad = pre_grad_ref[...]
    inverse = spread_wide(inverse_ref[...], width)
    message = (product(pre_grad, w_neigh_ref[...], 1, 1) * inverse).astype(BF16)
    message_ref[...] = message
    rows_ref[...] = product(slot_counts_ref[...], message, 1, 0)
    half = slots // 2
    length = 2 * near * cap
    bias = split_in_two(jnp.sum(pre_grad.astype(F32), axis=0, keepdims=True))
    for index, ref in ((core, keep_ref), (1 - core, send_ref)):
        for at in range(half // length):
            start = pl.multiple_of((at * 2 + index) * length, length)
            ref[at * length : (at + 1) * length, :] = rows_ref[pl.ds(start, length), :].astype(BF16)
        ref[half:, :] = bias


def own_grad_kernel(
    dims, pre_grad_ref, message_ref, neighbours_hbm, count_hbm, serve_hbm, w_self_hbm, out_ref, order_ref,
    neighbours_ref, count_ref, serve_ref, w_self_ref, live_ref, table_ref, sems,
):
    copies = start_all(
        sems,
        (neighbours_hbm, neighbours_ref),
        (count_hbm, count_ref),
        (serve_hbm, serve_ref),
        (w_self_hbm, w_self_ref),
    )
    for copy in copies:
        copy.wait()
    fill_counts(find_live(neighbours_ref, count_ref), live_ref, table_ref, 0)
    out_ref[...] = product(pre_grad_ref[...], w_self_ref[...], 1, 1) + product(
        table_ref[...], message_ref[...], 1, 0
    )
    across, near, cap = dims
    slots = serve_ref.shape[1]
    to = lax.broadcasted_iota(jnp.int32, (slots, slots), 1)
    slot = to % cap
    core = (to // cap % 2 + core_of(near)) % 2
    n = to // (2 * cap) % near
    a = to // (2 * cap * near) % across
    wide = (to // (2 * cap * near * across) + wide_of(near)) % 2
    source = (((a * 2 + core) * 2 + wide) * near + n) * cap + slot
    at = lax.broadcasted_iota(jnp.int32, (slots, slots), 0)
    moves = (at == source).astype(F32).astype(BF16)
    serve = serve_ref[...]
    high = (serve // 32).astype(F32).astype(BF16)
    low = (serve % 32).astype(F32).astype(BF16)
    order_ref[...] = (
        product(high, moves, 1, 0) * 32.0 + product(low, moves, 1, 0)
    ).astype(jnp.int32)


def pack_kernel(dims, order, gather_order, received_ref, keep_ref, received_rows_ref, keep_rows_ref, out_ref):
    across, near, cap = dims
    own_rows, width = keep_ref.shape
    peers, length = out_ref.shape[0], out_ref.shape[1]
    half = 2 * peers * cap
    share = own_rows // peers
    keep_rows = keep_rows_ref[...].astype(F32)
    other_rows = received_rows_ref[...].astype(F32)
    bias = split_in_two(join_two(keep_rows[half:]) + join_two(other_rows[half:])).astype(F32)
    summed = keep_ref[...] + received_ref[...].astype(F32)
    for peer in range(peers):
        start = gather_order.index(order[peer]) * share
        parts = [summed[start : start + share]]
        for wide in range(2):
            place = order[peer]
            at = ((place // near * 2 + wide) * near + place % near) * cap
            parts += [keep_rows[at : at + cap], other_rows[at : at + cap]]
        parts.append(bias[: length - share - 4 * cap])
        out_ref[peer] = jnp.concatenate(parts, axis=0).astype(BF16)


def sum_kernel(dims, order, payload_ref, grads_ref, keep_ref, send_ref):
    cap = dims[2]
    peers, length, width = payload_ref.shape
    pair = 2 * cap
    count = peers * pair
    share = grads_ref.shape[0]
    grads = jnp.zeros((share, width), F32)
    bias = jnp.zeros((1, width), F32)
    lower, upper = [None] * peers, [None] * peers
    for peer in range(peers):
        grads = grads + payload_ref[peer, :share, :].astype(F32)
        rest = payload_ref[peer, share:, :].astype(F32)
        lower[order[peer]] = rest[:pair]
        upper[order[peer]] = rest[pair : 2 * pair]
        bias = bias + join_two(rest[2 * pair :])
    grads_ref[...] = grads.astype(BF16)
    bias = split_in_two(bias)
    first = wide_of(dims[1]) == 0
    lower, upper = jnp.concatenate(lower, axis=0), jnp.concatenate(upper, axis=0)
    for ref, rows in (
        (keep_ref, jnp.where(first, lower, upper)),
        (send_ref, jnp.where(first, upper, lower)),
    ):
        ref[:count, :] = rows.astype(BF16)
        ref[count:, :] = bias


def total_kernel(keep_ref, received_ref, after_ref, out_ref):
    peers, share, width = out_ref.shape
    total = (keep_ref[...].astype(F32) + received_ref[...].astype(F32)).astype(BF16)
    for peer in range(peers):
        out_ref[peer] = total


def pass_kernel(source_ref, after_ref, out_ref):
    out_ref[...] = source_ref[...]


def send_half(matrix, source_ref, self_hbm, neigh_hbm, sem, rows, wait):
    source = source_ref.at[rows, :]
    for index, target in enumerate((self_hbm, neigh_hbm)):

        @pl.when(matrix == index)
        def _(target=target):
            copy = pltpu.make_async_copy(source, target.at[rows, :], sem)
            if wait:
                copy.wait()
            else:
                copy.start()


def tail_kernel(
    factor, near, order_ref, keep_ref, received_ref, base_ref, mine_ref,
    out_hbm, self_hbm, neigh_hbm, bias_hbm, wide_ref, out_ref, bias_ref, sems,
):
    own_rows, slots = base_ref.shape[0], order_ref.shape[1]
    half = slots // 2
    matrix = core_of(near)
    everything = pl.ds(0, own_rows)
    wide_ref[...] = mine_ref[...].astype(F32) * factor
    send_half(matrix, wide_ref, self_hbm, neigh_hbm, sems.at[0], everything, False)
    bias_ref[...] = (join_two(keep_ref[half:, :]) + join_two(received_ref[half:, :])) * factor
    copies = [pltpu.make_async_copy(bias_ref, bias_hbm, sems.at[1])]
    copies[0].start()
    rows = jnp.concatenate([keep_ref[:half, :], received_ref[:half, :]], axis=0)
    row = lax.broadcasted_iota(jnp.int32, (own_rows, slots), 0)
    picks = (row == order_ref[...]).astype(F32).astype(BF16)
    out_ref[...] = base_ref[...] + product(picks, rows, 1, 0)
    copies.append(pltpu.make_async_copy(out_ref, out_hbm, sems.at[2]))
    copies[1].start()
    send_half(matrix, wide_ref, self_hbm, neigh_hbm, sems.at[0], everything, True)
    for copy in copies:
        copy.wait()


def other_kernel(factor, near, half_ref, self_in, neigh_in, self_hbm, neigh_hbm, wide_ref, sems):
    own_rows = half_ref.shape[0]
    pieces = 4
    length = own_rows // pieces
    matrix = 1 - core_of(near)
    spans = [pl.ds(at * length, length) for at in range(pieces)]
    for at, span in enumerate(spans):
        wide_ref[span, :] = half_ref[span, :].astype(F32) * factor
        send_half(matrix, wide_ref, self_hbm, neigh_hbm, sems.at[at], span, False)
    for at, span in enumerate(spans):
        send_half(matrix, wide_ref, self_hbm, neigh_hbm, sems.at[at], span, True)


def local(across, near, features, cotangent, w_self, w_neigh, bias, neighbours, neigh_count, serve_rows):
    own_rows, width = features.shape
    fanout = neighbours.shape[1]
    peers = across * near
    devices = 4 * peers
    slots = serve_rows.shape[1]
    cap = slots // devices
    half = slots // 2
    share = own_rows // peers
    length = -(-(share + 4 * cap + 1) // 8) * 8
    dims = (across, near, cap)
    chips = [place ^ (place >> 1) for place in reversed(range(peers))]
    gather_chips = list(reversed(range(peers)))
    cubes, gather_cubes = (
        [[(place // near * 4 + plane) * near + place % near for place in listed] for plane in range(4)]
        for listed in (chips, gather_chips)
    )
    swap_core = [(at, at ^ (2 * near)) for at in range(devices)]
    swap_wide = [(at, at ^ near) for at in range(devices)]
    factor = 1.0 / math.sqrt(own_rows * devices)
    work = 2 * own_rows * own_rows * width
    square16 = shape((own_rows, width), BF16)
    square32 = shape((own_rows, width), F32)

    (outgoing,) = call(
        "serve", serve_kernel, (HBM, HBM), ((shape((devices, cap, width), BF16), VMEM),),
        scratch=[VMEM((1, slots), jnp.int32), VMEM((own_rows, width), BF16)],
        copies=2, flops=work // 4, moved=1 << 20,
    )(serve_rows, features)
    incoming = lax.all_to_all(outgoing, "node", 0, 0, tiled=True)
    neighbours = neighbours.T
    neigh_count = neigh_count.reshape(1, own_rows)
    held = [VMEM((fanout, own_rows), jnp.int32), VMEM((1, own_rows), jnp.int32)]
    counted = [VMEM((fanout, own_rows), BF16), VMEM((own_rows, own_rows), BF16)]
    own_sum, fetch_counts, slot_counts, inverse, pre = call(
        "own_aggregate", own_kernel, (HBM,) * 5,
        (
            (square32, VMEM),
            (shape((own_rows, slots), BF16), VMEM),
            (shape((slots, own_rows), BF16), VMEM),
            (shape((own_rows, 128), F32), VMEM),
            (square32, VMEM),
        ),
        scratch=[
            *held,
            VMEM((own_rows, width), BF16),
            VMEM((width, width), BF16),
            VMEM((1, width), F32),
            *counted,
        ],
        copies=5, flops=20 * work, moved=4 << 20,
    )(neighbours, neigh_count, features, w_self, bias.reshape(1, width))
    send, left, pre_grad = call(
        "layer_grad", functools.partial(main_kernel, near), (VMEM,) * 6 + (HBM,) * 2,
        ((square16, VMEM), (shape((2, own_rows, width), BF16), VMEM), (square16, VMEM)),
        scratch=[VMEM((own_rows, width), BF16), VMEM((own_rows, width), F32)],
        copies=3, flops=5 * work, moved=8 << 20,
    )(incoming, own_sum, fetch_counts, inverse, pre, w_neigh, cotangent, features)
    received = lax.ppermute(send, "node", swap_core)
    returns = shape((half + 8, width), BF16)
    message, send_rows, keep_rows = call(
        "messages", functools.partial(message_kernel, dims), (VMEM,) * 4,
        ((square16, VMEM), (returns, VMEM), (returns, VMEM)),
        scratch=[VMEM((slots, width), F32)], flops=2 * work, moved=4 << 20,
    )(pre_grad, w_neigh, inverse, slot_counts)
    received_rows = lax.ppermute(send_rows, "node", swap_core)
    (keep,) = call(
        "keep_grad", functools.partial(keep_kernel, near), (VMEM, VMEM), ((square32, VMEM),),
        flops=work, moved=2 << 20,
    )(left, pre_grad)
    base, order = call(
        "own_grad", functools.partial(own_grad_kernel, dims), (VMEM,) * 2 + (HBM,) * 4,
        ((square32, VMEM), (shape((1, slots), jnp.int32), VMEM)),
        scratch=[*held, VMEM((1, slots), jnp.int32), VMEM((width, width), BF16), *counted],
        copies=4, flops=2 * work, moved=4 << 20,
    )(pre_grad, message, neighbours, neigh_count, serve_rows, w_self)
    (payload,) = call(
        "pack", functools.partial(pack_kernel, dims, chips, gather_chips), (VMEM,) * 4,
        ((shape((peers, length, width), BF16), VMEM),), flops=work // 4, moved=4 << 20,
    )(received, keep, received_rows, keep_rows)
    arrived = lax.all_to_all(payload, "node", 0, 0, axis_index_groups=cubes, tiled=True)
    grads = shape((share, width), BF16)
    pairs = shape((half + 8, width), BF16)
    keep_grads, keep_sum, send_sum = call(
        "sum_shares", functools.partial(sum_kernel, dims, chips), (VMEM,),
        ((grads, VMEM), (pairs, VMEM), (pairs, VMEM)), flops=work // 8, moved=1 << 20,
    )(arrived)
    received_grads = lax.ppermute(keep_grads, "node", swap_wide)
    received_sum = lax.ppermute(send_sum, "node", swap_wide)
    (total,) = call(
        "total", total_kernel, (VMEM,) * 3, ((shape((peers, share, width), BF16), VMEM),),
        flops=work // 8, moved=1 << 20,
    )(keep_grads, received_grads, base)
    gathered = lax.all_to_all(total, "node", 0, 0, axis_index_groups=gather_cubes, tiled=True)
    (mine,) = call(
        "after_rows", pass_kernel, (VMEM, VMEM), ((square16, VMEM),), flops=work // 8, moved=1 << 20,
    )(gathered.reshape(own_rows, width), received_sum)
    other = lax.ppermute(mine, "node", swap_core)
    wide = VMEM((own_rows, width), F32)
    grad_features, self_part, neigh_part, bias_sum = call(
        "tail", functools.partial(tail_kernel, factor, near), (VMEM,) * 5,
        ((square32, HBM), (square32, HBM), (square32, HBM), (shape((1, width), F32), HBM)),
        scratch=[wide, wide, VMEM((1, width), F32)], copies=3, flops=work, moved=4 << 20,
    )(order, keep_sum, received_sum, base, mine)
    grad_self, grad_neigh = call(
        "other_half", functools.partial(other_kernel, factor, near), (VMEM, HBM, HBM),
        ((square32, HBM), (square32, HBM)),
        scratch=[wide], copies=4, flops=work // 2, moved=3 << 20, aliases={1: 0, 2: 1},
    )(other, self_part, neigh_part)
    return grad_features, grad_self, grad_neigh, bias_sum.reshape(width)


def solution(mesh):
    across, near = mesh.shape["group"] // 2, mesh.shape["member"] // 2
    line = Mesh(mesh.devices.reshape(-1), ("node",))
    rows = P("node", None)
    return jax.shard_map(
        functools.partial(local, across, near),
        mesh=line,
        in_specs=(rows, rows, P(), P(), P(), rows, P("node"), rows),
        out_specs=(rows, P(), P(), P()),
        check_vma=False,
    )
```

```python
import functools
import math

import jax
import jax.numpy as jnp
from jax import lax
from jax.experimental import pallas as pl
from jax.experimental.pallas import tpu as pltpu
from jax.sharding import Mesh
from jax.sharding import PartitionSpec as P

BF16 = jnp.bfloat16
F32 = jnp.float32
VMEM, HBM = pltpu.VMEM, pltpu.HBM
shape = jax.ShapeDtypeStruct


def product(left, right, left_dim, right_dim):
    return lax.dot_general(
        left, right, (((left_dim,), (right_dim,)), ((), ())), preferred_element_type=F32
    )


def call(name, body, ins, outs, scratch=(), copies=0, flops=0, moved=0, aliases=None):
    scratch = list(scratch)
    if copies:
        scratch.append(pltpu.SemaphoreType.DMA((copies,)))
    run = pl.pallas_call(
        body,
        out_shape=tuple(
            HBM(out.shape, out.dtype) if memory is HBM else out for out, memory in outs
        ),
        in_specs=[pl.BlockSpec(memory_space=memory) for memory in ins],
        out_specs=tuple(pl.BlockSpec(memory_space=memory) for _, memory in outs),
        scratch_shapes=scratch,
        input_output_aliases=aliases or {},
        compiler_params=pltpu.CompilerParams(vmem_limit_bytes=48 * 1024 * 1024),
        cost_estimate=pl.CostEstimate(flops=flops, bytes_accessed=moved, transcendentals=0),
        name=name,
    )

    def held(*operands):
        return run(*(
            pltpu.with_memory_space_constraint(operand, HBM) if memory is HBM else operand
            for operand, memory in zip(operands, ins, strict=True)
        ))

    return held


def core_of(near):
    return lax.axis_index("node") // (2 * near) % 2


def wide_of(near):
    return lax.axis_index("node") // near % 2


def start_all(sems, *pairs):
    copies = [pltpu.make_async_copy(a, b, sems.at[at]) for at, (a, b) in enumerate(pairs)]
    for copy in copies:
        copy.start()
    return copies


def serve_kernel(serve_hbm, features_hbm, out_ref, serve_ref, features_ref, sems):
    copies = start_all(sems, (serve_hbm, serve_ref), (features_hbm, features_ref))
    own_rows = features_ref.shape[0]
    slots = serve_ref.shape[1]
    copies[0].wait()
    wanted = jnp.broadcast_to(serve_ref[...], (128, slots)).astype(F32).T
    row = lax.broadcasted_iota(jnp.int32, (slots, 128), 1).astype(F32)
    picks = jnp.concatenate(
        [
            jnp.where(row + float(at) == wanted, 1.0, 0.0).astype(BF16)
            for at in range(0, own_rows, 128)
        ],
        axis=1,
    )
    copies[1].wait()
    rows = product(picks, features_ref[...], 1, 0)
    out_ref[...] = rows.reshape(out_ref.shape).astype(BF16)


def find_live(neighbours_ref, count_ref):
    fanout, own_rows = neighbours_ref.shape
    position = lax.broadcasted_iota(jnp.int32, (fanout, own_rows), 0)
    return jnp.where(position < count_ref[...], neighbours_ref[...], -1)


def fill_counts(live, live_ref, table_ref, base):
    fanout, own_rows = live.shape
    for block in range(0, table_ref.shape[0], 256):
        table_rows = min(256, table_ref.shape[0] - block)
        step = min(64, table_rows)
        live_ref[...] = (live - (base + block)).astype(F32).astype(BF16)

        def fill(at, carry):
            start = pl.multiple_of(at * step, step)
            row = (lax.broadcasted_iota(jnp.int32, (step, own_rows), 0) + start).astype(F32).astype(BF16)
            total = jnp.zeros((step, own_rows), BF16)
            for k in range(fanout):
                named = jnp.broadcast_to(live_ref[k : k + 1, :], (step, own_rows))
                total = total + jnp.where(row == named, jnp.bfloat16(1), jnp.bfloat16(0))
            table_ref[pl.ds(pl.multiple_of(block + start, step), step), :] = total
            return carry

        lax.fori_loop(0, table_rows // step, fill, 0)


def own_kernel(
    neighbours_hbm, count_hbm, features_hbm, w_self_hbm, bias_hbm,
    own_sum_ref, fetch_counts_ref, slot_counts_ref, inverse_ref, pre_ref,
    neighbours_ref, count_ref, features_ref, w_self_ref, bias_ref, live_ref, table_ref, sems,
):
    copies = start_all(
        sems,
        (neighbours_hbm, neighbours_ref),
        (count_hbm, count_ref),
        (features_hbm, features_ref),
        (w_self_hbm, w_self_ref),
        (bias_hbm, bias_ref),
    )
    own_rows = features_ref.shape[0]
    for copy in copies[:2]:
        copy.wait()
    inverse_ref[...] = jnp.broadcast_to(1.0 / count_ref[...].astype(F32), (128, own_rows)).T
    live = find_live(neighbours_ref, count_ref)
    fill_counts(live, live_ref, slot_counts_ref, own_rows)
    fetch_counts_ref[...] = slot_counts_ref[...].T
    fill_counts(live, live_ref, table_ref, 0)
    for copy in copies[2:]:
        copy.wait()
    features = features_ref[...]
    own_sum_ref[...] = product(table_ref[...], features, 0, 0)
    pre_ref[...] = product(features, w_self_ref[...], 1, 0) + bias_ref[...]


def split_in_two(bias):
    high = bias.astype(BF16).astype(F32)
    row = lax.broadcasted_iota(jnp.int32, (8, bias.shape[1]), 0)
    return jnp.where(row == 0, high, jnp.where(row == 1, bias - high, 0.0)).astype(BF16)


def join_two(rows):
    rows = rows.astype(F32)
    return rows[0:1] + rows[1:2]


def spread_wide(inverse, width):
    return jnp.concatenate([inverse] * (width // 128), axis=1)


def main_kernel(
    near, incoming_ref, own_sum_ref, fetch_counts_ref, inverse_ref, pre_ref, w_neigh_ref,
    cotangent_hbm, features_hbm,
    send_ref, left_ref, pre_grad_ref,
    cotangent_ref, slope_ref, sems,
):
    own_rows, width = own_sum_ref.shape
    slots = fetch_counts_ref.shape[1]
    core = core_of(near)
    parts = 2
    spans = [pl.ds(at * own_rows // parts, own_rows // parts) for at in range(parts)]
    copies = start_all(
        sems,
        *((cotangent_hbm.at[span, :], cotangent_ref.at[span, :]) for span in spans),
        (features_hbm, left_ref.at[0]),
    )
    incoming = incoming_ref[...].astype(F32).reshape(slots, width).astype(BF16)
    inverse = spread_wide(inverse_ref[...], width)
    summed = own_sum_ref[...] + product(fetch_counts_ref[...], incoming, 1, 0)
    aggregated = (summed * inverse).astype(BF16)
    left_ref[1] = aggregated
    pre = pre_ref[...] + product(aggregated, w_neigh_ref[...], 1, 0)
    sigmoid_pre = jax.nn.sigmoid(pre)
    slope = sigmoid_pre * (1.0 + pre * (1.0 - sigmoid_pre))
    slope_ref[...] = slope
    for span, copy in zip(spans, copies[:parts], strict=True):
        copy.wait()
        pre_grad_ref[span, :] = (
            cotangent_ref[span, :].astype(F32) * slope_ref[span, :]
        ).astype(BF16)
    pre_grad = pre_grad_ref[...]
    copies[parts].wait()
    send_ref[...] = product(left_ref[1 - core], pre_grad, 0, 0).astype(BF16)


def keep_kernel(near, left_ref, pre_grad_ref, keep_ref):
    keep_ref[...] = product(left_ref[core_of(near)], pre_grad_ref[...], 0, 0)


def message_kernel(
    dims, pre_grad_ref, w_neigh_ref, inverse_ref, slot_counts_ref, message_ref, send_ref, keep_ref, rows_ref
):
    own_rows, width = pre_grad_ref.shape
    slots = rows_ref.shape[0]
    _, near, cap = dims
    core = core_of(near)
    pre_grad = pre_grad_ref[...]
    inverse = spread_wide(inverse_ref[...], width)
    message = (product(pre_grad, w_neigh_ref[...], 1, 1) * inverse).astype(BF16)
    message_ref[...] = message
    rows_ref[...] = product(slot_counts_ref[...], message, 1, 0)
    half = slots // 2
    length = 2 * near * cap
    bias = split_in_two(jnp.sum(pre_grad.astype(F32), axis=0, keepdims=True))
    for index, ref in ((core, keep_ref), (1 - core, send_ref)):
        for at in range(half // length):
            start = pl.multiple_of((at * 2 + index) * length, length)
            ref[at * length : (at + 1) * length, :] = rows_ref[pl.ds(start, length), :].astype(BF16)
        ref[half:, :] = bias


def own_grad_kernel(
    dims, pre_grad_ref, message_ref, neighbours_hbm, count_hbm, serve_hbm, w_self_hbm, out_ref, order_ref,
    neighbours_ref, count_ref, serve_ref, w_self_ref, live_ref, table_ref, sems,
):
    copies = start_all(
        sems,
        (neighbours_hbm, neighbours_ref),
        (count_hbm, count_ref),
        (serve_hbm, serve_ref),
        (w_self_hbm, w_self_ref),
    )
    for copy in copies:
        copy.wait()
    fill_counts(find_live(neighbours_ref, count_ref), live_ref, table_ref, 0)
    out_ref[...] = product(pre_grad_ref[...], w_self_ref[...], 1, 1) + product(
        table_ref[...], message_ref[...], 1, 0
    )
    across, near, cap = dims
    slots = serve_ref.shape[1]
    to = lax.broadcasted_iota(jnp.int32, (slots, slots), 1)
    slot = to % cap
    core = (to // cap % 2 + core_of(near)) % 2
    n = to // (2 * cap) % near
    a = to // (2 * cap * near) % across
    wide = (to // (2 * cap * near * across) + wide_of(near)) % 2
    source = (((a * 2 + core) * 2 + wide) * near + n) * cap + slot
    at = lax.broadcasted_iota(jnp.int32, (slots, slots), 0)
    moves = (at == source).astype(F32).astype(BF16)
    serve = serve_ref[...]
    high = (serve // 32).astype(F32).astype(BF16)
    low = (serve % 32).astype(F32).astype(BF16)
    order_ref[...] = (
        product(high, moves, 1, 0) * 32.0 + product(low, moves, 1, 0)
    ).astype(jnp.int32)


def pack_kernel(dims, order, gather_order, received_ref, keep_ref, received_rows_ref, keep_rows_ref, out_ref):
    across, near, cap = dims
    own_rows, width = keep_ref.shape
    peers, length = out_ref.shape[0], out_ref.shape[1] * out_ref.shape[2]
    half = 2 * peers * cap
    share = own_rows // peers
    keep_rows = keep_rows_ref[...].astype(F32)
    other_rows = received_rows_ref[...].astype(F32)
    bias = split_in_two(join_two(keep_rows[half:]) + join_two(other_rows[half:])).astype(F32)
    summed = keep_ref[...] + received_ref[...].astype(F32)
    for peer in range(peers):
        start = gather_order.index(order[peer]) * share
        parts = [summed[start : start + share]]
        for wide in range(2):
            place = order[peer]
            at = ((place // near * 2 + wide) * near + place % near) * cap
            parts += [keep_rows[at : at + cap], other_rows[at : at + cap]]
        parts.append(bias[: length - share - 4 * cap])
        out_ref[peer] = jnp.concatenate(parts, axis=0).reshape(out_ref.shape[1:]).astype(BF16)


def sum_kernel(dims, order, payload_ref, grads_ref, keep_ref, send_ref):
    cap = dims[2]
    peers, width = payload_ref.shape[0], payload_ref.shape[3]
    pair = 2 * cap
    count = peers * pair
    share = grads_ref.shape[0]
    grads = jnp.zeros((share, width), F32)
    bias = jnp.zeros((1, width), F32)
    lower, upper = [None] * peers, [None] * peers
    for peer in range(peers):
        block = payload_ref[peer].astype(F32).reshape(-1, width)
        grads = grads + block[:share]
        rest = block[share:]
        lower[order[peer]] = rest[:pair]
        upper[order[peer]] = rest[pair : 2 * pair]
        bias = bias + join_two(rest[2 * pair :])
    grads_ref[...] = grads.astype(BF16)
    bias = split_in_two(bias)
    first = wide_of(dims[1]) == 0
    lower, upper = jnp.concatenate(lower, axis=0), jnp.concatenate(upper, axis=0)
    for ref, rows in (
        (keep_ref, jnp.where(first, lower, upper)),
        (send_ref, jnp.where(first, upper, lower)),
    ):
        ref[:count, :] = rows.astype(BF16)
        ref[count:, :] = bias


def total_kernel(keep_ref, received_ref, after_ref, out_ref):
    peers, share, width = out_ref.shape
    total = (keep_ref[...].astype(F32) + received_ref[...].astype(F32)).astype(BF16)
    for peer in range(peers):
        out_ref[peer] = total


def pass_kernel(source_ref, after_ref, out_ref):
    out_ref[...] = source_ref[...]


def send_half(matrix, source_ref, self_hbm, neigh_hbm, sem, rows, wait):
    source = source_ref.at[rows, :]
    for index, target in enumerate((self_hbm, neigh_hbm)):

        @pl.when(matrix == index)
        def _(target=target):
            copy = pltpu.make_async_copy(source, target.at[rows, :], sem)
            if wait:
                copy.wait()
            else:
                copy.start()


def tail_kernel(
    factor, near, order_ref, keep_ref, received_ref, base_ref, mine_ref,
    out_hbm, self_hbm, neigh_hbm, bias_hbm, wide_ref, out_ref, bias_ref, sems,
):
    own_rows, slots = base_ref.shape[0], order_ref.shape[1]
    half = slots // 2
    matrix = core_of(near)
    everything = pl.ds(0, own_rows)
    wide_ref[...] = mine_ref[...].astype(F32) * factor
    send_half(matrix, wide_ref, self_hbm, neigh_hbm, sems.at[0], everything, False)
    bias_ref[...] = (join_two(keep_ref[half:, :]) + join_two(received_ref[half:, :])) * factor
    copies = [pltpu.make_async_copy(bias_ref, bias_hbm, sems.at[1])]
    copies[0].start()
    rows = jnp.concatenate([keep_ref[:half, :], received_ref[:half, :]], axis=0)
    row = lax.broadcasted_iota(jnp.int32, (own_rows, slots), 0)
    picks = (row == order_ref[...]).astype(F32).astype(BF16)
    out_ref[...] = base_ref[...] + product(picks, rows, 1, 0)
    copies.append(pltpu.make_async_copy(out_ref, out_hbm, sems.at[2]))
    copies[1].start()
    send_half(matrix, wide_ref, self_hbm, neigh_hbm, sems.at[0], everything, True)
    for copy in copies:
        copy.wait()


def other_kernel(factor, near, half_ref, self_in, neigh_in, self_hbm, neigh_hbm, wide_ref, sems):
    own_rows = half_ref.shape[0]
    pieces = 4
    length = own_rows // pieces
    matrix = 1 - core_of(near)
    spans = [pl.ds(at * length, length) for at in range(pieces)]
    for at, span in enumerate(spans):
        wide_ref[span, :] = half_ref[span, :].astype(F32) * factor
        send_half(matrix, wide_ref, self_hbm, neigh_hbm, sems.at[at], span, False)
    for at, span in enumerate(spans):
        send_half(matrix, wide_ref, self_hbm, neigh_hbm, sems.at[at], span, True)


def local(across, near, features, cotangent, w_self, w_neigh, bias, neighbours, neigh_count, serve_rows):
    own_rows, width = features.shape
    fanout = neighbours.shape[1]
    peers = across * near
    devices = 4 * peers
    slots = serve_rows.shape[1]
    cap = slots // devices
    half = slots // 2
    share = own_rows // peers
    length = -(-(share + 4 * cap + 2) // 4) * 4
    dims = (across, near, cap)
    chips = [place ^ (place >> 1) for place in reversed(range(peers))]
    gather_chips = list(reversed(range(peers)))
    cubes, gather_cubes = (
        [[(place // near * 4 + plane) * near + place % near for place in listed] for plane in range(4)]
        for listed in (chips, gather_chips)
    )
    swap_core = [(at, at ^ (2 * near)) for at in range(devices)]
    swap_wide = [(at, at ^ near) for at in range(devices)]
    factor = 1.0 / math.sqrt(own_rows * devices)
    work = 2 * own_rows * own_rows * width
    square16 = shape((own_rows, width), BF16)
    square32 = shape((own_rows, width), F32)

    (outgoing,) = call(
        "serve", serve_kernel, (HBM, HBM), ((shape((devices, cap, width), BF16), VMEM),),
        scratch=[VMEM((1, slots), jnp.int32), VMEM((own_rows, width), BF16)],
        copies=2, flops=work // 4, moved=1 << 20,
    )(serve_rows, features)
    incoming = lax.all_to_all(outgoing, "node", 0, 0, tiled=True)
    neighbours = neighbours.T
    neigh_count = neigh_count.reshape(1, own_rows)
    held = [VMEM((fanout, own_rows), jnp.int32), VMEM((1, own_rows), jnp.int32)]
    counted = [VMEM((fanout, own_rows), BF16), VMEM((own_rows, own_rows), BF16)]
    own_sum, fetch_counts, slot_counts, inverse, pre = call(
        "own_aggregate", own_kernel, (HBM,) * 5,
        (
            (square32, VMEM),
            (shape((own_rows, slots), BF16), VMEM),
            (shape((slots, own_rows), BF16), VMEM),
            (shape((own_rows, 128), F32), VMEM),
            (square32, VMEM),
        ),
        scratch=[
            *held,
            VMEM((own_rows, width), BF16),
            VMEM((width, width), BF16),
            VMEM((1, width), F32),
            *counted,
        ],
        copies=5, flops=20 * work, moved=4 << 20,
    )(neighbours, neigh_count, features, w_self, bias.reshape(1, width))
    send, left, pre_grad = call(
        "layer_grad", functools.partial(main_kernel, near), (VMEM,) * 6 + (HBM,) * 2,
        ((square16, VMEM), (shape((2, own_rows, width), BF16), VMEM), (square16, VMEM)),
        scratch=[VMEM((own_rows, width), BF16), VMEM((own_rows, width), F32)],
        copies=3, flops=5 * work, moved=8 << 20,
    )(incoming, own_sum, fetch_counts, inverse, pre, w_neigh, cotangent, features)
    received = lax.ppermute(send, "node", swap_core)
    returns = shape((half + 8, width), BF16)
    message, send_rows, keep_rows = call(
        "messages", functools.partial(message_kernel, dims), (VMEM,) * 4,
        ((square16, VMEM), (returns, VMEM), (returns, VMEM)),
        scratch=[VMEM((slots, width), F32)], flops=2 * work, moved=4 << 20,
    )(pre_grad, w_neigh, inverse, slot_counts)
    received_rows = lax.ppermute(send_rows, "node", swap_core)
    (keep,) = call(
        "keep_grad", functools.partial(keep_kernel, near), (VMEM, VMEM), ((square32, VMEM),),
        flops=work, moved=2 << 20,
    )(left, pre_grad)
    base, order = call(
        "own_grad", functools.partial(own_grad_kernel, dims), (VMEM,) * 2 + (HBM,) * 4,
        ((square32, VMEM), (shape((1, slots), jnp.int32), VMEM)),
        scratch=[*held, VMEM((1, slots), jnp.int32), VMEM((width, width), BF16), *counted],
        copies=4, flops=2 * work, moved=4 << 20,
    )(pre_grad, message, neighbours, neigh_count, serve_rows, w_self)
    (payload,) = call(
        "pack", functools.partial(pack_kernel, dims, chips, gather_chips), (VMEM,) * 4,
        ((shape((peers, length // 4, 4, width), BF16), VMEM),), flops=work // 4, moved=4 << 20,
    )(received, keep, received_rows, keep_rows)
    arrived = lax.all_to_all(payload, "node", 0, 0, axis_index_groups=cubes, tiled=True)
    grads = shape((share, width), BF16)
    pairs = shape((half + 8, width), BF16)
    keep_grads, keep_sum, send_sum = call(
        "sum_shares", functools.partial(sum_kernel, dims, chips), (VMEM,),
        ((grads, VMEM), (pairs, VMEM), (pairs, VMEM)), flops=work // 8, moved=1 << 20,
    )(arrived)
    received_grads = lax.ppermute(keep_grads, "node", swap_wide)
    received_sum = lax.ppermute(send_sum, "node", swap_wide)
    (total,) = call(
        "total", total_kernel, (VMEM,) * 3, ((shape((peers, share, width), BF16), VMEM),),
        flops=work // 8, moved=1 << 20,
    )(keep_grads, received_grads, base)
    gathered = lax.all_to_all(total, "node", 0, 0, axis_index_groups=gather_cubes, tiled=True)
    (mine,) = call(
        "after_rows", pass_kernel, (VMEM, VMEM), ((square16, VMEM),), flops=work // 8, moved=1 << 20,
    )(gathered.reshape(own_rows, width), received_sum)
    other = lax.ppermute(mine, "node", swap_core)
    wide = VMEM((own_rows, width), F32)
    grad_features, self_part, neigh_part, bias_sum = call(
        "tail", functools.partial(tail_kernel, factor, near), (VMEM,) * 5,
        ((square32, HBM), (square32, HBM), (square32, HBM), (shape((1, width), F32), HBM)),
        scratch=[wide, wide, VMEM((1, width), F32)], copies=3, flops=work, moved=4 << 20,
    )(order, keep_sum, received_sum, base, mine)
    grad_self, grad_neigh = call(
        "other_half", functools.partial(other_kernel, factor, near), (VMEM, HBM, HBM),
        ((square32, HBM), (square32, HBM)),
        scratch=[wide], copies=4, flops=work // 2, moved=3 << 20, aliases={1: 0, 2: 1},
    )(other, self_part, neigh_part)
    return grad_features, grad_self, grad_neigh, bias_sum.reshape(width)


def solution(mesh):
    across, near = mesh.shape["group"] // 2, mesh.shape["member"] // 2
    line = Mesh(mesh.devices.reshape(-1), ("node",))
    rows = P("node", None)
    return jax.shard_map(
        functools.partial(local, across, near),
        mesh=line,
        in_specs=(rows, rows, P(), P(), P(), rows, P("node"), rows),
        out_specs=(rows, P(), P(), P()),
        check_vma=False,
    )
```

```python
import functools
import math

import jax
import jax.numpy as jnp
from jax import lax
from jax.experimental import pallas as pl
from jax.experimental.pallas import tpu as pltpu
from jax.sharding import Mesh
from jax.sharding import PartitionSpec as P

BF16 = jnp.bfloat16
F32 = jnp.float32
VMEM, HBM = pltpu.VMEM, pltpu.HBM
shape = jax.ShapeDtypeStruct


def product(left, right, left_dim, right_dim):
    return lax.dot_general(
        left, right, (((left_dim,), (right_dim,)), ((), ())), preferred_element_type=F32
    )


def call(name, body, ins, outs, scratch=(), copies=0, flops=0, moved=0, aliases=None):
    scratch = list(scratch)
    if copies:
        scratch.append(pltpu.SemaphoreType.DMA((copies,)))
    run = pl.pallas_call(
        body,
        out_shape=tuple(
            HBM(out.shape, out.dtype) if memory is HBM else out for out, memory in outs
        ),
        in_specs=[pl.BlockSpec(memory_space=memory) for memory in ins],
        out_specs=tuple(pl.BlockSpec(memory_space=memory) for _, memory in outs),
        scratch_shapes=scratch,
        input_output_aliases=aliases or {},
        compiler_params=pltpu.CompilerParams(vmem_limit_bytes=48 * 1024 * 1024),
        cost_estimate=pl.CostEstimate(flops=flops, bytes_accessed=moved, transcendentals=0),
        name=name,
    )

    def held(*operands):
        return run(*(
            pltpu.with_memory_space_constraint(operand, HBM) if memory is HBM else operand
            for operand, memory in zip(operands, ins, strict=True)
        ))

    return held


def core_of(near):
    return lax.axis_index("node") // (2 * near) % 2


def wide_of(near):
    return lax.axis_index("node") // near % 2


def start_all(sems, *pairs):
    copies = [pltpu.make_async_copy(a, b, sems.at[at]) for at, (a, b) in enumerate(pairs)]
    for copy in copies:
        copy.start()
    return copies


def serve_kernel(serve_hbm, features_hbm, out_ref, serve_ref, features_ref, sems):
    copies = start_all(sems, (serve_hbm, serve_ref), (features_hbm, features_ref))
    own_rows = features_ref.shape[0]
    slots = serve_ref.shape[1]
    copies[0].wait()
    wanted = jnp.broadcast_to(serve_ref[...], (128, slots)).astype(F32).T
    row = lax.broadcasted_iota(jnp.int32, (slots, 128), 1).astype(F32)
    picks = jnp.concatenate(
        [
            jnp.where(row + float(at) == wanted, 1.0, 0.0).astype(BF16)
            for at in range(0, own_rows, 128)
        ],
        axis=1,
    )
    copies[1].wait()
    rows = product(picks, features_ref[...], 1, 0)
    out_ref[...] = rows.reshape(out_ref.shape).astype(BF16)


def find_live(neighbours_ref, count_ref):
    fanout, own_rows = neighbours_ref.shape
    position = lax.broadcasted_iota(jnp.int32, (fanout, own_rows), 0)
    return jnp.where(position < count_ref[...], neighbours_ref[...], -1)


def fill_counts(live, live_ref, table_ref, base):
    fanout, own_rows = live.shape
    for block in range(0, table_ref.shape[0], 256):
        table_rows = min(256, table_ref.shape[0] - block)
        step = min(64, table_rows)
        live_ref[...] = (live - (base + block)).astype(F32).astype(BF16)

        def fill(at, carry):
            start = pl.multiple_of(at * step, step)
            row = (lax.broadcasted_iota(jnp.int32, (step, own_rows), 0) + start).astype(F32).astype(BF16)
            total = jnp.zeros((step, own_rows), BF16)
            for k in range(fanout):
                named = jnp.broadcast_to(live_ref[k : k + 1, :], (step, own_rows))
                total = total + jnp.where(row == named, jnp.bfloat16(1), jnp.bfloat16(0))
            table_ref[pl.ds(pl.multiple_of(block + start, step), step), :] = total
            return carry

        lax.fori_loop(0, table_rows // step, fill, 0)


def own_kernel(
    neighbours_hbm, count_hbm, features_hbm, w_self_hbm, bias_hbm,
    own_sum_ref, fetch_counts_ref, slot_counts_ref, inverse_ref, pre_ref,
    neighbours_ref, count_ref, features_ref, w_self_ref, bias_ref, live_ref, table_ref, sems,
):
    copies = start_all(
        sems,
        (neighbours_hbm, neighbours_ref),
        (count_hbm, count_ref),
        (features_hbm, features_ref),
        (w_self_hbm, w_self_ref),
        (bias_hbm, bias_ref),
    )
    own_rows = features_ref.shape[0]
    for copy in copies[:2]:
        copy.wait()
    inverse_ref[...] = jnp.broadcast_to(1.0 / count_ref[...].astype(F32), (128, own_rows)).T
    live = find_live(neighbours_ref, count_ref)
    fill_counts(live, live_ref, slot_counts_ref, own_rows)
    fetch_counts_ref[...] = slot_counts_ref[...].T
    fill_counts(live, live_ref, table_ref, 0)
    for copy in copies[2:]:
        copy.wait()
    features = features_ref[...]
    own_sum_ref[...] = product(table_ref[...], features, 0, 0)
    pre_ref[...] = product(features, w_self_ref[...], 1, 0) + bias_ref[...]


def split_in_two(bias):
    high = bias.astype(BF16).astype(F32)
    row = lax.broadcasted_iota(jnp.int32, (8, bias.shape[1]), 0)
    return jnp.where(row == 0, high, jnp.where(row == 1, bias - high, 0.0)).astype(BF16)


def join_two(rows):
    rows = rows.astype(F32)
    return rows[0:1] + rows[1:2]


def spread_wide(inverse, width):
    return jnp.concatenate([inverse] * (width // 128), axis=1)


def main_kernel(
    near, incoming_ref, own_sum_ref, fetch_counts_ref, inverse_ref, pre_ref, w_neigh_ref,
    cotangent_hbm, features_hbm,
    send_ref, left_ref, pre_grad_ref,
    cotangent_ref, slope_ref, sems,
):
    own_rows, width = own_sum_ref.shape
    slots = fetch_counts_ref.shape[1]
    core = core_of(near)
    parts = 2
    spans = [pl.ds(at * own_rows // parts, own_rows // parts) for at in range(parts)]
    copies = start_all(
        sems,
        *((cotangent_hbm.at[span, :], cotangent_ref.at[span, :]) for span in spans),
        (features_hbm, left_ref.at[0]),
    )
    incoming = incoming_ref[...].astype(F32).reshape(slots, width).astype(BF16)
    inverse = spread_wide(inverse_ref[...], width)
    summed = own_sum_ref[...] + product(fetch_counts_ref[...], incoming, 1, 0)
    aggregated = (summed * inverse).astype(BF16)
    left_ref[1] = aggregated
    pre = pre_ref[...] + product(aggregated, w_neigh_ref[...], 1, 0)
    sigmoid_pre = jax.nn.sigmoid(pre)
    slope = sigmoid_pre * (1.0 + pre * (1.0 - sigmoid_pre))
    slope_ref[...] = slope
    for span, copy in zip(spans, copies[:parts], strict=True):
        copy.wait()
        pre_grad_ref[span, :] = (
            cotangent_ref[span, :].astype(F32) * slope_ref[span, :]
        ).astype(BF16)
    pre_grad = pre_grad_ref[...]
    copies[parts].wait()
    send_ref[...] = product(left_ref[1 - core], pre_grad, 0, 0).astype(BF16)


def keep_kernel(near, left_ref, pre_grad_ref, keep_ref):
    keep_ref[...] = product(left_ref[core_of(near)], pre_grad_ref[...], 0, 0)


def message_kernel(
    dims, pre_grad_ref, w_neigh_ref, inverse_ref, slot_counts_ref, message_ref, send_ref, keep_ref, rows_ref
):
    own_rows, width = pre_grad_ref.shape
    slots = rows_ref.shape[0]
    _, near, cap = dims
    core = core_of(near)
    pre_grad = pre_grad_ref[...]
    inverse = spread_wide(inverse_ref[...], width)
    message = (product(pre_grad, w_neigh_ref[...], 1, 1) * inverse).astype(BF16)
    message_ref[...] = message
    rows_ref[...] = product(slot_counts_ref[...], message, 1, 0)
    half = slots // 2
    length = 2 * near * cap
    bias = split_in_two(jnp.sum(pre_grad.astype(F32), axis=0, keepdims=True))
    for index, ref in ((core, keep_ref), (1 - core, send_ref)):
        for at in range(half // length):
            start = pl.multiple_of((at * 2 + index) * length, length)
            ref[at * length : (at + 1) * length, :] = rows_ref[pl.ds(start, length), :].astype(BF16)
        ref[half:, :] = bias


def own_grad_kernel(
    dims, pre_grad_ref, message_ref, neighbours_hbm, count_hbm, serve_hbm, w_self_hbm, out_ref, order_ref,
    neighbours_ref, count_ref, serve_ref, w_self_ref, live_ref, table_ref, sems,
):
    copies = start_all(
        sems,
        (neighbours_hbm, neighbours_ref),
        (count_hbm, count_ref),
        (serve_hbm, serve_ref),
        (w_self_hbm, w_self_ref),
    )
    for copy in copies:
        copy.wait()
    fill_counts(find_live(neighbours_ref, count_ref), live_ref, table_ref, 0)
    out_ref[...] = product(pre_grad_ref[...], w_self_ref[...], 1, 1) + product(
        table_ref[...], message_ref[...], 1, 0
    )
    across, near, cap = dims
    slots = serve_ref.shape[1]
    to = lax.broadcasted_iota(jnp.int32, (slots, slots), 1)
    slot = to % cap
    core = (to // cap % 2 + core_of(near)) % 2
    n = to // (2 * cap) % near
    a = to // (2 * cap * near) % across
    wide = (to // (2 * cap * near * across) + wide_of(near)) % 2
    source = (((a * 2 + core) * 2 + wide) * near + n) * cap + slot
    at = lax.broadcasted_iota(jnp.int32, (slots, slots), 0)
    moves = (at == source).astype(F32).astype(BF16)
    serve = serve_ref[...]
    high = (serve // 32).astype(F32).astype(BF16)
    low = (serve % 32).astype(F32).astype(BF16)
    order_ref[...] = (
        product(high, moves, 1, 0) * 32.0 + product(low, moves, 1, 0)
    ).astype(jnp.int32)


def pack_kernel(dims, order, gather_order, received_ref, keep_ref, received_rows_ref, keep_rows_ref, out_ref):
    across, near, cap = dims
    own_rows, width = keep_ref.shape
    peers, length = out_ref.shape[0], out_ref.shape[1] * out_ref.shape[2]
    half = 2 * peers * cap
    share = own_rows // peers
    keep_rows = keep_rows_ref[...].astype(F32)
    other_rows = received_rows_ref[...].astype(F32)
    bias = split_in_two(join_two(keep_rows[half:]) + join_two(other_rows[half:])).astype(F32)
    summed = keep_ref[...] + received_ref[...].astype(F32)
    for peer in range(peers):
        start = gather_order.index(order[peer]) * share
        parts = [summed[start : start + share]]
        for wide in range(2):
            place = order[peer]
            at = ((place // near * 2 + wide) * near + place % near) * cap
            parts += [keep_rows[at : at + cap], other_rows[at : at + cap]]
        parts.append(bias[: length - share - 4 * cap])
        out_ref[peer] = jnp.concatenate(parts, axis=0).reshape(out_ref.shape[1:]).astype(BF16)


def sum_kernel(dims, order, payload_ref, grads_ref, keep_ref, send_ref):
    cap = dims[2]
    peers, width = payload_ref.shape[0], payload_ref.shape[3]
    pair = 2 * cap
    count = peers * pair
    share = grads_ref.shape[0]
    grads = jnp.zeros((share, width), F32)
    bias = jnp.zeros((1, width), F32)
    lower, upper = [None] * peers, [None] * peers
    for peer in range(peers):
        block = payload_ref[peer].astype(F32).reshape(-1, width)
        grads = grads + block[:share]
        rest = block[share:]
        lower[order[peer]] = rest[:pair]
        upper[order[peer]] = rest[pair : 2 * pair]
        bias = bias + join_two(rest[2 * pair :])
    grads_ref[...] = grads.astype(BF16)
    bias = split_in_two(bias).astype(F32)
    first = wide_of(dims[1]) == 0
    lower, upper = jnp.concatenate(lower, axis=0), jnp.concatenate(upper, axis=0)
    for ref, rows in (
        (keep_ref, jnp.where(first, lower, upper)),
        (send_ref, jnp.where(first, upper, lower)),
    ):
        both = jnp.concatenate([rows, bias], axis=0)[: count + 4]
        ref[...] = both.reshape(ref.shape).astype(BF16)


def total_kernel(keep_ref, received_ref, after_ref, out_ref):
    peers, share, width = out_ref.shape
    total = (keep_ref[...].astype(F32) + received_ref[...].astype(F32)).astype(BF16)
    for peer in range(peers):
        out_ref[peer] = total


def pass_kernel(source_ref, after_ref, out_ref):
    out_ref[...] = source_ref[...]


def send_half(matrix, source_ref, self_hbm, neigh_hbm, sem, rows, wait):
    source = source_ref.at[rows, :]
    for index, target in enumerate((self_hbm, neigh_hbm)):

        @pl.when(matrix == index)
        def _(target=target):
            copy = pltpu.make_async_copy(source, target.at[rows, :], sem)
            if wait:
                copy.wait()
            else:
                copy.start()


def tail_kernel(
    factor, near, order_ref, keep_ref, received_ref, base_ref, mine_ref,
    out_hbm, self_hbm, neigh_hbm, bias_hbm, wide_ref, out_ref, bias_ref, sems,
):
    own_rows, slots = base_ref.shape[0], order_ref.shape[1]
    half = slots // 2
    matrix = core_of(near)
    everything = pl.ds(0, own_rows)
    wide_ref[...] = mine_ref[...].astype(F32) * factor
    send_half(matrix, wide_ref, self_hbm, neigh_hbm, sems.at[0], everything, False)
    kept, received = (
        ref[...].astype(F32).reshape(half + 4, -1) for ref in (keep_ref, received_ref)
    )
    bias_ref[...] = (join_two(kept[half:]) + join_two(received[half:])) * factor
    copies = [pltpu.make_async_copy(bias_ref, bias_hbm, sems.at[1])]
    copies[0].start()
    rows = jnp.concatenate([kept[:half], received[:half]], axis=0).astype(BF16)
    row = lax.broadcasted_iota(jnp.int32, (own_rows, slots), 0)
    picks = (row == order_ref[...]).astype(F32).astype(BF16)
    out_ref[...] = base_ref[...] + product(picks, rows, 1, 0)
    copies.append(pltpu.make_async_copy(out_ref, out_hbm, sems.at[2]))
    copies[1].start()
    send_half(matrix, wide_ref, self_hbm, neigh_hbm, sems.at[0], everything, True)
    for copy in copies:
        copy.wait()


def other_kernel(factor, near, half_ref, self_in, neigh_in, self_hbm, neigh_hbm, wide_ref, sems):
    own_rows = half_ref.shape[0]
    pieces = 4
    length = own_rows // pieces
    matrix = 1 - core_of(near)
    spans = [pl.ds(at * length, length) for at in range(pieces)]
    for at, span in enumerate(spans):
        wide_ref[span, :] = half_ref[span, :].astype(F32) * factor
        send_half(matrix, wide_ref, self_hbm, neigh_hbm, sems.at[at], span, False)
    for at, span in enumerate(spans):
        send_half(matrix, wide_ref, self_hbm, neigh_hbm, sems.at[at], span, True)


def local(across, near, features, cotangent, w_self, w_neigh, bias, neighbours, neigh_count, serve_rows):
    own_rows, width = features.shape
    fanout = neighbours.shape[1]
    peers = across * near
    devices = 4 * peers
    slots = serve_rows.shape[1]
    cap = slots // devices
    half = slots // 2
    share = own_rows // peers
    length = -(-(share + 4 * cap + 2) // 4) * 4
    dims = (across, near, cap)
    chips = [place ^ (place >> 1) for place in reversed(range(peers))]
    gather_chips = list(reversed(range(peers)))
    cubes, gather_cubes = (
        [[(place // near * 4 + plane) * near + place % near for place in listed] for plane in range(4)]
        for listed in (chips, gather_chips)
    )
    swap_core = [(at, at ^ (2 * near)) for at in range(devices)]
    swap_wide = [(at, at ^ near) for at in range(devices)]
    factor = 1.0 / math.sqrt(own_rows * devices)
    work = 2 * own_rows * own_rows * width
    square16 = shape((own_rows, width), BF16)
    square32 = shape((own_rows, width), F32)

    (outgoing,) = call(
        "serve", serve_kernel, (HBM, HBM), ((shape((devices, cap, width), BF16), VMEM),),
        scratch=[VMEM((1, slots), jnp.int32), VMEM((own_rows, width), BF16)],
        copies=2, flops=work // 4, moved=1 << 20,
    )(serve_rows, features)
    incoming = lax.all_to_all(outgoing, "node", 0, 0, tiled=True)
    neighbours = neighbours.T
    neigh_count = neigh_count.reshape(1, own_rows)
    held = [VMEM((fanout, own_rows), jnp.int32), VMEM((1, own_rows), jnp.int32)]
    counted = [VMEM((fanout, own_rows), BF16), VMEM((own_rows, own_rows), BF16)]
    own_sum, fetch_counts, slot_counts, inverse, pre = call(
        "own_aggregate", own_kernel, (HBM,) * 5,
        (
            (square32, VMEM),
            (shape((own_rows, slots), BF16), VMEM),
            (shape((slots, own_rows), BF16), VMEM),
            (shape((own_rows, 128), F32), VMEM),
            (square32, VMEM),
        ),
        scratch=[
            *held,
            VMEM((own_rows, width), BF16),
            VMEM((width, width), BF16),
            VMEM((1, width), F32),
            *counted,
        ],
        copies=5, flops=20 * work, moved=4 << 20,
    )(neighbours, neigh_count, features, w_self, bias.reshape(1, width))
    send, left, pre_grad = call(
        "layer_grad", functools.partial(main_kernel, near), (VMEM,) * 6 + (HBM,) * 2,
        ((square16, VMEM), (shape((2, own_rows, width), BF16), VMEM), (square16, VMEM)),
        scratch=[VMEM((own_rows, width), BF16), VMEM((own_rows, width), F32)],
        copies=3, flops=5 * work, moved=8 << 20,
    )(incoming, own_sum, fetch_counts, inverse, pre, w_neigh, cotangent, features)
    received = lax.ppermute(send, "node", swap_core)
    returns = shape((half + 8, width), BF16)
    message, send_rows, keep_rows = call(
        "messages", functools.partial(message_kernel, dims), (VMEM,) * 4,
        ((square16, VMEM), (returns, VMEM), (returns, VMEM)),
        scratch=[VMEM((slots, width), F32)], flops=2 * work, moved=4 << 20,
    )(pre_grad, w_neigh, inverse, slot_counts)
    received_rows = lax.ppermute(send_rows, "node", swap_core)
    (keep,) = call(
        "keep_grad", functools.partial(keep_kernel, near), (VMEM, VMEM), ((square32, VMEM),),
        flops=work, moved=2 << 20,
    )(left, pre_grad)
    base, order = call(
        "own_grad", functools.partial(own_grad_kernel, dims), (VMEM,) * 2 + (HBM,) * 4,
        ((square32, VMEM), (shape((1, slots), jnp.int32), VMEM)),
        scratch=[*held, VMEM((1, slots), jnp.int32), VMEM((width, width), BF16), *counted],
        copies=4, flops=2 * work, moved=4 << 20,
    )(pre_grad, message, neighbours, neigh_count, serve_rows, w_self)
    (payload,) = call(
        "pack", functools.partial(pack_kernel, dims, chips, gather_chips), (VMEM,) * 4,
        ((shape((peers, length // 4, 4, width), BF16), VMEM),), flops=work // 4, moved=4 << 20,
    )(received, keep, received_rows, keep_rows)
    arrived = lax.all_to_all(payload, "node", 0, 0, axis_index_groups=cubes, tiled=True)
    grads = shape((share, width), BF16)
    pairs = shape((half // 4 + 1, 4, width), BF16)
    keep_grads, keep_sum, send_sum = call(
        "sum_shares", functools.partial(sum_kernel, dims, chips), (VMEM,),
        ((grads, VMEM), (pairs, VMEM), (pairs, VMEM)), flops=work // 8, moved=1 << 20,
    )(arrived)
    received_grads = lax.ppermute(keep_grads, "node", swap_wide)
    received_sum = lax.ppermute(send_sum, "node", swap_wide)
    (total,) = call(
        "total", total_kernel, (VMEM,) * 3, ((shape((peers, share, width), BF16), VMEM),),
        flops=work // 8, moved=1 << 20,
    )(keep_grads, received_grads, base)
    gathered = lax.all_to_all(total, "node", 0, 0, axis_index_groups=gather_cubes, tiled=True)
    (mine,) = call(
        "after_rows", pass_kernel, (VMEM, VMEM), ((square16, VMEM),), flops=work // 8, moved=1 << 20,
    )(gathered.reshape(own_rows, width), received_sum)
    other = lax.ppermute(mine, "node", swap_core)
    wide = VMEM((own_rows, width), F32)
    grad_features, self_part, neigh_part, bias_sum = call(
        "tail", functools.partial(tail_kernel, factor, near), (VMEM,) * 5,
        ((square32, HBM), (square32, HBM), (square32, HBM), (shape((1, width), F32), HBM)),
        scratch=[wide, wide, VMEM((1, width), F32)], copies=3, flops=work, moved=4 << 20,
    )(order, keep_sum, received_sum, base, mine)
    grad_self, grad_neigh = call(
        "other_half", functools.partial(other_kernel, factor, near), (VMEM, HBM, HBM),
        ((square32, HBM), (square32, HBM)),
        scratch=[wide], copies=4, flops=work // 2, moved=3 << 20, aliases={1: 0, 2: 1},
    )(other, self_part, neigh_part)
    return grad_features, grad_self, grad_neigh, bias_sum.reshape(width)


def solution(mesh):
    across, near = mesh.shape["group"] // 2, mesh.shape["member"] // 2
    line = Mesh(mesh.devices.reshape(-1), ("node",))
    rows = P("node", None)
    return jax.shard_map(
        functools.partial(local, across, near),
        mesh=line,
        in_specs=(rows, rows, P(), P(), P(), rows, P("node"), rows),
        out_specs=(rows, P(), P(), P()),
        check_vma=False,
    )
```

```python
import functools
import math

import jax
import jax.numpy as jnp
from jax import lax
from jax.experimental import pallas as pl
from jax.experimental.pallas import tpu as pltpu
from jax.sharding import Mesh
from jax.sharding import PartitionSpec as P

BF16 = jnp.bfloat16
F32 = jnp.float32
VMEM, HBM = pltpu.VMEM, pltpu.HBM
shape = jax.ShapeDtypeStruct


def product(left, right, left_dim, right_dim):
    return lax.dot_general(
        left, right, (((left_dim,), (right_dim,)), ((), ())), preferred_element_type=F32
    )


def call(name, body, ins, outs, scratch=(), copies=0, flops=0, moved=0, aliases=None):
    scratch = list(scratch)
    if copies:
        scratch.append(pltpu.SemaphoreType.DMA((copies,)))
    run = pl.pallas_call(
        body,
        out_shape=tuple(
            HBM(out.shape, out.dtype) if memory is HBM else out for out, memory in outs
        ),
        in_specs=[pl.BlockSpec(memory_space=memory) for memory in ins],
        out_specs=tuple(pl.BlockSpec(memory_space=memory) for _, memory in outs),
        scratch_shapes=scratch,
        input_output_aliases=aliases or {},
        compiler_params=pltpu.CompilerParams(vmem_limit_bytes=48 * 1024 * 1024),
        cost_estimate=pl.CostEstimate(flops=flops, bytes_accessed=moved, transcendentals=0),
        name=name,
    )

    def held(*operands):
        return run(*(
            pltpu.with_memory_space_constraint(operand, HBM) if memory is HBM else operand
            for operand, memory in zip(operands, ins, strict=True)
        ))

    return held


def core_of(near):
    return lax.axis_index("node") // (2 * near) % 2


def wide_of(near):
    return lax.axis_index("node") // near % 2


def start_all(sems, *pairs):
    copies = [pltpu.make_async_copy(a, b, sems.at[at]) for at, (a, b) in enumerate(pairs)]
    for copy in copies:
        copy.start()
    return copies


def serve_kernel(serve_hbm, features_hbm, out_ref, serve_ref, features_ref, sems):
    copies = start_all(sems, (serve_hbm, serve_ref), (features_hbm, features_ref))
    own_rows = features_ref.shape[0]
    slots = serve_ref.shape[1]
    copies[0].wait()
    wanted = jnp.broadcast_to(serve_ref[...], (128, slots)).astype(F32).T
    row = lax.broadcasted_iota(jnp.int32, (slots, 128), 1).astype(F32)
    picks = jnp.concatenate(
        [
            jnp.where(row + float(at) == wanted, 1.0, 0.0).astype(BF16)
            for at in range(0, own_rows, 128)
        ],
        axis=1,
    )
    copies[1].wait()
    rows = product(picks, features_ref[...], 1, 0)
    out_ref[...] = rows.reshape(out_ref.shape).astype(BF16)


def find_live(neighbours_ref, count_ref):
    fanout, own_rows = neighbours_ref.shape
    position = lax.broadcasted_iota(jnp.int32, (fanout, own_rows), 0)
    return jnp.where(position < count_ref[...], neighbours_ref[...], -1)


def fill_counts(live, live_ref, table_ref, base):
    fanout, own_rows = live.shape
    for block in range(0, table_ref.shape[0], 256):
        table_rows = min(256, table_ref.shape[0] - block)
        step = min(64, table_rows)
        live_ref[...] = (live - (base + block)).astype(F32).astype(BF16)

        def fill(at, carry):
            start = pl.multiple_of(at * step, step)
            row = (lax.broadcasted_iota(jnp.int32, (step, own_rows), 0) + start).astype(F32).astype(BF16)
            total = jnp.zeros((step, own_rows), BF16)
            for k in range(fanout):
                named = jnp.broadcast_to(live_ref[k : k + 1, :], (step, own_rows))
                total = total + jnp.where(row == named, jnp.bfloat16(1), jnp.bfloat16(0))
            table_ref[pl.ds(pl.multiple_of(block + start, step), step), :] = total
            return carry

        lax.fori_loop(0, table_rows // step, fill, 0)


def own_kernel(
    neighbours_hbm, count_hbm, features_hbm, w_self_hbm, bias_hbm,
    own_sum_ref, fetch_counts_ref, slot_counts_ref, inverse_ref, pre_ref,
    neighbours_ref, count_ref, features_ref, w_self_ref, bias_ref, live_ref, table_ref, sems,
):
    copies = start_all(
        sems,
        (neighbours_hbm, neighbours_ref),
        (count_hbm, count_ref),
        (features_hbm, features_ref),
        (w_self_hbm, w_self_ref),
        (bias_hbm, bias_ref),
    )
    own_rows = features_ref.shape[0]
    for copy in copies[:2]:
        copy.wait()
    inverse_ref[...] = jnp.broadcast_to(1.0 / count_ref[...].astype(F32), (128, own_rows)).T
    live = find_live(neighbours_ref, count_ref)
    fill_counts(live, live_ref, slot_counts_ref, own_rows)
    fetch_counts_ref[...] = slot_counts_ref[...].T
    fill_counts(live, live_ref, table_ref, 0)
    for copy in copies[2:]:
        copy.wait()
    features = features_ref[...]
    own_sum_ref[...] = product(table_ref[...], features, 0, 0)
    pre_ref[...] = product(features, w_self_ref[...], 1, 0) + bias_ref[...]


def split_in_two(bias):
    high = bias.astype(BF16).astype(F32)
    row = lax.broadcasted_iota(jnp.int32, (8, bias.shape[1]), 0)
    return jnp.where(row == 0, high, jnp.where(row == 1, bias - high, 0.0)).astype(BF16)


def join_two(rows):
    rows = rows.astype(F32)
    return rows[0:1] + rows[1:2]


def spread_wide(inverse, width):
    return jnp.concatenate([inverse] * (width // 128), axis=1)


def main_kernel(
    near, incoming_ref, own_sum_ref, fetch_counts_ref, inverse_ref, pre_ref, w_neigh_ref,
    cotangent_hbm, features_hbm,
    send_ref, left_ref, pre_grad_ref,
    cotangent_ref, slope_ref, sems,
):
    own_rows, width = own_sum_ref.shape
    slots = fetch_counts_ref.shape[1]
    core = core_of(near)
    parts = 2
    spans = [pl.ds(at * own_rows // parts, own_rows // parts) for at in range(parts)]
    copies = start_all(
        sems,
        *((cotangent_hbm.at[span, :], cotangent_ref.at[span, :]) for span in spans),
        (features_hbm, left_ref.at[0]),
    )
    incoming = incoming_ref[...].astype(F32).reshape(slots, width).astype(BF16)
    inverse = spread_wide(inverse_ref[...], width)
    summed = own_sum_ref[...] + product(fetch_counts_ref[...], incoming, 1, 0)
    aggregated = (summed * inverse).astype(BF16)
    left_ref[1] = aggregated
    pre = pre_ref[...] + product(aggregated, w_neigh_ref[...], 1, 0)
    sigmoid_pre = jax.nn.sigmoid(pre)
    slope = sigmoid_pre * (1.0 + pre * (1.0 - sigmoid_pre))
    slope_ref[...] = slope
    for span, copy in zip(spans, copies[:parts], strict=True):
        copy.wait()
        pre_grad_ref[span, :] = (
            cotangent_ref[span, :].astype(F32) * slope_ref[span, :]
        ).astype(BF16)
    pre_grad = pre_grad_ref[...]
    copies[parts].wait()
    send_ref[...] = product(left_ref[1 - core], pre_grad, 0, 0).astype(BF16)


def keep_kernel(near, left_ref, pre_grad_ref, keep_ref):
    keep_ref[...] = product(left_ref[core_of(near)], pre_grad_ref[...], 0, 0)


def message_kernel(
    dims, pre_grad_ref, w_neigh_ref, inverse_ref, slot_counts_ref, message_ref, send_ref, keep_ref, rows_ref
):
    own_rows, width = pre_grad_ref.shape
    slots = rows_ref.shape[0]
    _, near, cap = dims
    core = core_of(near)
    pre_grad = pre_grad_ref[...]
    inverse = spread_wide(inverse_ref[...], width)
    message = (product(pre_grad, w_neigh_ref[...], 1, 1) * inverse).astype(BF16)
    message_ref[...] = message
    rows_ref[...] = product(slot_counts_ref[...], message, 1, 0)
    half = slots // 2
    length = 2 * near * cap
    bias = split_in_two(jnp.sum(pre_grad.astype(F32), axis=0, keepdims=True))
    for index, ref in ((core, keep_ref), (1 - core, send_ref)):
        for at in range(half // length):
            start = pl.multiple_of((at * 2 + index) * length, length)
            ref[at * length : (at + 1) * length, :] = rows_ref[pl.ds(start, length), :].astype(BF16)
        ref[half:, :] = bias


def own_grad_kernel(
    dims, pre_grad_ref, message_ref, neighbours_hbm, count_hbm, serve_hbm, w_self_hbm, out_ref, order_ref,
    neighbours_ref, count_ref, serve_ref, w_self_ref, live_ref, table_ref, sems,
):
    copies = start_all(
        sems,
        (neighbours_hbm, neighbours_ref),
        (count_hbm, count_ref),
        (serve_hbm, serve_ref),
        (w_self_hbm, w_self_ref),
    )
    for copy in copies:
        copy.wait()
    fill_counts(find_live(neighbours_ref, count_ref), live_ref, table_ref, 0)
    out_ref[...] = product(pre_grad_ref[...], w_self_ref[...], 1, 1) + product(
        table_ref[...], message_ref[...], 1, 0
    )
    across, near, cap = dims
    slots = serve_ref.shape[1]
    to = lax.broadcasted_iota(jnp.int32, (slots, slots), 1)
    slot = to % cap
    core = (to // cap % 2 + core_of(near)) % 2
    n = to // (2 * cap) % near
    a = to // (2 * cap * near) % across
    wide = (to // (2 * cap * near * across) + wide_of(near)) % 2
    source = (((a * 2 + core) * 2 + wide) * near + n) * cap + slot
    at = lax.broadcasted_iota(jnp.int32, (slots, slots), 0)
    moves = (at == source).astype(F32).astype(BF16)
    serve = serve_ref[...]
    high = (serve // 32).astype(F32).astype(BF16)
    low = (serve % 32).astype(F32).astype(BF16)
    order_ref[...] = (
        product(high, moves, 1, 0) * 32.0 + product(low, moves, 1, 0)
    ).astype(jnp.int32)


def pack_kernel(dims, order, gather_order, received_ref, keep_ref, received_rows_ref, keep_rows_ref, out_ref):
    across, near, cap = dims
    own_rows, width = keep_ref.shape
    peers, length = out_ref.shape[0], out_ref.shape[1] * out_ref.shape[2]
    half = 2 * peers * cap
    share = own_rows // peers
    keep_rows = keep_rows_ref[...].astype(F32)
    other_rows = received_rows_ref[...].astype(F32)
    bias = split_in_two(join_two(keep_rows[half:]) + join_two(other_rows[half:])).astype(F32)
    summed = keep_ref[...] + received_ref[...].astype(F32)
    for peer in range(peers):
        start = gather_order.index(order[peer]) * share
        parts = [summed[start : start + share]]
        for wide in range(2):
            place = order[peer]
            at = ((place // near * 2 + wide) * near + place % near) * cap
            parts += [keep_rows[at : at + cap], other_rows[at : at + cap]]
        parts.append(bias[: length - share - 4 * cap])
        out_ref[peer] = jnp.concatenate(parts, axis=0).reshape(out_ref.shape[1:]).astype(BF16)


def sum_kernel(dims, order, payload_ref, grads_ref, keep_ref, send_ref):
    cap = dims[2]
    peers, width = payload_ref.shape[0], payload_ref.shape[3]
    pair = 2 * cap
    count = peers * pair
    share = grads_ref.shape[0]
    grads = jnp.zeros((share, width), F32)
    bias = jnp.zeros((1, width), F32)
    lower, upper = [None] * peers, [None] * peers
    for peer in range(peers):
        block = payload_ref[peer].astype(F32).reshape(-1, width)
        grads = grads + block[:share]
        rest = block[share:]
        lower[order[peer]] = rest[:pair]
        upper[order[peer]] = rest[pair : 2 * pair]
        bias = bias + join_two(rest[2 * pair :])
    grads_ref[...] = grads.astype(BF16)
    bias = split_in_two(bias)
    first = wide_of(dims[1]) == 0
    lower, upper = jnp.concatenate(lower, axis=0), jnp.concatenate(upper, axis=0)
    for ref, rows in (
        (keep_ref, jnp.where(first, lower, upper)),
        (send_ref, jnp.where(first, upper, lower)),
    ):
        ref[:count, :] = rows.astype(BF16)
        ref[count:, :] = bias


def total_kernel(keep_ref, received_ref, after_ref, out_ref):
    peers, share, width = out_ref.shape
    total = (keep_ref[...].astype(F32) + received_ref[...].astype(F32)).astype(BF16)
    for peer in range(peers):
        out_ref[peer] = total


def pass_kernel(source_ref, after_ref, out_ref):
    out_ref[...] = source_ref[...]


def send_half(matrix, source_ref, self_hbm, neigh_hbm, sem, rows, wait):
    source = source_ref.at[rows, :]
    for index, target in enumerate((self_hbm, neigh_hbm)):

        @pl.when(matrix == index)
        def _(target=target):
            copy = pltpu.make_async_copy(source, target.at[rows, :], sem)
            if wait:
                copy.wait()
            else:
                copy.start()


def tail_kernel(
    factor, near, order_ref, keep_ref, received_ref, base_ref, mine_ref,
    out_hbm, self_hbm, neigh_hbm, bias_hbm, wide_ref, out_ref, bias_ref, sems,
):
    own_rows, slots = base_ref.shape[0], order_ref.shape[1]
    half = slots // 2
    matrix = core_of(near)
    everything = pl.ds(0, own_rows)
    wide_ref[...] = mine_ref[...].astype(F32) * factor
    send_half(matrix, wide_ref, self_hbm, neigh_hbm, sems.at[0], everything, False)
    bias_ref[...] = (join_two(keep_ref[half:, :]) + join_two(received_ref[half:, :])) * factor
    copies = [pltpu.make_async_copy(bias_ref, bias_hbm, sems.at[1])]
    copies[0].start()
    rows = jnp.concatenate([keep_ref[:half, :], received_ref[:half, :]], axis=0)
    row = lax.broadcasted_iota(jnp.int32, (own_rows, slots), 0)
    picks = (row == order_ref[...]).astype(F32).astype(BF16)
    out_ref[...] = base_ref[...] + product(picks, rows, 1, 0)
    copies.append(pltpu.make_async_copy(out_ref, out_hbm, sems.at[2]))
    copies[1].start()
    send_half(matrix, wide_ref, self_hbm, neigh_hbm, sems.at[0], everything, True)
    for copy in copies:
        copy.wait()


def other_kernel(factor, near, half_ref, self_in, neigh_in, self_hbm, neigh_hbm, wide_ref, sems):
    own_rows = half_ref.shape[0]
    pieces = 1
    length = own_rows // pieces
    matrix = 1 - core_of(near)
    spans = [pl.ds(at * length, length) for at in range(pieces)]
    for at, span in enumerate(spans):
        wide_ref[span, :] = half_ref[span, :].astype(F32) * factor
        send_half(matrix, wide_ref, self_hbm, neigh_hbm, sems.at[at], span, False)
    for at, span in enumerate(spans):
        send_half(matrix, wide_ref, self_hbm, neigh_hbm, sems.at[at], span, True)


def local(across, near, features, cotangent, w_self, w_neigh, bias, neighbours, neigh_count, serve_rows):
    own_rows, width = features.shape
    fanout = neighbours.shape[1]
    peers = across * near
    devices = 4 * peers
    slots = serve_rows.shape[1]
    cap = slots // devices
    half = slots // 2
    share = own_rows // peers
    length = -(-(share + 4 * cap + 2) // 4) * 4
    dims = (across, near, cap)
    chips = [place ^ (place >> 1) for place in reversed(range(peers))]
    gather_chips = list(reversed(range(peers)))
    cubes, gather_cubes = (
        [[(place // near * 4 + plane) * near + place % near for place in listed] for plane in range(4)]
        for listed in (chips, gather_chips)
    )
    swap_core = [(at, at ^ (2 * near)) for at in range(devices)]
    swap_wide = [(at, at ^ near) for at in range(devices)]
    factor = 1.0 / math.sqrt(own_rows * devices)
    work = 2 * own_rows * own_rows * width
    square16 = shape((own_rows, width), BF16)
    square32 = shape((own_rows, width), F32)

    (outgoing,) = call(
        "serve", serve_kernel, (HBM, HBM), ((shape((devices, cap, width), BF16), VMEM),),
        scratch=[VMEM((1, slots), jnp.int32), VMEM((own_rows, width), BF16)],
        copies=2, flops=work // 4, moved=1 << 20,
    )(serve_rows, features)
    incoming = lax.all_to_all(outgoing, "node", 0, 0, tiled=True)
    neighbours = neighbours.T
    neigh_count = neigh_count.reshape(1, own_rows)
    held = [VMEM((fanout, own_rows), jnp.int32), VMEM((1, own_rows), jnp.int32)]
    counted = [VMEM((fanout, own_rows), BF16), VMEM((own_rows, own_rows), BF16)]
    own_sum, fetch_counts, slot_counts, inverse, pre = call(
        "own_aggregate", own_kernel, (HBM,) * 5,
        (
            (square32, VMEM),
            (shape((own_rows, slots), BF16), VMEM),
            (shape((slots, own_rows), BF16), VMEM),
            (shape((own_rows, 128), F32), VMEM),
            (square32, VMEM),
        ),
        scratch=[
            *held,
            VMEM((own_rows, width), BF16),
            VMEM((width, width), BF16),
            VMEM((1, width), F32),
            *counted,
        ],
        copies=5, flops=20 * work, moved=4 << 20,
    )(neighbours, neigh_count, features, w_self, bias.reshape(1, width))
    send, left, pre_grad = call(
        "layer_grad", functools.partial(main_kernel, near), (VMEM,) * 6 + (HBM,) * 2,
        ((square16, VMEM), (shape((2, own_rows, width), BF16), VMEM), (square16, VMEM)),
        scratch=[VMEM((own_rows, width), BF16), VMEM((own_rows, width), F32)],
        copies=3, flops=5 * work, moved=8 << 20,
    )(incoming, own_sum, fetch_counts, inverse, pre, w_neigh, cotangent, features)
    received = lax.ppermute(send, "node", swap_core)
    returns = shape((half + 8, width), BF16)
    message, send_rows, keep_rows = call(
        "messages", functools.partial(message_kernel, dims), (VMEM,) * 4,
        ((square16, VMEM), (returns, VMEM), (returns, VMEM)),
        scratch=[VMEM((slots, width), F32)], flops=2 * work, moved=4 << 20,
    )(pre_grad, w_neigh, inverse, slot_counts)
    received_rows = lax.ppermute(send_rows, "node", swap_core)
    (keep,) = call(
        "keep_grad", functools.partial(keep_kernel, near), (VMEM, VMEM), ((square32, VMEM),),
        flops=work, moved=2 << 20,
    )(left, pre_grad)
    base, order = call(
        "own_grad", functools.partial(own_grad_kernel, dims), (VMEM,) * 2 + (HBM,) * 4,
        ((square32, VMEM), (shape((1, slots), jnp.int32), VMEM)),
        scratch=[*held, VMEM((1, slots), jnp.int32), VMEM((width, width), BF16), *counted],
        copies=4, flops=2 * work, moved=4 << 20,
    )(pre_grad, message, neighbours, neigh_count, serve_rows, w_self)
    (payload,) = call(
        "pack", functools.partial(pack_kernel, dims, chips, gather_chips), (VMEM,) * 4,
        ((shape((peers, length // 4, 4, width), BF16), VMEM),), flops=work // 4, moved=4 << 20,
    )(received, keep, received_rows, keep_rows)
    arrived = lax.all_to_all(payload, "node", 0, 0, axis_index_groups=cubes, tiled=True)
    grads = shape((share, width), BF16)
    pairs = shape((half + 8, width), BF16)
    keep_grads, keep_sum, send_sum = call(
        "sum_shares", functools.partial(sum_kernel, dims, chips), (VMEM,),
        ((grads, VMEM), (pairs, VMEM), (pairs, VMEM)), flops=work // 8, moved=1 << 20,
    )(arrived)
    received_grads = lax.ppermute(keep_grads, "node", swap_wide)
    received_sum = lax.ppermute(send_sum, "node", swap_wide)
    (total,) = call(
        "total", total_kernel, (VMEM,) * 3, ((shape((peers, share, width), BF16), VMEM),),
        flops=work // 8, moved=1 << 20,
    )(keep_grads, received_grads, base)
    gathered = lax.all_to_all(total, "node", 0, 0, axis_index_groups=gather_cubes, tiled=True)
    (mine,) = call(
        "after_rows", pass_kernel, (VMEM, VMEM), ((square16, VMEM),), flops=work // 8, moved=1 << 20,
    )(gathered.reshape(own_rows, width), received_sum)
    other = lax.ppermute(mine, "node", swap_core)
    wide = VMEM((own_rows, width), F32)
    grad_features, self_part, neigh_part, bias_sum = call(
        "tail", functools.partial(tail_kernel, factor, near), (VMEM,) * 5,
        ((square32, HBM), (square32, HBM), (square32, HBM), (shape((1, width), F32), HBM)),
        scratch=[wide, wide, VMEM((1, width), F32)], copies=3, flops=work, moved=4 << 20,
    )(order, keep_sum, received_sum, base, mine)
    grad_self, grad_neigh = call(
        "other_half", functools.partial(other_kernel, factor, near), (VMEM, HBM, HBM),
        ((square32, HBM), (square32, HBM)),
        scratch=[wide], copies=4, flops=work // 2, moved=3 << 20, aliases={1: 0, 2: 1},
    )(other, self_part, neigh_part)
    return grad_features, grad_self, grad_neigh, bias_sum.reshape(width)


def solution(mesh):
    across, near = mesh.shape["group"] // 2, mesh.shape["member"] // 2
    line = Mesh(mesh.devices.reshape(-1), ("node",))
    rows = P("node", None)
    return jax.shard_map(
        functools.partial(local, across, near),
        mesh=line,
        in_specs=(rows, rows, P(), P(), P(), rows, P("node"), rows),
        out_specs=(rows, P(), P(), P()),
        check_vma=False,
    )
```
